32 devices in a mesh: frame: 8 (over z, x), mp: 4 (over y, core).
Axes of the slice: x: 2, y: 2, z: 4, core: 2. Of those that a mesh axis runs over, the one named last changes fastest.
Arguments:
- q_raw: bfloat16 [2048, 5120], P('frame', 'mp'), may hold values from -13 to 13
- k_raw: bfloat16 [2048, 5120], P('frame', 'mp'), may hold values from -13 to 13
- values: bfloat16 [2048, 5120], P('frame', 'mp'), may hold values from -6 to 6
- q_gain: float32 [5120], P('mp'), may hold values from 0.1 to 1.9
- k_gain: float32 [5120], P('mp'), may hold values from 0.1 to 1.9
- spatial_mask: int32 [8, 2, 2], P('frame'), may hold values from 0 to 1
- temporal_mask: int32 [8, 2, 2], P('frame'), may hold values from 0 to 1
- anchor_frame: int32 [1], replicated, may hold values from 0 to 7
Outputs:
- attended: bfloat16 [2048, 5120], P('frame', 'mp')
The draws below stay inside these ranges and needn't reach their ends.
All inputs are finite; a program needn't handle non-finite values.
Results may differ from the reference program's by a relative error of at most 0.013.
Values may be sent and summed in bfloat16 or wider, within the bound.
No kernel may reach another device: no remote copies, remote signals or barrier semaphores. Data moves between devices by JAX's collectives and lax.ppermute only.
A program may use at most 64 MiB of HBM per device.

```python
import jax
import jax.numpy as jnp
from jax import lax

D = 5120
HEADS = 40
HD = 128
BLOCK = 128
FTOK = 256
FRAMES = 8
TOKENS = 2048
NB = 2
POS_DEV = 32
N_FRAME = 8


def query_key_pair(key):
    base = jax.random.fold_in(key, 11)
    key_q, key_k = jax.random.split(base, 2)
    ramp = jnp.arange(HEADS, dtype=jnp.float32) / max(HEADS - 1, 1)
    scale = 0.6 * 3.0 ** ramp
    query = jnp.clip(jax.random.normal(key_q, (TOKENS, D), jnp.float32), -5.0, 5.0)
    keys = jnp.clip(jax.random.normal(key_k, (TOKENS, D), jnp.float32), -5.0, 5.0)
    col_scale = jnp.repeat(scale, HD)
    query = query * col_scale[None, :]
    keys = keys * col_scale[None, :]
    return (query, keys)


def draw_q_raw(key, part):
    return query_key_pair(key)[0].astype(jnp.bfloat16)


def draw_k_raw(key, part):
    return query_key_pair(key)[1].astype(jnp.bfloat16)


def level_mask(key, salt, count):
    key_level, key_vals = jax.random.split(jax.random.fold_in(key, salt))
    levels = jax.random.randint(key_level, (count, 1, 1), 1, 5)
    draws = jax.random.randint(key_vals, (count, NB, NB), 0, 4)
    return (draws < levels).astype(jnp.int32)


def draw_spatial_mask(key, part):
    return level_mask(key, 5, FRAMES)


def draw_temporal_mask(key, part):
    return level_mask(key, 6, FRAMES)


def shard_levels(own_key, extent, cuts, least, high):
    def one(axis_at, shards_of):
        steps = jax.random.uniform(jax.random.fold_in(jax.random.fold_in(own_key, 6), axis_at), (shards_of,), jnp.float32, least / len(cuts), high / len(cuts))
        return jnp.repeat(jnp.exp(steps), extent[axis_at] // shards_of).reshape((-1,) + (1,) * (len(extent) - axis_at - 1))

    gain = one(*cuts[0])
    for cut in cuts[1:]:
        gain = gain * one(*cut)
    return gain


def centred(own_key, extent, spread, limit, cuts=(), held_as=jnp.bfloat16):
    drawn = jax.random.normal(own_key, extent, jnp.float32) * spread
    if len(cuts) > 0:
        drawn = shard_levels(own_key, extent, cuts, -0.22, 0.18) * drawn
    return jnp.clip(drawn, min=-limit, max=limit).astype(held_as)


def setup_inputs(seed: int = 0) -> dict:
    splits = jax.random.split(jax.random.key(seed), 9)
    q_raw = draw_q_raw(jax.random.fold_in(splits[8], 71), 0)
    k_raw = draw_k_raw(jax.random.fold_in(splits[8], 71), 0)
    values = centred(splits[2], (TOKENS, D), 1.0, 6.0, ((0, 8), (1, 4)))
    q_gain = jnp.clip(1.0 + 0.18 * jax.random.normal(splits[3], (D,), jnp.float32), 0.1, 1.9)
    k_gain = jnp.clip(1.0 + 0.18 * jax.random.normal(splits[4], (D,), jnp.float32), 0.1, 1.9)
    spatial_mask = draw_spatial_mask(jax.random.fold_in(splits[8], 71), 0)
    temporal_mask = draw_temporal_mask(jax.random.fold_in(splits[8], 71), 0)
    anchor_frame = jax.random.randint(splits[7], (1,), 0, FRAMES).astype(jnp.int32)
    return {"q_raw": q_raw, "k_raw": k_raw, "values": values, "q_gain": q_gain, "k_gain": k_gain, "spatial_mask": spatial_mask, "temporal_mask": temporal_mask, "anchor_frame": anchor_frame}


def expand(block_mask):
    count = block_mask.shape[0]
    allowed = (block_mask == 1) | jnp.eye(count, dtype=jnp.bool_)
    return jnp.repeat(jnp.repeat(allowed, BLOCK, axis=0), BLOCK, axis=1)

def attend(query, keys, vals, allowed):
    scores = jnp.einsum('qhd,khd->hqk', query.astype(jnp.float32), keys.astype(jnp.float32)) / jnp.sqrt(jnp.float32(HD))
    scores = jnp.where(allowed[None], scores, -jnp.inf)
    probs = jax.nn.softmax(scores, axis=-1).astype(jnp.bfloat16)
    return jnp.einsum('hqk,khd->qhd', probs.astype(jnp.float32), vals.astype(jnp.float32))

def reference(q_raw, k_raw, values, q_gain, k_gain, spatial_mask, temporal_mask, anchor_frame):
    qf = q_raw.astype(jnp.float32)
    kf = k_raw.astype(jnp.float32)
    ms_q = lax.optimization_barrier(jnp.mean(qf * qf, axis=1, keepdims=True))
    ms_k = lax.optimization_barrier(jnp.mean(kf * kf, axis=1, keepdims=True))
    q_norm = (qf / jnp.sqrt(ms_q + 1e-06) * q_gain[None, :]).astype(jnp.bfloat16)
    k_norm = (kf / jnp.sqrt(ms_k + 1e-06) * k_gain[None, :]).astype(jnp.bfloat16)
    q_heads = q_norm.reshape(FRAMES, FTOK, HEADS, HD)
    k_heads = k_norm.reshape(FRAMES, FTOK, HEADS, HD)
    v_heads = values.reshape(FRAMES, FTOK, HEADS, HD)
    anchor = anchor_frame[0].astype(jnp.int32)
    k_anchor = lax.dynamic_index_in_dim(k_heads, anchor, 0, keepdims=False)
    v_anchor = lax.dynamic_index_in_dim(v_heads, anchor, 0, keepdims=False)
    always = jnp.ones((FTOK, FTOK), dtype=jnp.bool_)

    def frame_step(items):
        query, keys, vals, block_mask = items
        allowed = jnp.concatenate([expand(block_mask), always], axis=1)
        return attend(query, jnp.concatenate([keys, k_anchor], 0), jnp.concatenate([vals, v_anchor], 0), allowed)
    spatial = lax.map(frame_step, (q_heads, k_heads, v_heads, spatial_mask))

    def to_pencil(array):
        shaped = array.reshape(FRAMES, N_FRAME, POS_DEV, HEADS, HD)
        return jnp.transpose(shaped, (1, 0, 2, 3, 4)).reshape(N_FRAME, FRAMES * POS_DEV, HEADS, HD)

    def pencil_step(items):
        query, keys, vals, block_mask = items
        return attend(query, keys, vals, expand(block_mask)).astype(jnp.bfloat16)
    temporal = lax.map(pencil_step, (to_pencil(q_heads), to_pencil(k_heads), to_pencil(v_heads), temporal_mask))
    temporal = jnp.transpose(temporal.reshape(N_FRAME, FRAMES, POS_DEV, HEADS, HD), (1, 0, 2, 3, 4))
    temporal = temporal.reshape(FRAMES, FTOK, HEADS, HD)
    attended = (spatial + temporal.astype(jnp.float32)).astype(jnp.bfloat16)
    return attended.reshape(TOKENS, D)
```

```python
import functools

import jax
import jax.numpy as jnp
from jax import lax
from jax.experimental import pallas as pl
from jax.experimental.pallas import tpu as pltpu
from jax.sharding import PartitionSpec as P

D = 5120
HD = 128
BLOCK = 128
LOG2E = 1.4426950408889634
NEG = -1e30


def spread(value, axis, source):
    kept = jnp.where(lax.axis_index(axis) == source, value, 0).astype(value.dtype)
    return lax.psum(kept, axis)


def expand(block_mask):
    count = block_mask.shape[0]
    allowed = (block_mask == 1) | jnp.eye(count, dtype=jnp.bool_)
    return jnp.repeat(jnp.repeat(allowed, BLOCK, axis=0), BLOCK, axis=1)


def attend(query, keys, vals, allowed):
    rows = query.shape[0]
    width = query.shape[1]
    heads_dev = width // HD
    query3 = jnp.transpose(query.reshape(rows, heads_dev, HD), (1, 0, 2))
    keys3 = jnp.transpose(keys.reshape(keys.shape[0], heads_dev, HD), (1, 0, 2))
    vals3 = jnp.transpose(vals.reshape(vals.shape[0], heads_dev, HD), (1, 0, 2))
    scale = jnp.sqrt(jnp.float32(HD))

    def one_head(items):
        head_q, head_k, head_v = items
        scores = jnp.einsum("qd,kd->qk", head_q, head_k, preferred_element_type=jnp.float32) / scale
        scores = jnp.where(allowed, scores, -jnp.inf)
        probs = jax.nn.softmax(scores, axis=-1).astype(jnp.bfloat16)
        return jnp.dot(probs, head_v, preferred_element_type=jnp.float32)

    output = lax.map(one_head, (query3, keys3, vals3))
    return jnp.transpose(output, (1, 0, 2)).reshape(rows, width)


def local_general(
    q_raw, k_raw, values, q_gain, k_gain, spatial_mask, temporal_mask, anchor_frame
):
    frame_tok = q_raw.shape[0]
    width = q_raw.shape[1]
    q_float = q_raw.astype(jnp.float32)
    k_float = k_raw.astype(jnp.float32)
    sum_q, sum_k = lax.psum(
        (jnp.sum(q_float * q_float, axis=1), jnp.sum(k_float * k_float, axis=1)), "mp"
    )
    q_norm = (q_float / jnp.sqrt(sum_q[:, None] / D + 1e-06) * q_gain[None, :]).astype(jnp.bfloat16)
    k_norm = (k_float / jnp.sqrt(sum_k[:, None] / D + 1e-06) * k_gain[None, :]).astype(jnp.bfloat16)
    n_frames = lax.axis_size("frame")
    group_pos = frame_tok // n_frames

    def regroup(array):
        return lax.all_to_all(
            array.reshape(n_frames, group_pos, width),
            "frame",
            split_axis=0,
            concat_axis=0,
            tiled=True,
        ).reshape(frame_tok, width)

    anchor = anchor_frame[0]
    k_anchor, v_anchor = (spread(k_norm, "frame", anchor), spread(values, "frame", anchor))
    own_allowed = jnp.concatenate(
        [expand(spatial_mask[0]), jnp.ones((frame_tok, frame_tok), dtype=jnp.bool_)], axis=1
    )
    spatial = attend(
        q_norm,
        jnp.concatenate([k_norm, k_anchor], 0),
        jnp.concatenate([values, v_anchor], 0),
        own_allowed,
    )
    temporal = attend(
        regroup(q_norm), regroup(k_norm), regroup(values), expand(temporal_mask[0])
    ).astype(jnp.bfloat16)
    returned = regroup(temporal)
    return (spatial + returned.astype(jnp.float32)).astype(jnp.bfloat16)


def dot_t(a, b):
    return lax.dot_general(a, b, (((1,), (1,)), ((), ())), preferred_element_type=jnp.float32)


def softmax_parts(scores):
    top = jnp.max(scores, axis=1, keepdims=True)
    weights = jnp.exp2(scores - top)
    total = jnp.sum(weights, axis=1, keepdims=True)
    return top, weights.astype(jnp.bfloat16), total


def pack_kernel(half, n_half, pos, heads2, k_ref, v_ref, out_ref):
    for hh in range(half):
        for p in range(n_half):
            dst = hh * n_half + p
            for h in range(heads2):
                cols = slice((hh * heads2 + h) * HD, (hh * heads2 + h + 1) * HD)
                rows = slice(p * pos, (p + 1) * pos)
                out_ref[dst, h * pos : (h + 1) * pos, :] = k_ref[rows, cols]
                out_ref[dst, (heads2 + h) * pos : (heads2 + h + 1) * pos, :] = v_ref[rows, cols]


def squares_kernel(heads, q_ref, k_ref, out_ref):
    rows = []
    for ref in (q_ref, k_ref):
        total = None
        for h in range(heads):
            part = ref[:, h * HD : (h + 1) * HD].astype(jnp.float32)
            total = part * part if total is None else total + part * part
        rows.append(jnp.sum(total.T, axis=0, keepdims=True))
    pad = jnp.zeros((6, rows[0].shape[1]), jnp.float32)
    out_ref[...] = jnp.concatenate(rows + [pad], axis=0)


def own_kernel(
    n_half, pos, heads2, q_ref, k_ref, v_ref, sums_ref, qg_ref, kg_ref, bias_ref, mask_ref,
    qb_ref, own_ref, side_ref,
):
    heads = 2 * heads2
    inv = lax.rsqrt(sums_ref[...] / D + 1e-06)
    inv_t = inv.T
    inv_q, inv_k = inv_t[:, 0:1], inv_t[:, 1:2]
    tok = q_ref.shape[0]
    lses = []
    for hi in range(heads):
        cols = slice(hi * HD, (hi + 1) * HD)
        gain_q = qg_ref[:, cols] * (LOG2E / float(HD) ** 0.5)
        query = (q_ref[:, cols].astype(jnp.float32) * inv_q * gain_q).astype(jnp.bfloat16)
        keys = (k_ref[:, cols].astype(jnp.float32) * inv_k * kg_ref[:, cols]).astype(jnp.bfloat16)
        hh, h = hi // heads2, hi % heads2
        for p in range(n_half):
            qb_ref[hh * n_half + p, h * pos : (h + 1) * pos, :] = query[p * pos : (p + 1) * pos]
        parts = []
        for i in range(tok // BLOCK):
            rows = slice(i * BLOCK, (i + 1) * BLOCK)
            scores = dot_t(query[rows], keys) + bias_ref[i : i + 1, :]
            top, weights, total = softmax_parts(scores)
            out = jnp.dot(weights, v_ref[:, cols], preferred_element_type=jnp.float32)
            own_ref[rows, cols] = out / total
            parts.append(top + jnp.log2(total))
        lses.append(jnp.concatenate(parts, axis=0))
    lane = lax.broadcasted_iota(jnp.int32, (tok, HD), 1)
    packed = jnp.where(lane == heads, inv_k, 0.0)
    for hi in range(heads):
        packed = jnp.where(lane == hi, lses[hi], packed)
    rows = packed.T[: side_ref.shape[0]]
    sub = lax.broadcasted_iota(jnp.int32, rows.shape, 0)
    side_ref[...] = jnp.where(sub == heads + 1, mask_ref[...], rows)


def far_kernel(
    n, pos, heads2, q_ref, kv_ref, a0_ref, a1_ref, a2_ref, a3_ref, col_ref, acol_ref, kg_ref,
    bias_ref, out_ref,
):
    gp = pos // 2
    rows_u = n * gp
    anchors = (a0_ref, a1_ref, a2_ref, a3_ref)
    lane = lax.broadcasted_iota(jnp.int32, (rows_u, HD), 1)
    sig = [jnp.zeros((rows_u, HD), jnp.float32) for _ in range(2)]
    v_off = heads2 * pos
    for h in range(heads2):
        gain = kg_ref[h : h + 1, :]
        ka = jnp.concatenate([a[h * pos : (h + 1) * pos, :] for a in anchors], axis=0)
        va = jnp.concatenate([a[v_off + h * pos : v_off + (h + 1) * pos, :] for a in anchors], axis=0)
        ka = (ka.astype(jnp.float32) * acol_ref[:, 0:1] * gain).astype(jnp.bfloat16)
        for u in range(2):
            at = h * pos + u * gp
            query = q_ref[:, at : at + gp, :].reshape(rows_u, HD)
            keys = kv_ref[:, at : at + gp, :].reshape(rows_u, HD)
            vals = kv_ref[:, v_off + at : v_off + at + gp, :].reshape(rows_u, HD)
            keys = (keys.astype(jnp.float32) * col_ref[u, :, heads2 : heads2 + 1] * gain).astype(
                jnp.bfloat16
            )
            temporal = []
            for i in range(rows_u // BLOCK):
                rows = slice(i * BLOCK, (i + 1) * BLOCK)
                scores = dot_t(query[rows], keys) + bias_ref[2 * u + i : 2 * u + i + 1, :]
                _, weights, total = softmax_parts(scores)
                temporal.append(jnp.dot(weights, vals, preferred_element_type=jnp.float32) / total)
            top, weights, total = softmax_parts(dot_t(query, ka))
            anchored = jnp.dot(weights, va, preferred_element_type=jnp.float32)
            gap = col_ref[u, :, h : h + 1] - (top + jnp.log2(total))
            share = 1.0 / (1.0 + jnp.exp2(jnp.clip(gap, -126.0, 126.0)))
            result = jnp.concatenate(temporal, axis=0) + anchored * (share / total)
            out_ref[:, at : at + gp, :] = result.astype(jnp.bfloat16).reshape(n, gp, HD)
            sig[u] = jnp.where(lane == h, 1.0 - share, sig[u])
    for u in range(2):
        out_ref[:, v_off + u * gp : v_off + (u + 1) * gp, :] = (
            sig[u].astype(jnp.bfloat16).reshape(n, gp, HD)
        )


def join_kernel(n_half, pos, heads2, own_ref, back_ref, out_ref):
    for hh in range(2):
        for p in range(n_half):
            src = hh * n_half + p
            rows = slice(p * pos, (p + 1) * pos)
            keep = back_ref[src, heads2 * pos : (heads2 + 1) * pos, :].astype(jnp.float32)
            for h in range(heads2):
                cols = slice((hh * heads2 + h) * HD, (hh * heads2 + h + 1) * HD)
                got = back_ref[src, h * pos : (h + 1) * pos, :].astype(jnp.float32)
                out_ref[rows, cols] = (own_ref[rows, cols] * keep[:, h : h + 1] + got).astype(
                    jnp.bfloat16
                )


def call(kernel, out_shape, *args):
    return pl.pallas_call(
        kernel,
        out_shape=out_shape,
        compiler_params=pltpu.CompilerParams(vmem_limit_bytes=40 * 1024 * 1024),
    )(*args)


def exchange(array):
    return lax.all_to_all(array, "frame", split_axis=0, concat_axis=0, tiled=True)


def local_halves(
    q_raw, k_raw, values, q_gain, k_gain, spatial_mask, temporal_mask, anchor_frame
):
    tok, width = q_raw.shape
    n = lax.axis_size("frame")
    n_mp = lax.axis_size("mp")
    n_half = n // 2
    heads = width // HD
    heads2 = heads // 2
    pos = tok // n_half
    gp = pos // 2
    me = lax.axis_index("frame")
    my_half, my_quarter = me // n_half, me % n_half
    shape = jax.ShapeDtypeStruct

    kv_blocks = call(
        functools.partial(pack_kernel, 2, n_half, pos, heads2),
        shape((n, 2 * heads2 * pos, HD), jnp.bfloat16),
        k_raw,
        values,
    )
    kv_far = exchange(kv_blocks)

    sums = call(
        functools.partial(squares_kernel, heads), shape((8, tok), jnp.float32), q_raw, k_raw
    )
    total = sums
    for step in range(1, n_mp):
        total = total + lax.ppermute(sums, "mp", [(i, (i + step) % n_mp) for i in range(n_mp)])

    blocks = tok // BLOCK
    own_bias = jnp.where(expand(spatial_mask[0])[::BLOCK], 0.0, NEG)
    mask_row = jnp.zeros((1, tok), jnp.float32)
    mask_row = lax.dynamic_update_slice(
        mask_row, temporal_mask.reshape(1, blocks * blocks).astype(jnp.float32), (0, 0)
    )
    side_rows = -(-(heads + 2) // 8) * 8
    q_blocks, own, side = call(
        functools.partial(own_kernel, n_half, pos, heads2),
        (
            shape((n, heads2 * pos, HD), jnp.bfloat16),
            shape((tok, width), jnp.float32),
            shape((side_rows, tok), jnp.float32),
        ),
        q_raw,
        k_raw,
        values,
        total,
        q_gain[None, :],
        k_gain[None, :],
        own_bias,
        mask_row,
    )
    sides = lax.all_gather(side, "frame", axis=0)

    lse = lax.dynamic_slice(
        sides, (0, my_half * heads2, my_quarter * pos), (n, heads2, pos)
    )
    inv_k = lax.dynamic_slice(sides, (0, heads, my_quarter * pos), (n, 1, pos))
    columns = jnp.concatenate([lse, inv_k], axis=1).reshape(n, heads2 + 1, 2, gp)
    columns = jnp.transpose(columns, (2, 0, 3, 1)).reshape(2, n * gp, heads2 + 1)
    anchor = anchor_frame[0]
    inv_anchor = lax.dynamic_slice(sides, (anchor, heads, 0), (1, 1, tok)).reshape(n_half, pos)
    inv_anchor = jnp.concatenate(
        [lax.dynamic_slice(inv_anchor, (my_quarter ^ s, 0), (1, pos)) for s in range(n_half)], 0
    ).reshape(tok, 1)
    masks = lax.dynamic_slice(
        sides, (2 * my_quarter, heads + 1, 0), (2, 1, blocks * blocks)
    ).reshape(2, blocks, blocks)
    far_bias = jnp.concatenate(
        [jnp.where(expand(masks[u])[::BLOCK], 0.0, NEG) for u in range(2)], axis=0
    )
    gain_half = lax.dynamic_slice(k_gain.reshape(heads, HD), (my_half * heads2, 0), (heads2, HD))

    q_far = exchange(q_blocks)
    mine = lax.dynamic_index_in_dim(kv_far, anchor, 0, keepdims=False)
    anchors = [mine] + [
        lax.ppermute(mine, "frame", [(i, i ^ s) for i in range(n)]) for s in range(1, n_half)
    ]
    result = call(
        functools.partial(far_kernel, n, pos, heads2),
        shape((n, (heads2 + 1) * pos, HD), jnp.bfloat16),
        q_far,
        kv_far,
        *anchors,
        columns,
        inv_anchor,
        gain_half,
        far_bias,
    )
    back = exchange(result)
    return call(
        functools.partial(join_kernel, n_half, pos, heads2),
        shape((tok, width), jnp.bfloat16),
        own,
        back,
    )


def solution(mesh):
    n = mesh.shape["frame"]

    def local(*args):
        tok, width = args[0].shape
        fits = n == 8 and (width // HD) % 2 == 0 and tok % (n * 16) == 0
        return local_halves(*args) if fits else local_general(*args)

    return jax.shard_map(
        local,
        mesh=mesh,
        in_specs=(
            P("frame", "mp"),
            P("frame", "mp"),
            P("frame", "mp"),
            P("mp"),
            P("mp"),
            P("frame", None, None),
            P("frame", None, None),
            P(),
        ),
        out_specs=P("frame", "mp"),
        check_vma=False,
    )
```

```python
import functools

import jax
import jax.numpy as jnp
from jax import lax
from jax.experimental import pallas as pl
from jax.experimental.pallas import tpu as pltpu
from jax.sharding import PartitionSpec as P

D = 5120
HD = 128
BLOCK = 128
LOG2E = 1.4426950408889634
NEG = -1e30


def spread(value, axis, source):
    kept = jnp.where(lax.axis_index(axis) == source, value, 0).astype(value.dtype)
    return lax.psum(kept, axis)


def expand(block_mask):
    count = block_mask.shape[0]
    allowed = (block_mask == 1) | jnp.eye(count, dtype=jnp.bool_)
    return jnp.repeat(jnp.repeat(allowed, BLOCK, axis=0), BLOCK, axis=1)


def attend(query, keys, vals, allowed):
    rows = query.shape[0]
    width = query.shape[1]
    heads_dev = width // HD
    query3 = jnp.transpose(query.reshape(rows, heads_dev, HD), (1, 0, 2))
    keys3 = jnp.transpose(keys.reshape(keys.shape[0], heads_dev, HD), (1, 0, 2))
    vals3 = jnp.transpose(vals.reshape(vals.shape[0], heads_dev, HD), (1, 0, 2))
    scale = jnp.sqrt(jnp.float32(HD))

    def one_head(items):
        head_q, head_k, head_v = items
        scores = jnp.einsum("qd,kd->qk", head_q, head_k, preferred_element_type=jnp.float32) / scale
        scores = jnp.where(allowed, scores, -jnp.inf)
        probs = jax.nn.softmax(scores, axis=-1).astype(jnp.bfloat16)
        return jnp.dot(probs, head_v, preferred_element_type=jnp.float32)

    output = lax.map(one_head, (query3, keys3, vals3))
    return jnp.transpose(output, (1, 0, 2)).reshape(rows, width)


def local_general(
    q_raw, k_raw, values, q_gain, k_gain, spatial_mask, temporal_mask, anchor_frame
):
    frame_tok = q_raw.shape[0]
    width = q_raw.shape[1]
    q_float = q_raw.astype(jnp.float32)
    k_float = k_raw.astype(jnp.float32)
    sum_q, sum_k = lax.psum(
        (jnp.sum(q_float * q_float, axis=1), jnp.sum(k_float * k_float, axis=1)), "mp"
    )
    q_norm = (q_float / jnp.sqrt(sum_q[:, None] / D + 1e-06) * q_gain[None, :]).astype(jnp.bfloat16)
    k_norm = (k_float / jnp.sqrt(sum_k[:, None] / D + 1e-06) * k_gain[None, :]).astype(jnp.bfloat16)
    n_frames = lax.axis_size("frame")
    group_pos = frame_tok // n_frames

    def regroup(array):
        return lax.all_to_all(
            array.reshape(n_frames, group_pos, width),
            "frame",
            split_axis=0,
            concat_axis=0,
            tiled=True,
        ).reshape(frame_tok, width)

    anchor = anchor_frame[0]
    k_anchor, v_anchor = (spread(k_norm, "frame", anchor), spread(values, "frame", anchor))
    own_allowed = jnp.concatenate(
        [expand(spatial_mask[0]), jnp.ones((frame_tok, frame_tok), dtype=jnp.bool_)], axis=1
    )
    spatial = attend(
        q_norm,
        jnp.concatenate([k_norm, k_anchor], 0),
        jnp.concatenate([values, v_anchor], 0),
        own_allowed,
    )
    temporal = attend(
        regroup(q_norm), regroup(k_norm), regroup(values), expand(temporal_mask[0])
    ).astype(jnp.bfloat16)
    returned = regroup(temporal)
    return (spatial + returned.astype(jnp.float32)).astype(jnp.bfloat16)


def dot_t(a, b):
    return lax.dot_general(a, b, (((1,), (1,)), ((), ())), preferred_element_type=jnp.float32)


def softmax_parts(scores):
    top = jnp.max(scores, axis=1, keepdims=True)
    weights = jnp.exp2(scores - top)
    total = jnp.sum(weights, axis=1, keepdims=True)
    return top, weights.astype(jnp.bfloat16), total


def pack_kernel(half, n_half, pos, heads2, k_ref, v_ref, out_ref):
    for hh in range(half):
        for p in range(n_half):
            dst = hh * n_half + p
            for h in range(heads2):
                cols = slice((hh * heads2 + h) * HD, (hh * heads2 + h + 1) * HD)
                rows = slice(p * pos, (p + 1) * pos)
                out_ref[dst, h * pos : (h + 1) * pos, :] = k_ref[rows, cols]
                out_ref[dst, (heads2 + h) * pos : (heads2 + h + 1) * pos, :] = v_ref[rows, cols]


def squares_kernel(heads, q_ref, k_ref, out_ref):
    rows = []
    for ref in (q_ref, k_ref):
        total = None
        for h in range(heads):
            part = ref[:, h * HD : (h + 1) * HD].astype(jnp.float32)
            total = part * part if total is None else total + part * part
        rows.append(jnp.sum(total.T, axis=0, keepdims=True))
    pad = jnp.zeros((6, rows[0].shape[1]), jnp.float32)
    out_ref[...] = jnp.concatenate(rows + [pad], axis=0)


def own_kernel(
    n_half, pos, heads2, q_ref, k_ref, v_ref, sums_ref, qg_ref, kg_ref, bias_ref, mask_ref,
    qb_ref, own_ref, side_ref,
):
    heads = 2 * heads2
    inv = lax.rsqrt(sums_ref[...] / D + 1e-06)
    inv_t = inv.T
    inv_q, inv_k = inv_t[:, 0:1], inv_t[:, 1:2]
    tok = q_ref.shape[0]
    lses = []
    for hi in range(heads):
        cols = slice(hi * HD, (hi + 1) * HD)
        gain_q = qg_ref[:, cols] * (LOG2E / float(HD) ** 0.5)
        query = (q_ref[:, cols].astype(jnp.float32) * inv_q * gain_q).astype(jnp.bfloat16)
        keys = (k_ref[:, cols].astype(jnp.float32) * inv_k * kg_ref[:, cols]).astype(jnp.bfloat16)
        hh, h = hi // heads2, hi % heads2
        for p in range(n_half):
            qb_ref[hh * n_half + p, h * pos : (h + 1) * pos, :] = query[p * pos : (p + 1) * pos]
        parts = []
        for i in range(tok // BLOCK):
            rows = slice(i * BLOCK, (i + 1) * BLOCK)
            scores = dot_t(query[rows], keys) + bias_ref[i : i + 1, :]
            top, weights, total = softmax_parts(scores)
            out = jnp.dot(weights, v_ref[:, cols], preferred_element_type=jnp.float32)
            own_ref[rows, cols] = out / total
            parts.append(top + jnp.log2(total))
        lses.append(jnp.concatenate(parts, axis=0))
    lane = lax.broadcasted_iota(jnp.int32, (tok, HD), 1)
    packed = jnp.where(lane == heads, inv_k, 0.0)
    for hi in range(heads):
        packed = jnp.where(lane == hi, lses[hi], packed)
    rows = packed.T[: side_ref.shape[0]]
    sub = lax.broadcasted_iota(jnp.int32, rows.shape, 0)
    side_ref[...] = jnp.where(sub == heads + 1, mask_ref[...], rows)


def far_kernel(
    n, pos, heads2, q_ref, kv_ref, a0_ref, a1_ref, a2_ref, a3_ref, col_ref, acol_ref, kg_ref,
    bias_ref, out_ref,
):
    gp = pos // 2
    rows_u = n * gp
    anchors = (a0_ref, a1_ref, a2_ref, a3_ref)
    lane = lax.broadcasted_iota(jnp.int32, (rows_u, HD), 1)
    sig = [jnp.zeros((rows_u, HD), jnp.float32) for _ in range(2)]
    v_off = heads2 * pos
    for h in range(heads2):
        gain = kg_ref[h : h + 1, :]
        ka = jnp.concatenate([a[h * pos : (h + 1) * pos, :] for a in anchors], axis=0)
        va = jnp.concatenate([a[v_off + h * pos : v_off + (h + 1) * pos, :] for a in anchors], axis=0)
        ka = (ka.astype(jnp.float32) * acol_ref[:, 0:1] * gain).astype(jnp.bfloat16)
        for u in range(2):
            at = h * pos + u * gp
            query = q_ref[:, at : at + gp, :].reshape(rows_u, HD)
            keys = kv_ref[:, at : at + gp, :].reshape(rows_u, HD)
            vals = kv_ref[:, v_off + at : v_off + at + gp, :].reshape(rows_u, HD)
            keys = (keys.astype(jnp.float32) * col_ref[u, :, heads2 : heads2 + 1] * gain).astype(
                jnp.bfloat16
            )
            temporal = []
            for i in range(rows_u // BLOCK):
                rows = slice(i * BLOCK, (i + 1) * BLOCK)
                scores = dot_t(query[rows], keys) + bias_ref[2 * u + i : 2 * u + i + 1, :]
                _, weights, total = softmax_parts(scores)
                temporal.append(jnp.dot(weights, vals, preferred_element_type=jnp.float32) / total)
            top, weights, total = softmax_parts(dot_t(query, ka))
            anchored = jnp.dot(weights, va, preferred_element_type=jnp.float32)
            gap = col_ref[u, :, h : h + 1] - (top + jnp.log2(total))
            share = 1.0 / (1.0 + jnp.exp2(jnp.clip(gap, -126.0, 126.0)))
            result = jnp.concatenate(temporal, axis=0) + anchored * (share / total)
            out_ref[:, at : at + gp, :] = result.astype(jnp.bfloat16).reshape(n, gp, HD)
            sig[u] = jnp.where(lane == h, 1.0 - share, sig[u])
    for u in range(2):
        out_ref[:, v_off + u * gp : v_off + (u + 1) * gp, :] = (
            sig[u].astype(jnp.bfloat16).reshape(n, gp, HD)
        )


def join_kernel(n_half, pos, heads2, own_ref, back_ref, out_ref):
    for hh in range(2):
        for p in range(n_half):
            src = hh * n_half + p
            rows = slice(p * pos, (p + 1) * pos)
            keep = back_ref[src, heads2 * pos : (heads2 + 1) * pos, :].astype(jnp.float32)
            for h in range(heads2):
                cols = slice((hh * heads2 + h) * HD, (hh * heads2 + h + 1) * HD)
                got = back_ref[src, h * pos : (h + 1) * pos, :].astype(jnp.float32)
                out_ref[rows, cols] = (own_ref[rows, cols] * keep[:, h : h + 1] + got).astype(
                    jnp.bfloat16
                )


def call(kernel, out_shape, *args):
    return pl.pallas_call(
        kernel,
        out_shape=out_shape,
        compiler_params=pltpu.CompilerParams(vmem_limit_bytes=40 * 1024 * 1024),
    )(*args)


def exchange(array):
    return lax.all_to_all(array, "frame", split_axis=0, concat_axis=0, tiled=True)


def local_halves(
    q_raw, k_raw, values, q_gain, k_gain, spatial_mask, temporal_mask, anchor_frame
):
    tok, width = q_raw.shape
    n = lax.axis_size("frame")
    n_mp = lax.axis_size("mp")
    n_half = n // 2
    heads = width // HD
    heads2 = heads // 2
    pos = tok // n_half
    gp = pos // 2
    me = lax.axis_index("frame")
    my_half, my_quarter = me // n_half, me % n_half
    shape = jax.ShapeDtypeStruct

    kv_blocks = call(
        functools.partial(pack_kernel, 2, n_half, pos, heads2),
        shape((n, 2 * heads2 * pos, HD), jnp.bfloat16),
        k_raw,
        values,
    )
    kv_far = exchange(kv_blocks)

    sums = call(
        functools.partial(squares_kernel, heads), shape((8, tok), jnp.float32), q_raw, k_raw
    )
    total = sums
    for step in range(1, n_mp):
        total = total + lax.ppermute(sums, "mp", [(i, (i + step) % n_mp) for i in range(n_mp)])

    blocks = tok // BLOCK
    own_bias = jnp.where(expand(spatial_mask[0])[::BLOCK], 0.0, NEG)
    mask_row = jnp.zeros((1, tok), jnp.float32)
    mask_row = lax.dynamic_update_slice(
        mask_row, temporal_mask.reshape(1, blocks * blocks).astype(jnp.float32), (0, 0)
    )
    side_rows = -(-(heads + 2) // 8) * 8
    q_blocks, own, side = call(
        functools.partial(own_kernel, n_half, pos, heads2),
        (
            shape((n, heads2 * pos, HD), jnp.bfloat16),
            shape((tok, width), jnp.float32),
            shape((side_rows, tok), jnp.float32),
        ),
        q_raw,
        k_raw,
        values,
        total,
        q_gain[None, :],
        k_gain[None, :],
        own_bias,
        mask_row,
    )
    sides = jnp.zeros((n,) + side.shape, side.dtype)
    for s in range(n):
        came = side
        if s > 0:
            came = lax.ppermute(side, "frame", [(i, i ^ s) for i in range(n)])
        sides = lax.dynamic_update_slice(sides, came[None], (me ^ s, 0, 0))

    lse = lax.dynamic_slice(
        sides, (0, my_half * heads2, my_quarter * pos), (n, heads2, pos)
    )
    inv_k = lax.dynamic_slice(sides, (0, heads, my_quarter * pos), (n, 1, pos))
    columns = jnp.concatenate([lse, inv_k], axis=1).reshape(n, heads2 + 1, 2, gp)
    columns = jnp.transpose(columns, (2, 0, 3, 1)).reshape(2, n * gp, heads2 + 1)
    anchor = anchor_frame[0]
    inv_anchor = lax.dynamic_slice(sides, (anchor, heads, 0), (1, 1, tok)).reshape(n_half, pos)
    inv_anchor = jnp.concatenate(
        [lax.dynamic_slice(inv_anchor, (my_quarter ^ s, 0), (1, pos)) for s in range(n_half)], 0
    ).reshape(tok, 1)
    masks = lax.dynamic_slice(
        sides, (2 * my_quarter, heads + 1, 0), (2, 1, blocks * blocks)
    ).reshape(2, blocks, blocks)
    far_bias = jnp.concatenate(
        [jnp.where(expand(masks[u])[::BLOCK], 0.0, NEG) for u in range(2)], axis=0
    )
    gain_half = lax.dynamic_slice(k_gain.reshape(heads, HD), (my_half * heads2, 0), (heads2, HD))

    q_far = exchange(q_blocks)
    mine = lax.dynamic_index_in_dim(kv_far, anchor, 0, keepdims=False)
    anchors = [mine] + [
        lax.ppermute(mine, "frame", [(i, i ^ s) for i in range(n)]) for s in range(1, n_half)
    ]
    result = call(
        functools.partial(far_kernel, n, pos, heads2),
        shape((n, (heads2 + 1) * pos, HD), jnp.bfloat16),
        q_far,
        kv_far,
        *anchors,
        columns,
        inv_anchor,
        gain_half,
        far_bias,
    )
    back = exchange(result)
    return call(
        functools.partial(join_kernel, n_half, pos, heads2),
        shape((tok, width), jnp.bfloat16),
        own,
        back,
    )


def solution(mesh):
    n = mesh.shape["frame"]

    def local(*args):
        tok, width = args[0].shape
        fits = n == 8 and (width // HD) % 2 == 0 and tok % (n * 16) == 0
        return local_halves(*args) if fits else local_general(*args)

    return jax.shard_map(
        local,
        mesh=mesh,
        in_specs=(
            P("frame", "mp"),
            P("frame", "mp"),
            P("frame", "mp"),
            P("mp"),
            P("mp"),
            P("frame", None, None),
            P("frame", None, None),
            P(),
        ),
        out_specs=P("frame", "mp"),
        check_vma=False,
    )
```

```python
import functools

import jax
import jax.numpy as jnp
from jax import lax
from jax.experimental import pallas as pl
from jax.experimental.pallas import tpu as pltpu
from jax.sharding import PartitionSpec as P

D = 5120
HD = 128
BLOCK = 128
LOG2E = 1.4426950408889634
NEG = -1e30


def spread(value, axis, source):
    kept = jnp.where(lax.axis_index(axis) == source, value, 0).astype(value.dtype)
    return lax.psum(kept, axis)


def expand(block_mask):
    count = block_mask.shape[0]
    allowed = (block_mask == 1) | jnp.eye(count, dtype=jnp.bool_)
    return jnp.repeat(jnp.repeat(allowed, BLOCK, axis=0), BLOCK, axis=1)


def attend(query, keys, vals, allowed):
    rows = query.shape[0]
    width = query.shape[1]
    heads_dev = width // HD
    query3 = jnp.transpose(query.reshape(rows, heads_dev, HD), (1, 0, 2))
    keys3 = jnp.transpose(keys.reshape(keys.shape[0], heads_dev, HD), (1, 0, 2))
    vals3 = jnp.transpose(vals.reshape(vals.shape[0], heads_dev, HD), (1, 0, 2))
    scale = jnp.sqrt(jnp.float32(HD))

    def one_head(items):
        head_q, head_k, head_v = items
        scores = jnp.einsum("qd,kd->qk", head_q, head_k, preferred_element_type=jnp.float32) / scale
        scores = jnp.where(allowed, scores, -jnp.inf)
        probs = jax.nn.softmax(scores, axis=-1).astype(jnp.bfloat16)
        return jnp.dot(probs, head_v, preferred_element_type=jnp.float32)

    output = lax.map(one_head, (query3, keys3, vals3))
    return jnp.transpose(output, (1, 0, 2)).reshape(rows, width)


def local_general(
    q_raw, k_raw, values, q_gain, k_gain, spatial_mask, temporal_mask, anchor_frame
):
    frame_tok = q_raw.shape[0]
    width = q_raw.shape[1]
    q_float = q_raw.astype(jnp.float32)
    k_float = k_raw.astype(jnp.float32)
    sum_q, sum_k = lax.psum(
        (jnp.sum(q_float * q_float, axis=1), jnp.sum(k_float * k_float, axis=1)), "mp"
    )
    q_norm = (q_float / jnp.sqrt(sum_q[:, None] / D + 1e-06) * q_gain[None, :]).astype(jnp.bfloat16)
    k_norm = (k_float / jnp.sqrt(sum_k[:, None] / D + 1e-06) * k_gain[None, :]).astype(jnp.bfloat16)
    n_frames = lax.axis_size("frame")
    group_pos = frame_tok // n_frames

    def regroup(array):
        return lax.all_to_all(
            array.reshape(n_frames, group_pos, width),
            "frame",
            split_axis=0,
            concat_axis=0,
            tiled=True,
        ).reshape(frame_tok, width)

    anchor = anchor_frame[0]
    k_anchor, v_anchor = (spread(k_norm, "frame", anchor), spread(values, "frame", anchor))
    own_allowed = jnp.concatenate(
        [expand(spatial_mask[0]), jnp.ones((frame_tok, frame_tok), dtype=jnp.bool_)], axis=1
    )
    spatial = attend(
        q_norm,
        jnp.concatenate([k_norm, k_anchor], 0),
        jnp.concatenate([values, v_anchor], 0),
        own_allowed,
    )
    temporal = attend(
        regroup(q_norm), regroup(k_norm), regroup(values), expand(temporal_mask[0])
    ).astype(jnp.bfloat16)
    returned = regroup(temporal)
    return (spatial + returned.astype(jnp.float32)).astype(jnp.bfloat16)


ROWS = 16
LANES = 32


def dot_t(a, b):
    return lax.dot_general(a, b, (((1,), (1,)), ((), ())), preferred_element_type=jnp.float32)


def weigh(weights, vals):
    ones = jnp.ones(vals.shape, vals.dtype)
    both = jnp.dot(
        weights.astype(jnp.bfloat16),
        jnp.concatenate([vals, ones], axis=1),
        preferred_element_type=jnp.float32,
    )
    return both[:, :HD], both[:, HD:]


def blocked_scores(query, keys, flag, i):
    scores = dot_t(query, keys)
    near = scores[:, i * BLOCK : (i + 1) * BLOCK]
    away = scores[:, (1 - i) * BLOCK : (2 - i) * BLOCK] + flag
    return jnp.concatenate([near, away] if i == 0 else [away, near], axis=1)


def fold(parts, lane):
    out = parts[0]
    for g in range(1, len(parts)):
        out = jnp.where(lane // LANES == g, parts[g], out)
    return out


def pack_kernel(n_half, pos, wide, k_ref, v_ref, out_ref, sems):
    copies = []
    for hh in range(2):
        for p in range(n_half):
            dst = hh * n_half + p
            for t, ref in enumerate((k_ref, v_ref)):
                copies.append(
                    pltpu.make_async_copy(
                        ref.at[pl.ds(p * pos, pos), pl.ds(hh * wide, wide)],
                        out_ref.at[dst, :, pl.ds(t * wide, wide)],
                        sems.at[2 * dst + t],
                    )
                )
    for copy in copies:
        copy.start()
    for copy in copies:
        copy.wait()


def squares_kernel(heads, q_ref, k_ref, out_ref):
    rows = []
    for ref in (q_ref, k_ref):
        total = None
        for h in range(heads):
            part = ref[:, h * HD : (h + 1) * HD].astype(jnp.float32)
            total = part * part if total is None else total + part * part
        rows.append(jnp.sum(total.T, axis=0, keepdims=True))
    pad = jnp.zeros((6, rows[0].shape[1]), jnp.float32)
    out_ref[...] = jnp.concatenate(rows + [pad], axis=0)


def own_kernel(
    n_half, pos, heads2, q_ref, k_ref, v_ref, sums_ref, qg_ref, kg_ref, flag_ref, qb_ref, own_ref
):
    inv = lax.rsqrt(sums_ref[...] / D + 1e-06)
    inv_t = inv.T
    inv_q, inv_k = inv_t[:, 0:1], inv_t[:, 1:2]
    tok = q_ref.shape[0]
    lane = lax.broadcasted_iota(jnp.int32, (tok, HD), 1) % LANES
    short = lax.broadcasted_iota(jnp.int32, (ROWS, HD), 1)
    for hh in range(2):
        side = jnp.zeros((tok, HD), jnp.bfloat16)
        for h in range(heads2):
            cols = slice((hh * heads2 + h) * HD, (hh * heads2 + h + 1) * HD)
            gain_q = qg_ref[:, cols] * (LOG2E / float(HD) ** 0.5)
            query = (q_ref[:, cols].astype(jnp.float32) * inv_q * gain_q).astype(jnp.bfloat16)
            keys = (k_ref[:, cols].astype(jnp.float32) * inv_k * kg_ref[:, cols]).astype(
                jnp.bfloat16
            )
            for p in range(n_half):
                qb_ref[hh * n_half + p, h * pos : (h + 1) * pos, :] = query[
                    p * pos : (p + 1) * pos
                ]
            lse = []
            for i in range(tok // BLOCK):
                rows = slice(i * BLOCK, (i + 1) * BLOCK)
                scores = blocked_scores(query[rows], keys, flag_ref[i : i + 1, :], i)
                top = jnp.max(scores, axis=1, keepdims=True)
                out, total = weigh(jnp.exp2(scores - top), v_ref[:, cols])
                own_ref[rows, cols] = out / total
                lse.append(top + jnp.log2(total))
            rest = jnp.concatenate(lse, axis=0)
            for part in range(3):
                piece = rest.astype(jnp.bfloat16)
                side = jnp.where(lane == 3 * h + part, piece, side)
                rest = rest - piece.astype(jnp.float32)
        for p in range(n_half):
            at = p * pos
            groups = [side[at + g * ROWS : at + (g + 1) * ROWS] for g in range(pos // ROWS)]
            qb_ref[hh * n_half + p, heads2 * pos : heads2 * pos + ROWS, :] = fold(groups, short)


def far_kernel(
    n, pos, heads2, q_ref, kv_ref, a0_ref, a1_ref, a2_ref, a3_ref, col_ref, acol_ref, kg_ref,
    flag_ref, out_ref,
):
    gp = pos // 2
    rows_u = n * gp
    wide = heads2 * HD
    per = gp // ROWS
    anchors = (a0_ref, a1_ref, a2_ref, a3_ref)
    lane = lax.broadcasted_iota(jnp.int32, (rows_u, HD), 1) % LANES
    group = lax.broadcasted_iota(jnp.int32, (n, ROWS, HD), 2) // LANES
    at_side = heads2 * pos
    came = q_ref[:, at_side : at_side + ROWS, :].astype(jnp.float32).reshape(n * ROWS, HD)
    lses = []
    for u in range(2):
        turned = []
        for g in range(u * per, (u + 1) * per):
            turn = came if g == 0 else pltpu.roll(came, HD - LANES * g, 1)
            turned.append(turn.reshape(n, ROWS, HD))
        lses.append(jnp.concatenate(turned, axis=1).reshape(rows_u, HD))
    sig = [jnp.zeros((rows_u, HD), jnp.float32) for _ in range(2)]
    for h in range(heads2):
        cols = slice(h * HD, (h + 1) * HD)
        vcols = slice(wide + h * HD, wide + (h + 1) * HD)
        gain = kg_ref[h : h + 1, :]
        ka = jnp.concatenate([a[:, cols] for a in anchors], axis=0)
        va = jnp.concatenate([a[:, vcols] for a in anchors], axis=0)
        ka = (ka.astype(jnp.float32) * acol_ref[:, 0:1] * gain).astype(jnp.bfloat16)
        for u in range(2):
            at = h * pos + u * gp
            span = slice(u * gp, (u + 1) * gp)
            query = q_ref[:, at : at + gp, :].reshape(rows_u, HD)
            keys = kv_ref[:, span, cols].reshape(rows_u, HD)
            vals = kv_ref[:, span, vcols].reshape(rows_u, HD)
            keys = (keys.astype(jnp.float32) * col_ref[u] * gain).astype(jnp.bfloat16)
            lse = lses[u][:, 3 * h : 3 * h + 1]
            lse = lse + lses[u][:, 3 * h + 1 : 3 * h + 2] + lses[u][:, 3 * h + 2 : 3 * h + 3]
            keep = []
            for i in range(rows_u // BLOCK):
                rows = slice(i * BLOCK, (i + 1) * BLOCK)
                flag = flag_ref[2 * u + i : 2 * u + i + 1, :]
                scores = blocked_scores(query[rows], keys, flag, i)
                top = jnp.max(scores, axis=1, keepdims=True)
                out, total = weigh(jnp.exp2(scores - top), vals)
                temporal = out / total
                scores = dot_t(query[rows], ka)
                top = jnp.maximum(jnp.max(scores, axis=1, keepdims=True), lse[rows])
                own = jnp.exp2(lse[rows] - top)
                out, total = weigh(jnp.exp2(scores - top), va)
                scale = 1.0 / (total + own)
                result = temporal + out * scale
                keep.append(own * scale)
                f0 = i * BLOCK // gp
                out_ref[f0 : f0 + BLOCK // gp, at : at + gp, :] = result.astype(
                    jnp.bfloat16
                ).reshape(BLOCK // gp, gp, HD)
            sig[u] = jnp.where(lane == h, jnp.concatenate(keep, axis=0), sig[u])
    groups = []
    for u in range(2):
        back = sig[u].reshape(n, gp, HD)
        groups += [back[:, g * ROWS : (g + 1) * ROWS, :] for g in range(per)]
    out_ref[:, at_side : at_side + ROWS, :] = fold(
        groups, group * LANES
    ).astype(jnp.bfloat16)


def join_kernel(n_half, pos, heads2, own_ref, back_ref, out_ref):
    for hh in range(2):
        for p in range(n_half):
            src = hh * n_half + p
            rows = slice(p * pos, (p + 1) * pos)
            side = back_ref[src, heads2 * pos : heads2 * pos + ROWS, :].astype(jnp.float32)
            keep = jnp.concatenate(
                [
                    side if g == 0 else pltpu.roll(side, HD - LANES * g, 1)
                    for g in range(pos // ROWS)
                ],
                axis=0,
            )
            for h in range(heads2):
                cols = slice((hh * heads2 + h) * HD, (hh * heads2 + h + 1) * HD)
                got = back_ref[src, h * pos : (h + 1) * pos, :].astype(jnp.float32)
                out_ref[rows, cols] = (own_ref[rows, cols] * keep[:, h : h + 1] + got).astype(
                    jnp.bfloat16
                )


def call(kernel, out_shape, *args, **more):
    return pl.pallas_call(
        kernel,
        out_shape=out_shape,
        compiler_params=pltpu.CompilerParams(vmem_limit_bytes=40 * 1024 * 1024),
        **more,
    )(*args)


def exchange(array):
    return lax.all_to_all(array, "frame", split_axis=0, concat_axis=0, tiled=True)


def pairwise(array, axis, step):
    size = lax.axis_size(axis)
    return lax.ppermute(array, axis, [(i, i ^ step) for i in range(size)])


def local_halves(
    q_raw, k_raw, values, q_gain, k_gain, spatial_mask, temporal_mask, anchor_frame
):
    tok, width = q_raw.shape
    n = lax.axis_size("frame")
    n_mp = lax.axis_size("mp")
    n_half = n // 2
    heads = width // HD
    heads2 = heads // 2
    wide = heads2 * HD
    pos = tok // n_half
    gp = pos // 2
    blocks = tok // BLOCK
    me = lax.axis_index("frame")
    my_half, my_quarter = me // n_half, me % n_half
    shape = jax.ShapeDtypeStruct

    kv_blocks = call(
        functools.partial(pack_kernel, n_half, pos, wide),
        shape((n, pos, 2 * wide), jnp.bfloat16),
        k_raw,
        values,
        in_specs=[pl.BlockSpec(memory_space=pltpu.HBM)] * 2,
        out_specs=pl.BlockSpec(memory_space=pltpu.HBM),
        scratch_shapes=[pltpu.SemaphoreType.DMA((2 * n,))],
    )
    kv_far = exchange(kv_blocks)

    sums = call(
        functools.partial(squares_kernel, heads), shape((8, tok), jnp.float32), q_raw, k_raw
    )
    total = sums
    for step in range(1, n_mp):
        total = total + lax.ppermute(sums, "mp", [(i, (i + step) % n_mp) for i in range(n_mp)])

    sides = jnp.zeros((2 * n, tok), jnp.float32)
    sides = lax.dynamic_update_slice(sides, lax.rsqrt(total[1:2] / D + 1e-06), (me, 0))
    sides = lax.dynamic_update_slice(
        sides,
        temporal_mask.reshape(1, blocks * blocks).astype(jnp.float32),
        (n, me * blocks * blocks),
    )
    step = 1
    while step < n:
        sides = sides + pairwise(sides, "frame", step)
        step *= 2

    def flags(mask):
        away = jnp.stack([mask[..., i, 1 - i] for i in range(blocks)], axis=-1).reshape(-1, 1)
        return jnp.broadcast_to(jnp.where(away == 1, 0.0, NEG), (away.shape[0], BLOCK))

    q_blocks, own = call(
        functools.partial(own_kernel, n_half, pos, heads2),
        (
            shape((n, heads2 * pos + ROWS, HD), jnp.bfloat16),
            shape((tok, width), jnp.float32),
        ),
        q_raw,
        k_raw,
        values,
        total,
        q_gain[None, :],
        k_gain[None, :],
        flags(spatial_mask),
    )
    q_far = exchange(q_blocks)

    inv_k = lax.dynamic_slice(sides, (0, my_quarter * pos), (n, pos)).reshape(n, 2, gp)
    inv_k = jnp.transpose(inv_k, (1, 0, 2)).reshape(2, n * gp, 1)
    anchor = anchor_frame[0]
    inv_anchor = lax.dynamic_slice(sides, (anchor, 0), (1, tok)).reshape(n_half, pos)
    inv_anchor = jnp.concatenate(
        [lax.dynamic_slice(inv_anchor, (my_quarter ^ s, 0), (1, pos)) for s in range(n_half)], 0
    ).reshape(tok, 1)
    masks = lax.dynamic_slice(
        sides, (n, 2 * my_quarter * blocks * blocks), (1, 2 * blocks * blocks)
    ).reshape(2, blocks, blocks)
    gain_half = lax.dynamic_slice(k_gain.reshape(heads, HD), (my_half * heads2, 0), (heads2, HD))

    mine = lax.dynamic_index_in_dim(kv_far, anchor, 0, keepdims=False)
    anchors = [mine] + [pairwise(mine, "frame", s) for s in range(1, n_half)]
    result = call(
        functools.partial(far_kernel, n, pos, heads2),
        shape((n, heads2 * pos + ROWS, HD), jnp.bfloat16),
        q_far,
        kv_far,
        *anchors,
        inv_k,
        inv_anchor,
        gain_half,
        flags(masks),
    )
    back = exchange(result)
    return call(
        functools.partial(join_kernel, n_half, pos, heads2),
        shape((tok, width), jnp.bfloat16),
        own,
        back,
    )


def solution(mesh):
    n = mesh.shape["frame"]

    def local(*args):
        tok, width = args[0].shape
        fits = n == 8 and (width // HD) % 2 == 0 and tok == 2 * BLOCK
        return local_halves(*args) if fits else local_general(*args)

    return jax.shard_map(
        local,
        mesh=mesh,
        in_specs=(
            P("frame", "mp"),
            P("frame", "mp"),
            P("frame", "mp"),
            P("mp"),
            P("mp"),
            P("frame", None, None),
            P("frame", None, None),
            P(),
        ),
        out_specs=P("frame", "mp"),
        check_vma=False,
    )
```

```python
import functools

import jax
import jax.numpy as jnp
from jax import lax
from jax.experimental import pallas as pl
from jax.experimental.pallas import tpu as pltpu
from jax.sharding import PartitionSpec as P

D = 5120
HD = 128
BLOCK = 128
LOG2E = 1.4426950408889634
NEG = -1e30


def spread(value, axis, source):
    kept = jnp.where(lax.axis_index(axis) == source, value, 0).astype(value.dtype)
    return lax.psum(kept, axis)


def expand(block_mask):
    count = block_mask.shape[0]
    allowed = (block_mask == 1) | jnp.eye(count, dtype=jnp.bool_)
    return jnp.repeat(jnp.repeat(allowed, BLOCK, axis=0), BLOCK, axis=1)


def attend(query, keys, vals, allowed):
    rows = query.shape[0]
    width = query.shape[1]
    heads_dev = width // HD
    query3 = jnp.transpose(query.reshape(rows, heads_dev, HD), (1, 0, 2))
    keys3 = jnp.transpose(keys.reshape(keys.shape[0], heads_dev, HD), (1, 0, 2))
    vals3 = jnp.transpose(vals.reshape(vals.shape[0], heads_dev, HD), (1, 0, 2))
    scale = jnp.sqrt(jnp.float32(HD))

    def one_head(items):
        head_q, head_k, head_v = items
        scores = jnp.einsum("qd,kd->qk", head_q, head_k, preferred_element_type=jnp.float32) / scale
        scores = jnp.where(allowed, scores, -jnp.inf)
        probs = jax.nn.softmax(scores, axis=-1).astype(jnp.bfloat16)
        return jnp.dot(probs, head_v, preferred_element_type=jnp.float32)

    output = lax.map(one_head, (query3, keys3, vals3))
    return jnp.transpose(output, (1, 0, 2)).reshape(rows, width)


def local_general(
    q_raw, k_raw, values, q_gain, k_gain, spatial_mask, temporal_mask, anchor_frame
):
    frame_tok = q_raw.shape[0]
    width = q_raw.shape[1]
    q_float = q_raw.astype(jnp.float32)
    k_float = k_raw.astype(jnp.float32)
    sum_q, sum_k = lax.psum(
        (jnp.sum(q_float * q_float, axis=1), jnp.sum(k_float * k_float, axis=1)), "mp"
    )
    q_norm = (q_float / jnp.sqrt(sum_q[:, None] / D + 1e-06) * q_gain[None, :]).astype(jnp.bfloat16)
    k_norm = (k_float / jnp.sqrt(sum_k[:, None] / D + 1e-06) * k_gain[None, :]).astype(jnp.bfloat16)
    n_frames = lax.axis_size("frame")
    group_pos = frame_tok // n_frames

    def regroup(array):
        return lax.all_to_all(
            array.reshape(n_frames, group_pos, width),
            "frame",
            split_axis=0,
            concat_axis=0,
            tiled=True,
        ).reshape(frame_tok, width)

    anchor = anchor_frame[0]
    k_anchor, v_anchor = (spread(k_norm, "frame", anchor), spread(values, "frame", anchor))
    own_allowed = jnp.concatenate(
        [expand(spatial_mask[0]), jnp.ones((frame_tok, frame_tok), dtype=jnp.bool_)], axis=1
    )
    spatial = attend(
        q_norm,
        jnp.concatenate([k_norm, k_anchor], 0),
        jnp.concatenate([values, v_anchor], 0),
        own_allowed,
    )
    temporal = attend(
        regroup(q_norm), regroup(k_norm), regroup(values), expand(temporal_mask[0])
    ).astype(jnp.bfloat16)
    returned = regroup(temporal)
    return (spatial + returned.astype(jnp.float32)).astype(jnp.bfloat16)


ROWS = 16
MASK_ROW = 12


def dot_t(a, b):
    return lax.dot_general(a, b, (((1,), (1,)), ((), ())), preferred_element_type=jnp.float32)


def weigh(weights, vals):
    ones = jnp.ones(vals.shape, vals.dtype)
    both = jnp.dot(
        weights.astype(jnp.bfloat16),
        jnp.concatenate([vals, ones], axis=1),
        preferred_element_type=jnp.float32,
    )
    return both[:, :HD], both[:, HD:]


def blocked_scores(query, keys, flag, i):
    scores = dot_t(query, keys)
    near = scores[:, i * BLOCK : (i + 1) * BLOCK]
    away = scores[:, (1 - i) * BLOCK : (2 - i) * BLOCK] + flag
    return jnp.concatenate([near, away] if i == 0 else [away, near], axis=1)


def scaled(rows, column, gain):
    return (rows.astype(jnp.float32) * column * gain).astype(jnp.bfloat16)


def first_kernel(n, pos, q_ref, k_ref, v_ref, sum_ref, out_ref, held, cut, sems, v_sems):
    tok = q_ref.shape[0]
    chunks = sems.shape[1]
    parts = tok // pos
    step = tok // chunks
    copies = []
    for t, ref in enumerate((q_ref, k_ref)):
        for c in range(chunks):
            rows = pl.ds(c * step, step)
            copies.append(pltpu.make_async_copy(ref.at[rows], held.at[t, rows], sems.at[t, c]))
    loads, stores = [], []
    for d in range(n):
        heads = ((d, 0, tok, 0), (n + d // parts, d % parts * pos, pos, tok))
        for j, (head, row, rows, at) in enumerate(heads):
            loads.append(
                pltpu.make_async_copy(
                    v_ref.at[pl.ds(row, rows), pl.ds(head * HD, HD)],
                    cut.at[d, pl.ds(at, rows)],
                    v_sems.at[j, d],
                )
            )
        stores.append(pltpu.make_async_copy(cut.at[d], out_ref.at[d], v_sems.at[2, d]))
    for copy in copies + loads:
        copy.start()
    rows = []
    for t in range(2):
        parts = []
        for c in range(chunks):
            copies[t * chunks + c].wait()
            total = None
            for h in range(q_ref.shape[1] // HD):
                part = held[t, c * step : (c + 1) * step, h * HD : (h + 1) * HD]
                part = part.astype(jnp.float32)
                total = part * part if total is None else total + part * part
            parts.append(total)
        rows.append(jnp.sum(jnp.concatenate(parts, axis=0).T, axis=0, keepdims=True))
    sum_ref[...] = jnp.concatenate(rows + [jnp.zeros((6, tok), jnp.float32)], axis=0)
    for copy in loads:
        copy.wait()
    for copy in stores:
        copy.start()
    for copy in stores:
        copy.wait()


def copy_kernel(in_ref, out_ref):
    out_ref[...] = in_ref[...]


def own_kernel(n, pos, *refs):
    args, blocks, own_ref = refs[:11], refs[11 : 11 + n], refs[11 + n]
    ins, held, extra, own, sums, gains, masks, in_sems, out_sems = refs[12 + n :]
    q_ref, k_ref, v_ref = args[:3]
    tok = q_ref.shape[0]
    heads = q_ref.shape[1] // HD
    parts = tok // pos
    me = lax.axis_index("frame")
    order = [n + e for e in range(heads - n)] + [me ^ s for s in range(n)]

    def cols(h):
        return pl.ds(pl.multiple_of(h * HD, HD), HD)

    small = []
    for j in range(4):
        small.append(pltpu.make_async_copy(args[3 + j], sums.at[j], in_sems.at[3 * heads + j]))
    for j in range(2):
        at = in_sems.at[3 * heads + 4 + j]
        small.append(pltpu.make_async_copy(args[7 + j], gains.at[j], at))
        at = in_sems.at[3 * heads + 6 + j]
        small.append(pltpu.make_async_copy(args[9 + j], masks.at[j], at))
    loads = [
        pltpu.make_async_copy(ref.at[:, cols(h)], ins.at[t, x], in_sems.at[3 * x + t])
        for x, h in enumerate(order)
        for t, ref in enumerate((q_ref, k_ref, v_ref))
    ]
    for copy in small + loads:
        copy.start()
    for copy in small:
        copy.wait()
    inv = lax.rsqrt((sums[0] + sums[1] + sums[2] + sums[3]) / D + 1e-06).T
    inv_q = jnp.broadcast_to(inv[:, 0:1] * (LOG2E / float(HD) ** 0.5), (tok, HD))
    inv_k = jnp.broadcast_to(inv[:, 1:2], (tok, HD))
    flags = [jnp.where(masks[0, i, 1 - i] == 1, 0.0, NEG) for i in range(2)]
    lane = lax.broadcasted_iota(jnp.int32, (BLOCK, HD), 1)
    lses = [jnp.zeros((BLOCK, HD), jnp.float32) for _ in range(tok // BLOCK)]
    stores = []
    for x, h in enumerate(order):
        if x in (0, heads // 2):
            for copy in loads[3 * x : 3 * (x + heads // 2)]:
                copy.wait()
        query = scaled(ins[0, x], inv_q, gains[0, pl.ds(h, 1), :])
        keys = scaled(ins[1, x], inv_k, gains[1, pl.ds(h, 1), :])
        vals = ins[2, x]
        for t, array in enumerate((query, keys)):
            if x < heads - n:
                extra[x, t] = array
            else:
                s = x - (heads - n)
                held[s, t * tok : (t + 1) * tok, :] = array
                at = 2 * tok + t * pos
                rows = pl.ds(pl.multiple_of((me ^ s) % parts * pos, pos), pos)
                held[s, at : at + pos, :] = extra[(me ^ s) // parts, t, rows, :]
        if x >= heads - n:
            rows = pl.ds(0, 2 * (tok + pos))
            stores.append(
                pltpu.make_async_copy(held.at[s, rows], blocks[s].at[rows], out_sems.at[x])
            )
            stores[-1].start()
        for i in range(tok // BLOCK):
            rows = slice(i * BLOCK, (i + 1) * BLOCK)
            scores = blocked_scores(query[rows], keys, flags[i], i)
            top = jnp.max(scores, axis=1, keepdims=True)
            out, weight = weigh(jnp.exp2(scores - top), vals)
            own[x, rows, :] = out / weight
            lses[i] = jnp.where(lane == x, top + jnp.log2(weight), lses[i])
        stores.append(
            pltpu.make_async_copy(own.at[x], own_ref.at[:, cols(h)], out_sems.at[heads + x])
        )
        stores[-1].start()
    pieces = []
    for lse in lses:
        rest = lse.T[:ROWS]
        split = []
        for _ in range(3):
            split.append(rest.astype(jnp.bfloat16).astype(jnp.float32))
            rest = rest - split[-1]
        pieces.append(split)
    pad = jnp.zeros((ROWS - 1 - MASK_ROW, HD), jnp.float32)
    lane = lax.broadcasted_iota(jnp.int32, (1, HD), 1)
    mask = jnp.where(lane == 0, masks[1, 0, 1], masks[1, 1, 0])
    mask = (mask == 1).astype(jnp.float32)
    at = 2 * (tok + pos)
    for s in range(n):
        late = (me ^ s) // parts == 1
        rows = []
        for split in pieces:
            rows += [piece[s + heads - n : s + heads - n + 1, :] for piece in split]
        for split in pieces:
            rows += [jnp.where(late, piece[1:2, :], piece[0:1, :]) for piece in split]
        side = jnp.concatenate(rows + [mask, pad], axis=0)
        held[s, at : at + ROWS, :] = side.astype(jnp.bfloat16)
        rows = pl.ds(at, ROWS)
        stores.append(
            pltpu.make_async_copy(held.at[s, rows], blocks[s].at[rows], out_sems.at[2 * heads + s])
        )
        stores[-1].start()
    for copy in stores:
        copy.wait()


def pencil(n, query, keys, vals, lse, anchor_keys, anchor_vals, flags, put):
    keep = []
    for i in range(query.shape[0] // BLOCK):
        rows = slice(i * BLOCK, (i + 1) * BLOCK)
        scores = blocked_scores(query[rows], keys, flags[i], i)
        top = jnp.max(scores, axis=1, keepdims=True)
        out, total = weigh(jnp.exp2(scores - top), vals)
        temporal = out / total
        scores = dot_t(query[rows], anchor_keys)
        top = jnp.maximum(jnp.max(scores, axis=1, keepdims=True), lse[rows])
        own = jnp.exp2(lse[rows] - top)
        out, total = weigh(jnp.exp2(scores - top), anchor_vals)
        scale = 1.0 / (total + own)
        result = (temporal + out * scale).astype(jnp.bfloat16)
        keep.append(own * scale)
        gp = query.shape[0] // n
        for j in range(BLOCK // gp):
            put(i * (BLOCK // gp) + j, result[j * gp : (j + 1) * gp])
    return jnp.concatenate(keep, axis=0)


def add_side(side, keep, gp, first):
    n = side.shape[0]
    lane = lax.broadcasted_iota(jnp.int32, side.shape, 2)
    keep = keep.reshape(n, gp, HD)
    for g in range(gp // ROWS):
        side = jnp.where(lane == first + g, keep[:, g * ROWS : (g + 1) * ROWS, :], side)
    return side


def read_side(blocks, at, which, mask_ref):
    rows, masks = [], []
    for block in blocks:
        side = block[at : at + ROWS, :].astype(jnp.float32)
        for half in range(2):
            first = 6 * which + 3 * half
            rows.append(
                side[first : first + 1] + side[first + 1 : first + 2] + side[first + 2 : first + 3]
            )
        masks.append(side[MASK_ROW : MASK_ROW + 1])
    mask_ref[...] = jnp.concatenate(masks, axis=0)
    rows.append(jnp.zeros((HD - len(rows), HD), jnp.float32))
    return jnp.concatenate(rows, axis=0).T


def pencil_flags(mask_ref, row, upper):
    mask = mask_ref[pl.ds(row, 1), :]
    flags = [jnp.where(mask[:, i : i + 1] == 1.0, 0.0, NEG) for i in range(2)]
    return [jnp.where(upper, flags[1 - i], flags[i]) for i in range(2)]


def whole_kernel(n, tok, pos, at_ref, *refs):
    v_ref, blocks, outs, side_ref = refs[0], refs[1 : n + 1], refs[n + 1 : 2 * n + 1], refs[2 * n + 1]
    held_ref, mask_ref = refs[2 * n + 2 :]
    gp = tok // n
    me = lax.axis_index("frame")
    for s in range(n):

        @pl.when(at_ref[0] == me ^ s)
        def _():
            held_ref[...] = blocks[s][tok : 2 * tok, :]

    ka, va = held_ref[...], v_ref[at_ref[0], :tok, :]
    lses = read_side(blocks, 2 * (tok + pos), 0, mask_ref)
    upper = me >= n // 2
    side = jnp.zeros((n, ROWS, HD), jnp.float32)
    for g in range(n):

        def rows(at):
            return jnp.concatenate(
                [block[at + g * gp : at + (g + 1) * gp, :] for block in blocks], axis=0
            )

        def put(s, result):
            outs[s][g * gp : (g + 1) * gp, :] = result

        vals = [v_ref[me ^ s, g * gp : (g + 1) * gp, :] for s in range(n)]
        half, first = g * gp // BLOCK, g * gp % BLOCK
        lse = [lses[first : first + gp, 2 * s + half : 2 * s + half + 1] for s in range(n)]
        keep = pencil(
            n,
            rows(0),
            rows(tok),
            jnp.concatenate(vals, axis=0),
            jnp.concatenate(lse, axis=0),
            ka,
            va,
            pencil_flags(mask_ref, g ^ me, upper),
            put,
        )
        side = add_side(side, keep, gp, g * gp // ROWS)
    side_ref[...] = side


def part_kernel(n, tok, pos, *refs):
    v_ref, refs = refs[0], refs[1:]
    blocks, held = refs[:n], refs[n : n + 4]
    done, came_ref = refs[n + 4 : 2 * n + 4], refs[2 * n + 4]
    outs = refs[2 * n + 5 : 3 * n + 5]
    lse_ref, mask_ref = refs[3 * n + 5 :]
    gp = tok // n
    me = lax.axis_index("frame")
    quarter = me % (tok // pos)
    per_block = BLOCK // pos
    for s in range(n):
        outs[s][:tok, :] = done[s][...]
    ka = jnp.concatenate([a[:pos, :] for a in held], axis=0)
    va = jnp.concatenate([a[pos:, :] for a in held], axis=0)
    lse_ref[...] = read_side(blocks, 2 * (tok + pos), 1, mask_ref)
    upper = me >= n // 2
    late = quarter >= per_block
    side = came_ref[...]
    for u in range(pos // gp):

        def rows(at):
            return jnp.concatenate(
                [block[at + u * gp : at + (u + 1) * gp, :] for block in blocks], axis=0
            )

        def put(s, result):
            outs[s][tok + u * gp : tok + (u + 1) * gp, :] = result

        at = tok + u * gp
        vals = [v_ref[me ^ s, at : at + gp, :] for s in range(n)]
        first = pl.multiple_of(quarter % per_block * pos + u * gp, gp)
        lses = lse_ref[pl.ds(first, gp), :]
        lse = [
            jnp.where(late, lses[:, 2 * s + 1 : 2 * s + 2], lses[:, 2 * s : 2 * s + 1])
            for s in range(n)
        ]
        keep = pencil(
            n,
            rows(2 * tok),
            rows(2 * tok + pos),
            jnp.concatenate(vals, axis=0),
            jnp.concatenate(lse, axis=0),
            ka,
            va,
            pencil_flags(mask_ref, (quarter * (pos // gp) + u) ^ me, upper),
            put,
        )
        side = add_side(side, keep, gp, (tok + u * gp) // ROWS)
    for s in range(n):
        outs[s][tok + pos : tok + pos + ROWS, :] = side[s].astype(jnp.bfloat16)


def join_kernel(n, pos, own_ref, *refs):
    back, out_ref = refs[:n], refs[n]
    tok = own_ref.shape[0]
    parts = tok // pos
    me = lax.axis_index("frame")
    for s in range(n):
        d = me ^ s
        side = back[s][tok + pos : tok + pos + ROWS, :].astype(jnp.float32)
        row = pl.multiple_of(d % parts * pos, pos)
        for head, rows, at in ((d, pl.ds(0, tok), 0), (n + d // parts, pl.ds(row, pos), tok)):
            cols = pl.ds(pl.multiple_of(head * HD, HD), HD)
            keep = [side[:, g : g + 1] for g in range(at // ROWS, (at + rows.size) // ROWS)]
            keep = jnp.concatenate(keep, axis=0)
            got = back[s][at : at + rows.size, :].astype(jnp.float32)
            out_ref[rows, cols] = (own_ref[rows, cols] * keep + got).astype(jnp.bfloat16)


def call(kernel, out_shape, *args, vmem=40, **more):
    return pl.pallas_call(
        kernel,
        out_shape=out_shape,
        compiler_params=pltpu.CompilerParams(vmem_limit_bytes=vmem * 1024 * 1024),
        **more,
    )(*args)


def pairwise(array, axis, step):
    size = lax.axis_size(axis)
    return lax.ppermute(array, axis, [(i, i ^ step) for i in range(size)])


def swap_blocks(blocks):
    n = len(blocks)
    got = {0: blocks[0]}
    wide = sorted(range(n // 2, n), key=lambda s: (s % 2, s))
    for s in wide + [1, 2]:
        got[s] = pairwise(blocks[s], "frame", s)
    for s in range(3, n // 2):
        block, _ = lax.optimization_barrier((blocks[s], got[s - 1]))
        got[s] = pairwise(block, "frame", s)
    return [got[s] for s in range(n)]


def local_heads(
    q_raw, k_raw, values, q_gain, k_gain, spatial_mask, temporal_mask, anchor_frame
):
    tok, width = q_raw.shape
    n = lax.axis_size("frame")
    n_mp = lax.axis_size("mp")
    heads = width // HD
    parts = n // (heads - n)
    pos = tok // parts
    me = lax.axis_index("frame")
    shape = jax.ShapeDtypeStruct
    vm = pl.BlockSpec(memory_space=pltpu.VMEM)
    sm = pl.BlockSpec(memory_space=pltpu.SMEM)
    hbm = pl.BlockSpec(memory_space=pltpu.HBM)
    dma = pltpu.SemaphoreType.DMA
    bf16, f32 = jnp.bfloat16, jnp.float32

    sums, v_blocks = call(
        functools.partial(first_kernel, n, pos),
        (shape((8, tok), f32), shape((n, tok + pos, HD), bf16)),
        q_raw,
        k_raw,
        values,
        in_specs=[hbm] * 3,
        out_specs=(vm, hbm),
        scratch_shapes=[
            pltpu.VMEM((2, tok, width), bf16),
            pltpu.VMEM((n, tok + pos, HD), bf16),
            dma((2, 4)),
            dma((3, n)),
        ],
        vmem=60,
    )
    v_far = lax.all_to_all(v_blocks, "frame", split_axis=0, concat_axis=0, tiled=True)
    all_sums = [sums] + [pairwise(sums, "mp", step) for step in range(1, n_mp)]
    rows = 2 * (tok + pos) + ROWS
    *sent, own = call(
        functools.partial(own_kernel, n, pos),
        [shape((rows, HD), bf16)] * n + [shape((tok, width), f32)],
        q_raw,
        k_raw,
        values,
        *all_sums,
        q_gain.reshape(heads, HD),
        k_gain.reshape(heads, HD),
        spatial_mask[0],
        temporal_mask[0],
        in_specs=[hbm] * 11,
        out_specs=[hbm] * (n + 1),
        scratch_shapes=[
            pltpu.VMEM((3, heads, tok, HD), bf16),
            pltpu.VMEM((n, rows, HD), bf16),
            pltpu.VMEM((heads - n, 2, tok, HD), bf16),
            pltpu.VMEM((heads, tok, HD), f32),
            pltpu.VMEM((4, 8, tok), f32),
            pltpu.VMEM((2, heads, HD), f32),
            pltpu.SMEM((2, 2, 2), jnp.int32),
            dma((3 * heads + 8,)),
            dma((2 * heads + n,)),
        ],
        vmem=60,
    )
    far = swap_blocks(sent)

    anchor = anchor_frame[0]
    part = slice(2 * tok + pos, 2 * (tok + pos))
    mine = far[0][part]
    for s in range(1, n):
        mine = jnp.where(anchor == me ^ s, far[s][part], mine)
    v_mine = lax.dynamic_slice(v_far, (anchor, tok, 0), (1, pos, HD))[0]
    mine = jnp.concatenate([mine, v_mine], axis=0)
    held = [mine] + [pairwise(mine, "frame", step) for step in range(1, parts)]
    *done, weights = call(
        functools.partial(whole_kernel, n, tok, pos),
        [shape((tok, HD), bf16)] * n + [shape((n, ROWS, HD), f32)],
        anchor_frame,
        v_far,
        *far,
        in_specs=[sm] + [vm] * (n + 1),
        scratch_shapes=[pltpu.VMEM((tok, HD), bf16), pltpu.VMEM((n, HD), f32)],
    )
    result = call(
        functools.partial(part_kernel, n, tok, pos),
        [shape((tok + pos + ROWS, HD), bf16)] * n,
        v_far,
        *far,
        *held,
        *done,
        weights,
        scratch_shapes=[pltpu.VMEM((HD, HD), f32), pltpu.VMEM((n, HD), f32)],
    )
    back = swap_blocks(result)
    return call(
        functools.partial(join_kernel, n, pos), shape((tok, width), bf16), own, *back
    )


def solution(mesh):
    n = mesh.shape["frame"]

    def local(*args):
        tok, width = args[0].shape
        fits = n == 8 and mesh.shape["mp"] == 4 and width == 10 * HD and tok == 2 * BLOCK
        return local_heads(*args) if fits else local_general(*args)

    return jax.shard_map(
        local,
        mesh=mesh,
        in_specs=(
            P("frame", "mp"),
            P("frame", "mp"),
            P("frame", "mp"),
            P("mp"),
            P("mp"),
            P("frame", None, None),
            P("frame", None, None),
            P(),
        ),
        out_specs=P("frame", "mp"),
        check_vma=False,
    )
```

```python
import functools

import jax
import jax.numpy as jnp
from jax import lax
from jax.experimental import pallas as pl
from jax.experimental.pallas import tpu as pltpu
from jax.sharding import PartitionSpec as P

D = 5120
HD = 128
BLOCK = 128
LOG2E = 1.4426950408889634
NEG = -1e30


def spread(value, axis, source):
    kept = jnp.where(lax.axis_index(axis) == source, value, 0).astype(value.dtype)
    return lax.psum(kept, axis)


def expand(block_mask):
    count = block_mask.shape[0]
    allowed = (block_mask == 1) | jnp.eye(count, dtype=jnp.bool_)
    return jnp.repeat(jnp.repeat(allowed, BLOCK, axis=0), BLOCK, axis=1)


def attend(query, keys, vals, allowed):
    rows = query.shape[0]
    width = query.shape[1]
    heads_dev = width // HD
    query3 = jnp.transpose(query.reshape(rows, heads_dev, HD), (1, 0, 2))
    keys3 = jnp.transpose(keys.reshape(keys.shape[0], heads_dev, HD), (1, 0, 2))
    vals3 = jnp.transpose(vals.reshape(vals.shape[0], heads_dev, HD), (1, 0, 2))
    scale = jnp.sqrt(jnp.float32(HD))

    def one_head(items):
        head_q, head_k, head_v = items
        scores = jnp.einsum("qd,kd->qk", head_q, head_k, preferred_element_type=jnp.float32) / scale
        scores = jnp.where(allowed, scores, -jnp.inf)
        probs = jax.nn.softmax(scores, axis=-1).astype(jnp.bfloat16)
        return jnp.dot(probs, head_v, preferred_element_type=jnp.float32)

    output = lax.map(one_head, (query3, keys3, vals3))
    return jnp.transpose(output, (1, 0, 2)).reshape(rows, width)


def local_general(
    q_raw, k_raw, values, q_gain, k_gain, spatial_mask, temporal_mask, anchor_frame
):
    frame_tok = q_raw.shape[0]
    width = q_raw.shape[1]
    q_float = q_raw.astype(jnp.float32)
    k_float = k_raw.astype(jnp.float32)
    sum_q, sum_k = lax.psum(
        (jnp.sum(q_float * q_float, axis=1), jnp.sum(k_float * k_float, axis=1)), "mp"
    )
    q_norm = (q_float / jnp.sqrt(sum_q[:, None] / D + 1e-06) * q_gain[None, :]).astype(jnp.bfloat16)
    k_norm = (k_float / jnp.sqrt(sum_k[:, None] / D + 1e-06) * k_gain[None, :]).astype(jnp.bfloat16)
    n_frames = lax.axis_size("frame")
    group_pos = frame_tok // n_frames

    def regroup(array):
        return lax.all_to_all(
            array.reshape(n_frames, group_pos, width),
            "frame",
            split_axis=0,
            concat_axis=0,
            tiled=True,
        ).reshape(frame_tok, width)

    anchor = anchor_frame[0]
    k_anchor, v_anchor = (spread(k_norm, "frame", anchor), spread(values, "frame", anchor))
    own_allowed = jnp.concatenate(
        [expand(spatial_mask[0]), jnp.ones((frame_tok, frame_tok), dtype=jnp.bool_)], axis=1
    )
    spatial = attend(
        q_norm,
        jnp.concatenate([k_norm, k_anchor], 0),
        jnp.concatenate([values, v_anchor], 0),
        own_allowed,
    )
    temporal = attend(
        regroup(q_norm), regroup(k_norm), regroup(values), expand(temporal_mask[0])
    ).astype(jnp.bfloat16)
    returned = regroup(temporal)
    return (spatial + returned.astype(jnp.float32)).astype(jnp.bfloat16)


ROWS = 16
LSE_ROW = 6
NORM_ROW = 9
MASK_ROW = 15


def dot_t(a, b):
    return lax.dot_general(a, b, (((1,), (1,)), ((), ())), preferred_element_type=jnp.float32)


def weigh(weights, vals):
    ones = jnp.ones(vals.shape, vals.dtype)
    both = jnp.dot(
        weights.astype(jnp.bfloat16),
        jnp.concatenate([vals, ones], axis=1),
        preferred_element_type=jnp.float32,
    )
    return both[:, :HD], both[:, HD:]


def blocked_scores(query, keys, flag, i):
    scores = dot_t(query, keys)
    near = scores[:, i * BLOCK : (i + 1) * BLOCK]
    away = scores[:, (1 - i) * BLOCK : (2 - i) * BLOCK] + flag
    return jnp.concatenate([near, away] if i == 0 else [away, near], axis=1)


def scaled(rows, column, gain):
    return (rows.astype(jnp.float32) * column * gain).astype(jnp.bfloat16)


def first_kernel(n, pos, q_ref, k_ref, v_ref, sum_ref, out_ref, held, cut, sems, v_sems):
    tok = q_ref.shape[0]
    chunks = sems.shape[1]
    parts = tok // pos
    step = tok // chunks
    copies = []
    for t, ref in enumerate((q_ref, k_ref)):
        for c in range(chunks):
            rows = pl.ds(c * step, step)
            copies.append(pltpu.make_async_copy(ref.at[rows], held.at[t, rows], sems.at[t, c]))
    loads, stores = [], []
    for d in range(n):
        row = d % parts * pos
        pieces = (
            (v_ref, d, 0, tok, 0),
            (v_ref, n + d // parts, row, pos, tok),
            (k_ref, n + d // parts, row, pos, tok + pos),
        )
        for j, (ref, head, row, rows, at) in enumerate(pieces):
            loads.append(
                pltpu.make_async_copy(
                    ref.at[pl.ds(row, rows), pl.ds(head * HD, HD)],
                    cut.at[d, pl.ds(at, rows)],
                    v_sems.at[j, d],
                )
            )
        stores.append(pltpu.make_async_copy(cut.at[d], out_ref.at[d], v_sems.at[3, d]))
    for copy in copies + loads:
        copy.start()
    rows = []
    for t in range(2):
        parts = []
        for c in range(chunks):
            copies[t * chunks + c].wait()
            total = None
            for h in range(q_ref.shape[1] // HD):
                part = held[t, c * step : (c + 1) * step, h * HD : (h + 1) * HD]
                part = part.astype(jnp.float32)
                total = part * part if total is None else total + part * part
            parts.append(total)
        rows.append(jnp.sum(jnp.concatenate(parts, axis=0).T, axis=0, keepdims=True))
    sum_ref[...] = jnp.concatenate(rows + [jnp.zeros((6, tok), jnp.float32)], axis=0)
    for copy in loads:
        copy.wait()
    for copy in stores:
        copy.start()
    for copy in stores:
        copy.wait()


def copy_kernel(in_ref, out_ref):
    out_ref[...] = in_ref[...]


def own_kernel(n, pos, *refs):
    args, blocks, own_ref = refs[:11], refs[11 : 11 + n], refs[11 + n]
    ins, held, extra, own, sums, gains, masks, in_sems, out_sems = refs[12 + n :]
    q_ref, k_ref, v_ref = args[:3]
    tok = q_ref.shape[0]
    heads = q_ref.shape[1] // HD
    parts = tok // pos
    me = lax.axis_index("frame")
    order = [n + e for e in range(heads - n)] + [me ^ s for s in range(n)]

    def cols(h):
        return pl.ds(pl.multiple_of(h * HD, HD), HD)

    small = []
    for j in range(4):
        small.append(pltpu.make_async_copy(args[3 + j], sums.at[j], in_sems.at[3 * heads + j]))
    for j in range(2):
        at = in_sems.at[3 * heads + 4 + j]
        small.append(pltpu.make_async_copy(args[7 + j], gains.at[j], at))
        at = in_sems.at[3 * heads + 6 + j]
        small.append(pltpu.make_async_copy(args[9 + j], masks.at[j], at))
    loads = [
        pltpu.make_async_copy(ref.at[:, cols(h)], ins.at[t, x], in_sems.at[3 * x + t])
        for x, h in enumerate(order)
        for t, ref in enumerate((q_ref, k_ref, v_ref))
    ]
    for copy in small + loads:
        copy.start()
    for copy in small:
        copy.wait()
    inv = lax.rsqrt((sums[0] + sums[1] + sums[2] + sums[3]) / D + 1e-06)
    inv_row = inv[1:2, :]
    inv = inv.T
    inv_q = jnp.broadcast_to(inv[:, 0:1] * (LOG2E / float(HD) ** 0.5), (tok, HD))
    inv_k = jnp.broadcast_to(inv[:, 1:2], (tok, HD))
    flags = [jnp.where(masks[0, i, 1 - i] == 1, 0.0, NEG) for i in range(2)]
    lane = lax.broadcasted_iota(jnp.int32, (BLOCK, HD), 1)
    lses = [jnp.zeros((BLOCK, HD), jnp.float32) for _ in range(tok // BLOCK)]
    stores = []
    for x, h in enumerate(order):
        if x in (0, heads // 2):
            for copy in loads[3 * x : 3 * (x + heads // 2)]:
                copy.wait()
        query = scaled(ins[0, x], inv_q, gains[0, pl.ds(h, 1), :])
        keys = scaled(ins[1, x], inv_k, gains[1, pl.ds(h, 1), :])
        vals = ins[2, x]
        if x < heads - n:
            extra[x] = query
        else:
            s = x - (heads - n)
            held[s, :tok, :] = query
            held[s, tok : 2 * tok, :] = keys
            rows = pl.ds(pl.multiple_of((me ^ s) % parts * pos, pos), pos)
            held[s, 2 * tok : 2 * tok + pos, :] = extra[(me ^ s) // parts, rows, :]
            rows = pl.ds(0, 2 * tok + pos)
            stores.append(
                pltpu.make_async_copy(held.at[s, rows], blocks[s].at[rows], out_sems.at[x])
            )
            stores[-1].start()
        for i in range(tok // BLOCK):
            rows = slice(i * BLOCK, (i + 1) * BLOCK)
            scores = blocked_scores(query[rows], keys, flags[i], i)
            top = jnp.max(scores, axis=1, keepdims=True)
            out, weight = weigh(jnp.exp2(scores - top), vals)
            own[x, rows, :] = out / weight
            lses[i] = jnp.where(lane == x, top + jnp.log2(weight), lses[i])
        stores.append(
            pltpu.make_async_copy(own.at[x], own_ref.at[:, cols(h)], out_sems.at[heads + x])
        )
        stores[-1].start()
    def split(rest):
        parts = []
        for _ in range(3):
            parts.append(rest.astype(jnp.bfloat16).astype(jnp.float32))
            rest = rest - parts[-1]
        return parts

    lses = [split(lse.T[:ROWS]) for lse in lses]
    norms = [split(inv_row[:, i * BLOCK : (i + 1) * BLOCK]) for i in range(tok // BLOCK)]
    lane = lax.broadcasted_iota(jnp.int32, (1, HD), 1)
    mask = jnp.where(lane == 0, masks[1, 0, 1], masks[1, 1, 0])
    tail = norms[0] + norms[1] + [(mask == 1).astype(jnp.float32)]
    at = 2 * tok + pos
    for s in range(n):
        first = heads - n + s
        rows = [piece[first : first + 1, :] for half in lses for piece in half]
        late = (me ^ s) // parts == 1
        upper = (me ^ s) % parts * pos >= BLOCK
        for low, high in zip(*lses):
            piece = jnp.where(upper, high, low)
            rows.append(jnp.where(late, piece[1:2, :], piece[0:1, :]))
        held[s, at : at + ROWS, :] = jnp.concatenate(rows + tail, axis=0).astype(jnp.bfloat16)
        rows = pl.ds(at, ROWS)
        stores.append(
            pltpu.make_async_copy(held.at[s, rows], blocks[s].at[rows], out_sems.at[2 * heads + s])
        )
        stores[-1].start()
    for copy in stores:
        copy.wait()


def pencil(n, query, keys, vals, lse, anchor_keys, anchor_vals, flags, put):
    keep = []
    for i in range(query.shape[0] // BLOCK):
        rows = slice(i * BLOCK, (i + 1) * BLOCK)
        scores = blocked_scores(query[rows], keys, flags[i], i)
        top = jnp.max(scores, axis=1, keepdims=True)
        out, total = weigh(jnp.exp2(scores - top), vals)
        temporal = out / total
        scores = dot_t(query[rows], anchor_keys)
        top = jnp.maximum(jnp.max(scores, axis=1, keepdims=True), lse[rows])
        own = jnp.exp2(lse[rows] - top)
        out, total = weigh(jnp.exp2(scores - top), anchor_vals)
        scale = 1.0 / (total + own)
        result = (temporal + out * scale).astype(jnp.bfloat16)
        keep.append(own * scale)
        gp = query.shape[0] // n
        for j in range(BLOCK // gp):
            put(i * (BLOCK // gp) + j, result[j * gp : (j + 1) * gp])
    return jnp.concatenate(keep, axis=0)


def add_side(side, keep, gp, first):
    n = side.shape[0]
    lane = lax.broadcasted_iota(jnp.int32, side.shape, 2)
    keep = keep.reshape(n, gp, HD)
    for g in range(gp // ROWS):
        side = jnp.where(lane == first + g, keep[:, g * ROWS : (g + 1) * ROWS, :], side)
    return side


def read_side(blocks, at, col_ref, mask_ref):
    whole, part, norm, masks = [], [], [], []
    for block in blocks:
        side = block[at : at + ROWS, :].astype(jnp.float32)

        def joined(first):
            return side[first : first + 1] + side[first + 1 : first + 2] + side[first + 2 : first + 3]

        whole += [joined(0), joined(3)]
        part.append(joined(LSE_ROW))
        norm += [joined(NORM_ROW), joined(NORM_ROW + 3)]
        masks.append(side[MASK_ROW : MASK_ROW + 1])
    mask_ref[...] = jnp.concatenate(masks, axis=0)
    rows = whole + part + norm
    rows.append(jnp.zeros((HD - len(rows), HD), jnp.float32))
    col_ref[...] = jnp.concatenate(rows, axis=0).T


def pencil_flags(mask_ref, row, upper):
    mask = mask_ref[pl.ds(row, 1), :]
    flags = [jnp.where(mask[:, i : i + 1] == 1.0, 0.0, NEG) for i in range(2)]
    return [jnp.where(upper, flags[1 - i], flags[i]) for i in range(2)]


def run_pencil(n, gp, mask_ref, query, keys, vals, lse, ka, va, row, outs, at, side):
    me = lax.axis_index("frame")

    def put(s, result):
        outs[s][at : at + gp, :] = result

    flags = pencil_flags(mask_ref, row ^ me, me >= n // 2)
    lse = jnp.concatenate(lse, axis=0)
    keep = pencil(n, query, keys, vals, lse, ka, va, flags, put)
    return add_side(side, keep, gp, at // ROWS)


def stack_rows(blocks, at, gp):
    return jnp.concatenate([block[at : at + gp, :] for block in blocks], axis=0)


def whole_kernel(n, tok, pos, at_ref, v_ref, *refs):
    blocks, outs, side_ref = refs[:n], refs[n : 2 * n], refs[2 * n]
    col_ref, mask_ref, key_ref = refs[2 * n + 1 :]
    gp = tok // n
    me = lax.axis_index("frame")
    anchor = at_ref[0]
    for s in range(n):

        @pl.when(anchor == me ^ s)
        def _():
            key_ref[...] = blocks[s][tok : 2 * tok, :]

    read_side(blocks, 2 * tok + pos, col_ref, mask_ref)
    ka, va = key_ref[...], v_ref[anchor, :tok, :]
    values = [v_ref.at[me ^ s] for s in range(n)]
    side = jnp.zeros((n, ROWS, HD), jnp.float32)
    for g in range(n):
        half, first, at = g * gp // BLOCK, g * gp % BLOCK, g * gp
        lse = [col_ref[first : first + gp, 2 * s + half : 2 * s + half + 1] for s in range(n)]
        query, keys = stack_rows(blocks, at, gp), stack_rows(blocks, tok + at, gp)
        vals = stack_rows(values, at, gp)
        side = run_pencil(
            n, gp, mask_ref, query, keys, vals, lse, ka, va, g, outs, at, side
        )
    side_ref[...] = side


def part_kernel(n, tok, pos, at_ref, gain_ref, held_ref, v_ref, *refs):
    blocks, done, (came_ref, col_ref, mask_ref) = refs[:n], refs[n : 2 * n], refs[2 * n : 2 * n + 3]
    outs = refs[2 * n + 3 :]
    gp = tok // n
    parts = tok // pos
    me = lax.axis_index("frame")
    anchor = at_ref[0]
    quarter = me % parts
    gain = jnp.where(me // parts == 1, gain_ref[n + 1 : n + 2, :], gain_ref[n : n + 1, :])
    late = quarter * pos >= BLOCK
    for s in range(n):
        outs[s][:tok, :] = done[s][...]
    norm = []
    for half in range(tok // BLOCK):
        norm.append(jnp.zeros((BLOCK, 1), jnp.float32))
        for s in range(n):
            lane = 3 * n + 2 * s + half
            norm[-1] = jnp.where(anchor == me ^ s, col_ref[:, lane : lane + 1], norm[-1])
    va = jnp.concatenate([held_ref[j, :pos, :] for j in range(parts)], axis=0)
    ka = jnp.concatenate([held_ref[j, pos:, :] for j in range(parts)], axis=0)
    ka = scaled(ka, jnp.concatenate(norm, axis=0), gain)
    values = [v_ref.at[me ^ s] for s in range(n)]
    side = came_ref[...]
    for u in range(pos // gp):
        first = pl.multiple_of(quarter * pos % BLOCK + u * gp, gp)
        cols = col_ref[pl.ds(first, gp), :]
        lse, norm = [], []
        for s in range(n):
            lse.append(cols[:, 2 * n + s : 2 * n + s + 1])
            lane = 3 * n + 2 * s
            norm.append(jnp.where(late, cols[:, lane + 1 : lane + 2], cols[:, lane : lane + 1]))
        at = tok + u * gp
        query, vals = stack_rows(blocks, tok + at, gp), stack_rows(values, at, gp)
        keys = scaled(stack_rows(values, at + pos, gp), jnp.concatenate(norm, axis=0), gain)
        row = quarter * (pos // gp) + u
        side = run_pencil(
            n, gp, mask_ref, query, keys, vals, lse, ka, va, row, outs, at, side
        )
    for s in range(n):
        outs[s][tok + pos : tok + pos + ROWS, :] = side[s].astype(jnp.bfloat16)


def join_kernel(n, pos, own_ref, *refs):
    back, out_ref = refs[:n], refs[n]
    tok = own_ref.shape[0]
    parts = tok // pos
    me = lax.axis_index("frame")
    for s in range(n):
        d = me ^ s
        side = back[s][tok + pos : tok + pos + ROWS, :].astype(jnp.float32)
        row = pl.multiple_of(d % parts * pos, pos)
        for head, rows, at in ((d, pl.ds(0, tok), 0), (n + d // parts, pl.ds(row, pos), tok)):
            cols = pl.ds(pl.multiple_of(head * HD, HD), HD)
            keep = [side[:, g : g + 1] for g in range(at // ROWS, (at + rows.size) // ROWS)]
            keep = jnp.concatenate(keep, axis=0)
            got = back[s][at : at + rows.size, :].astype(jnp.float32)
            out_ref[rows, cols] = (own_ref[rows, cols] * keep + got).astype(jnp.bfloat16)


def call(kernel, out_shape, *args, vmem=40, **more):
    return pl.pallas_call(
        kernel,
        out_shape=out_shape,
        compiler_params=pltpu.CompilerParams(vmem_limit_bytes=vmem * 1024 * 1024),
        **more,
    )(*args)


def pairwise(array, axis, step):
    size = lax.axis_size(axis)
    return lax.ppermute(array, axis, [(i, i ^ step) for i in range(size)])


def swap_blocks(blocks):
    n = len(blocks)
    got = {0: blocks[0]}
    wide = sorted(range(n // 2, n), key=lambda s: (s % 2, s))
    for s in wide + [1, 2]:
        got[s] = pairwise(blocks[s], "frame", s)
    for s in range(3, n // 2):
        block, _ = lax.optimization_barrier((blocks[s], got[s - 1]))
        got[s] = pairwise(block, "frame", s)
    return [got[s] for s in range(n)]


def local_heads(
    q_raw, k_raw, values, q_gain, k_gain, spatial_mask, temporal_mask, anchor_frame
):
    tok, width = q_raw.shape
    n = lax.axis_size("frame")
    n_mp = lax.axis_size("mp")
    heads = width // HD
    parts = n // (heads - n)
    pos = tok // parts
    me = lax.axis_index("frame")
    shape = jax.ShapeDtypeStruct
    vm = pl.BlockSpec(memory_space=pltpu.VMEM)
    sm = pl.BlockSpec(memory_space=pltpu.SMEM)
    hbm = pl.BlockSpec(memory_space=pltpu.HBM)
    dma = pltpu.SemaphoreType.DMA
    bf16, f32 = jnp.bfloat16, jnp.float32

    sums, v_blocks = call(
        functools.partial(first_kernel, n, pos),
        (shape((8, tok), f32), shape((n, tok + 2 * pos, HD), bf16)),
        q_raw,
        k_raw,
        values,
        in_specs=[hbm] * 3,
        out_specs=(vm, hbm),
        scratch_shapes=[
            pltpu.VMEM((2, tok, width), bf16),
            pltpu.VMEM((n, tok + 2 * pos, HD), bf16),
            dma((2, 4)),
            dma((4, n)),
        ],
        vmem=60,
    )
    all_sums = [sums] + [pairwise(sums, "mp", step) for step in range(1, n_mp)]
    v_far = lax.all_to_all(v_blocks, "frame", split_axis=0, concat_axis=0, tiled=True)
    rows = 2 * tok + pos + ROWS
    *sent, own = call(
        functools.partial(own_kernel, n, pos),
        [shape((rows, HD), bf16)] * n + [shape((tok, width), f32)],
        q_raw,
        k_raw,
        values,
        *all_sums,
        q_gain.reshape(heads, HD),
        k_gain.reshape(heads, HD),
        spatial_mask[0],
        temporal_mask[0],
        in_specs=[hbm] * 11,
        out_specs=[hbm] * (n + 1),
        scratch_shapes=[
            pltpu.VMEM((3, heads, tok, HD), bf16),
            pltpu.VMEM((n, rows, HD), bf16),
            pltpu.VMEM((heads - n, tok, HD), bf16),
            pltpu.VMEM((heads, tok, HD), f32),
            pltpu.VMEM((4, 8, tok), f32),
            pltpu.VMEM((2, heads, HD), f32),
            pltpu.SMEM((2, 2, 2), jnp.int32),
            dma((3 * heads + 8,)),
            dma((2 * heads + n,)),
        ],
        vmem=60,
    )
    far = swap_blocks(sent)
    block, v_far = lax.optimization_barrier((sent[0], v_far))
    far[0] = call(copy_kernel, shape((rows, HD), bf16), block, vmem=8)

    anchor = anchor_frame[0]
    mine = lax.dynamic_slice(v_far, (anchor, tok, 0), (1, 2 * pos, HD))
    groups = [list(range(first, first + parts)) for first in range(0, n, parts)]
    held = lax.all_to_all(
        jnp.broadcast_to(mine, (parts, 2 * pos, HD)),
        "frame",
        split_axis=0,
        concat_axis=0,
        axis_index_groups=groups,
        tiled=True,
    )
    exps = n * tok * 2 * tok
    *done, side, columns, masks = call(
        functools.partial(whole_kernel, n, tok, pos),
        [shape((tok, HD), bf16)] * n
        + [shape((n, ROWS, HD), f32), shape((HD, HD), f32), shape((n, HD), f32)],
        anchor_frame,
        v_far,
        *far,
        in_specs=[sm] + [vm] * (n + 1),
        scratch_shapes=[pltpu.VMEM((tok, HD), bf16)],
        cost_estimate=pl.CostEstimate(
            flops=6 * exps * HD, bytes_accessed=8 * n * tok * HD, transcendentals=exps
        ),
    )
    result = call(
        functools.partial(part_kernel, n, tok, pos),
        [shape((tok + pos + ROWS, HD), bf16)] * n,
        anchor_frame,
        k_gain.reshape(heads, HD),
        held,
        v_far,
        *far,
        *done,
        side,
        columns,
        masks,
        in_specs=[sm] + [vm] * (2 * n + 6),
    )
    back = swap_blocks(result)
    return call(
        functools.partial(join_kernel, n, pos), shape((tok, width), bf16), own, *back
    )


def solution(mesh):
    n = mesh.shape["frame"]

    def local(*args):
        tok, width = args[0].shape
        fits = n == 8 and mesh.shape["mp"] == 4 and width == 10 * HD and tok == 2 * BLOCK
        return local_heads(*args) if fits else local_general(*args)

    return jax.shard_map(
        local,
        mesh=mesh,
        in_specs=(
            P("frame", "mp"),
            P("frame", "mp"),
            P("frame", "mp"),
            P("mp"),
            P("mp"),
            P("frame", None, None),
            P("frame", None, None),
            P(),
        ),
        out_specs=P("frame", "mp"),
        check_vma=False,
    )
```

```python
import functools

import jax
import jax.numpy as jnp
from jax import lax
from jax.experimental import pallas as pl
from jax.experimental.pallas import tpu as pltpu
from jax.sharding import PartitionSpec as P

D = 5120
HD = 128
BLOCK = 128
LOG2E = 1.4426950408889634
NEG = -1e30


def spread(value, axis, source):
    kept = jnp.where(lax.axis_index(axis) == source, value, 0).astype(value.dtype)
    return lax.psum(kept, axis)


def expand(block_mask):
    count = block_mask.shape[0]
    allowed = (block_mask == 1) | jnp.eye(count, dtype=jnp.bool_)
    return jnp.repeat(jnp.repeat(allowed, BLOCK, axis=0), BLOCK, axis=1)


def attend(query, keys, vals, allowed):
    rows = query.shape[0]
    width = query.shape[1]
    heads_dev = width // HD
    query3 = jnp.transpose(query.reshape(rows, heads_dev, HD), (1, 0, 2))
    keys3 = jnp.transpose(keys.reshape(keys.shape[0], heads_dev, HD), (1, 0, 2))
    vals3 = jnp.transpose(vals.reshape(vals.shape[0], heads_dev, HD), (1, 0, 2))
    scale = jnp.sqrt(jnp.float32(HD))

    def one_head(items):
        head_q, head_k, head_v = items
        scores = jnp.einsum("qd,kd->qk", head_q, head_k, preferred_element_type=jnp.float32) / scale
        scores = jnp.where(allowed, scores, -jnp.inf)
        probs = jax.nn.softmax(scores, axis=-1).astype(jnp.bfloat16)
        return jnp.dot(probs, head_v, preferred_element_type=jnp.float32)

    output = lax.map(one_head, (query3, keys3, vals3))
    return jnp.transpose(output, (1, 0, 2)).reshape(rows, width)


def local_general(
    q_raw, k_raw, values, q_gain, k_gain, spatial_mask, temporal_mask, anchor_frame
):
    frame_tok = q_raw.shape[0]
    width = q_raw.shape[1]
    q_float = q_raw.astype(jnp.float32)
    k_float = k_raw.astype(jnp.float32)
    sum_q, sum_k = lax.psum(
        (jnp.sum(q_float * q_float, axis=1), jnp.sum(k_float * k_float, axis=1)), "mp"
    )
    q_norm = (q_float / jnp.sqrt(sum_q[:, None] / D + 1e-06) * q_gain[None, :]).astype(jnp.bfloat16)
    k_norm = (k_float / jnp.sqrt(sum_k[:, None] / D + 1e-06) * k_gain[None, :]).astype(jnp.bfloat16)
    n_frames = lax.axis_size("frame")
    group_pos = frame_tok // n_frames

    def regroup(array):
        return lax.all_to_all(
            array.reshape(n_frames, group_pos, width),
            "frame",
            split_axis=0,
            concat_axis=0,
            tiled=True,
        ).reshape(frame_tok, width)

    anchor = anchor_frame[0]
    k_anchor, v_anchor = (spread(k_norm, "frame", anchor), spread(values, "frame", anchor))
    own_allowed = jnp.concatenate(
        [expand(spatial_mask[0]), jnp.ones((frame_tok, frame_tok), dtype=jnp.bool_)], axis=1
    )
    spatial = attend(
        q_norm,
        jnp.concatenate([k_norm, k_anchor], 0),
        jnp.concatenate([values, v_anchor], 0),
        own_allowed,
    )
    temporal = attend(
        regroup(q_norm), regroup(k_norm), regroup(values), expand(temporal_mask[0])
    ).astype(jnp.bfloat16)
    returned = regroup(temporal)
    return (spatial + returned.astype(jnp.float32)).astype(jnp.bfloat16)


ROWS = 16
LSE_ROW = 6
NORM_ROW = 9
MASK_ROW = 15
ONES = 8


def dot_t(a, b):
    return lax.dot_general(a, b, (((1,), (1,)), ((), ())), preferred_element_type=jnp.float32)


def weigh(weights, vals):
    ones = jnp.ones(vals.shape, vals.dtype)
    both = jnp.dot(
        weights.astype(jnp.bfloat16),
        jnp.concatenate([vals, ones], axis=1),
        preferred_element_type=jnp.float32,
    )
    return both[:, :HD], both[:, HD:]


def blocked_scores(query, keys, flag, i):
    scores = dot_t(query, keys)
    near = scores[:, i * BLOCK : (i + 1) * BLOCK]
    away = scores[:, (1 - i) * BLOCK : (2 - i) * BLOCK] + flag
    return jnp.concatenate([near, away] if i == 0 else [away, near], axis=1)


def scaled(rows, column, gain):
    return (rows.astype(jnp.float32) * column * gain).astype(jnp.bfloat16)


def cut_kernel(n, pos, k_ref, v_ref, out_ref, cut, sems):
    tok = k_ref.shape[0]
    parts = tok // pos
    loads, stores = [], []
    for d in range(n):
        row = d % parts * pos
        pieces = (
            (v_ref, d, 0, tok, 0),
            (v_ref, n + d // parts, row, pos, tok),
            (k_ref, n + d // parts, row, pos, tok + pos),
        )
        for j, (ref, head, row, rows, at) in enumerate(pieces):
            loads.append(
                pltpu.make_async_copy(
                    ref.at[pl.ds(row, rows), pl.ds(head * HD, HD)],
                    cut.at[d, pl.ds(at, rows)],
                    sems.at[j, d],
                )
            )
            loads[-1].start()
        stores.append(pltpu.make_async_copy(cut.at[d], out_ref.at[d], sems.at[3, d]))
    for d in range(n):
        for copy in loads[3 * d : 3 * d + 3]:
            copy.wait()
        stores[d].start()
    for copy in stores:
        copy.wait()


def squares_kernel(q_ref, k_ref, out_ref, held, sems):
    tok = q_ref.shape[0]
    chunks = sems.shape[1]
    step = tok // chunks
    copies = []
    for t, ref in enumerate((q_ref, k_ref)):
        for c in range(chunks):
            rows = pl.ds(c * step, step)
            copies.append(pltpu.make_async_copy(ref.at[rows], held.at[t, rows], sems.at[t, c]))
    for copy in copies:
        copy.start()
    rows = []
    for t in range(2):
        parts = []
        for c in range(chunks):
            copies[t * chunks + c].wait()
            total = None
            for h in range(q_ref.shape[1] // HD):
                part = held[t, c * step : (c + 1) * step, h * HD : (h + 1) * HD]
                part = part.astype(jnp.float32)
                total = part * part if total is None else total + part * part
            parts.append(total)
        rows.append(jnp.sum(jnp.concatenate(parts, axis=0).T, axis=0, keepdims=True))
    out_ref[...] = jnp.concatenate(rows + [jnp.zeros((6, tok), jnp.float32)], axis=0)


def copy_kernel(in_ref, out_ref):
    out_ref[...] = in_ref[...]


def own_kernel(n, pos, *refs):
    args, blocks, own_ref = refs[:11], refs[11 : 11 + n], refs[11 + n]
    ins, held, extra, own, sums, gains, masks, in_sems, out_sems = refs[12 + n :]
    q_ref, k_ref, v_ref = args[:3]
    tok = q_ref.shape[0]
    heads = q_ref.shape[1] // HD
    parts = tok // pos
    me = lax.axis_index("frame")
    order = [n + e for e in range(heads - n)] + [me ^ s for s in range(n)]

    def cols(h):
        return pl.ds(pl.multiple_of(h * HD, HD), HD)

    small = []
    for j in range(4):
        small.append(pltpu.make_async_copy(args[3 + j], sums.at[j], in_sems.at[3 * heads + j]))
    for j in range(2):
        at = in_sems.at[3 * heads + 4 + j]
        small.append(pltpu.make_async_copy(args[7 + j], gains.at[j], at))
        at = in_sems.at[3 * heads + 6 + j]
        small.append(pltpu.make_async_copy(args[9 + j], masks.at[j], at))
    loads = [
        pltpu.make_async_copy(ref.at[:, cols(h)], ins.at[t, x], in_sems.at[3 * x + t])
        for x, h in enumerate(order)
        for t, ref in enumerate((q_ref, k_ref, v_ref))
    ]
    for copy in small + loads:
        copy.start()
    for copy in small:
        copy.wait()
    inv = lax.rsqrt((sums[0] + sums[1] + sums[2] + sums[3]) / D + 1e-06)
    inv_row = inv[1:2, :]
    inv = inv.T
    inv_q = jnp.broadcast_to(inv[:, 0:1] * (LOG2E / float(HD) ** 0.5), (tok, HD))
    inv_k = jnp.broadcast_to(inv[:, 1:2], (tok, HD))
    flags = [jnp.where(masks[0, i, 1 - i] == 1, 0.0, NEG) for i in range(2)]
    lane = lax.broadcasted_iota(jnp.int32, (BLOCK, HD), 1)
    lses = [jnp.zeros((BLOCK, HD), jnp.float32) for _ in range(tok // BLOCK)]
    stores = []
    for x, h in enumerate(order):
        if x in (0, heads // 2):
            for copy in loads[3 * x : 3 * (x + heads // 2)]:
                copy.wait()
        query = scaled(ins[0, x], inv_q, gains[0, pl.ds(h, 1), :])
        keys = scaled(ins[1, x], inv_k, gains[1, pl.ds(h, 1), :])
        vals = ins[2, x]
        if x < heads - n:
            extra[x] = query
        else:
            s = x - (heads - n)
            held[s, :tok, :] = query
            held[s, tok : 2 * tok, :] = keys
            rows = pl.ds(pl.multiple_of((me ^ s) % parts * pos, pos), pos)
            held[s, 2 * tok : 2 * tok + pos, :] = extra[(me ^ s) // parts, rows, :]
            rows = pl.ds(0, 2 * tok + pos)
            stores.append(
                pltpu.make_async_copy(held.at[s, rows], blocks[s].at[rows], out_sems.at[x])
            )
            stores[-1].start()
        for i in range(tok // BLOCK):
            rows = slice(i * BLOCK, (i + 1) * BLOCK)
            scores = blocked_scores(query[rows], keys, flags[i], i)
            top = jnp.max(scores, axis=1, keepdims=True)
            out, weight = weigh(jnp.exp2(scores - top), vals)
            own[x, rows, :] = out / weight
            lses[i] = jnp.where(lane == x, top + jnp.log2(weight), lses[i])
        stores.append(
            pltpu.make_async_copy(own.at[x], own_ref.at[:, cols(h)], out_sems.at[heads + x])
        )
        stores[-1].start()
    def split(rest):
        parts = []
        for _ in range(3):
            parts.append(rest.astype(jnp.bfloat16).astype(jnp.float32))
            rest = rest - parts[-1]
        return parts

    lses = [split(lse.T[:ROWS]) for lse in lses]
    norms = [split(inv_row[:, i * BLOCK : (i + 1) * BLOCK]) for i in range(tok // BLOCK)]
    lane = lax.broadcasted_iota(jnp.int32, (1, HD), 1)
    mask = jnp.where(lane == 0, masks[1, 0, 1], masks[1, 1, 0])
    tail = norms[0] + norms[1] + [(mask == 1).astype(jnp.float32)]
    at = 2 * tok + pos
    for s in range(n):
        first = heads - n + s
        rows = [piece[first : first + 1, :] for half in lses for piece in half]
        late = (me ^ s) // parts == 1
        upper = (me ^ s) % parts * pos >= BLOCK
        for low, high in zip(*lses):
            piece = jnp.where(upper, high, low)
            rows.append(jnp.where(late, piece[1:2, :], piece[0:1, :]))
        held[s, at : at + ROWS, :] = jnp.concatenate(rows + tail, axis=0).astype(jnp.bfloat16)
        rows = pl.ds(at, ROWS)
        stores.append(
            pltpu.make_async_copy(held.at[s, rows], blocks[s].at[rows], out_sems.at[2 * heads + s])
        )
        stores[-1].start()
    for copy in stores:
        copy.wait()


def inverse(value):
    guess = pl.reciprocal(value, approx=True)
    return guess * (2.0 - value * guess)


def turned(vals):
    return jnp.concatenate([vals.T, jnp.ones((ONES, vals.shape[0]), vals.dtype)], axis=0)


def turn_kernel(n, tok, pos, at_ref, v_ref, out_ref):
    gp = tok // n
    me = lax.axis_index("frame")
    for g in range((tok + pos) // gp):
        rows = [v_ref[me ^ s, g * gp : (g + 1) * gp, :] for s in range(n)]
        out_ref[g] = turned(jnp.concatenate(rows, axis=0))
    out_ref[(tok + pos) // gp] = turned(v_ref[at_ref[0], :tok, :])


def attend_tiles(tiles):
    scores = [(dot_t(t[1], t[0]), dot_t(t[3], t[0])) for t in tiles]
    weights = []
    for t, (paired, anchored) in zip(tiles, scores):
        lse, flag, i = t[5:]
        near = paired[i * BLOCK : (i + 1) * BLOCK]
        away = paired[(1 - i) * BLOCK : (2 - i) * BLOCK] + flag
        top = jnp.maximum(
            jnp.max(near, axis=0, keepdims=True), jnp.max(away, axis=0, keepdims=True)
        )
        both = [jnp.exp2(near - top), jnp.exp2(away - top)]
        both = jnp.concatenate(both if i == 0 else both[::-1], axis=0)
        top = jnp.maximum(jnp.max(anchored, axis=0, keepdims=True), lse)
        own = jnp.exp2(lse - top)
        anchored = jnp.exp2(anchored - top)
        weights.append((both.astype(jnp.bfloat16), anchored.astype(jnp.bfloat16), own))
    sums = [
        (
            jnp.dot(t[2], both, preferred_element_type=jnp.float32),
            jnp.dot(t[4], anchored, preferred_element_type=jnp.float32),
            own,
        )
        for t, (both, anchored, own) in zip(tiles, weights)
    ]
    results = []
    for paired, anchored, own in sums:
        scale = inverse(anchored[HD : HD + 1] + own)
        result = paired[:HD] * inverse(paired[HD : HD + 1]) + anchored[:HD] * scale
        results.append((result.T.astype(jnp.bfloat16), own * scale))
    return results


def spin(rows, parts):
    parts %= HD // rows[1]
    return rows[0] if parts == 0 else pltpu.roll(rows[0], parts * rows[1], 1)


def gather_lanes(rows, place, gp):
    lane = lax.broadcasted_iota(jnp.int32, (1, HD), 1) // gp
    out = None
    for j in range(rows.shape[0]):
        row = spin((rows, gp), j - place)[j : j + 1]
        out = row if out is None else jnp.where(lane == j, row, out)
    return out


def scatter_lanes(kept, row, place, gp):
    lane = lax.broadcasted_iota(jnp.int32, (1, HD), 1) // gp
    for j in range(len(kept)):
        kept[j] = jnp.where(lane == place, spin((row, gp), place - j), kept[j])


def side_rows(blocks, at, first):
    rows = []
    for block in blocks:
        side = block[at : at + ROWS, :].astype(jnp.float32)
        rows.append(side[first : first + 1] + side[first + 1 : first + 2] + side[first + 2 : first + 3])
    return jnp.concatenate(rows, axis=0)


def keep_flags(n, blocks, at, flag_ref):
    masks = [block[at : at + ROWS, :].astype(jnp.float32)[MASK_ROW:] for block in blocks]
    masks = jnp.concatenate(masks, axis=0)
    flags = [jnp.broadcast_to(masks[:, i : i + 1], (n, HD)) for i in range(2)]
    flags = [jnp.where(flag == 1.0, 0.0, NEG) for flag in flags]
    upper = lax.axis_index("frame") >= n // 2
    for i in range(2):
        flag_ref[i] = jnp.where(upper, flags[1 - i], flags[i])


def stack_rows(blocks, at, gp):
    return jnp.concatenate([block[at : at + gp, :] for block in blocks], axis=0)


def whole_kernel(n, tok, pos, at_ref, vt_ref, *refs):
    blocks, outs, side_ref = refs[:n], refs[n : 2 * n], refs[2 * n]
    key_ref, flag_ref = refs[2 * n + 1 :]
    gp = tok // n
    per = n // 2
    me = lax.axis_index("frame")
    for s in range(n):

        @pl.when(at_ref[0] == me ^ s)
        def _():
            key_ref[...] = blocks[s][tok : 2 * tok, :]

    at_side = 2 * tok + pos
    keep_flags(n, blocks, at_side, flag_ref)
    ka, va = key_ref[...], vt_ref[(tok + pos) // gp]
    halves = [blocks[:per], blocks[per:]]
    lses = [[side_rows(half, at_side, 3 * b) for b in range(2)] for half in halves]
    kept = [[[jnp.zeros((1, HD), jnp.float32)] * per for _ in range(2)] for _ in range(2)]
    across = BLOCK // gp
    together = 2
    for g0 in range(0, n, together):
        tiles, places = [], []
        for g in range(g0, g0 + together):
            keys = stack_rows(blocks, tok + g * gp, gp)
            for i, half in enumerate(halves):
                query = stack_rows(half, g * gp, gp)
                lse = gather_lanes(lses[i][g // across], g % across, gp)
                flag = flag_ref[i, pl.ds(g ^ me, 1), :]
                tiles.append((query, keys, vt_ref[g], ka, va, lse, flag, i))
                places.append((g, i))
        for (g, i), (result, keep) in zip(places, attend_tiles(tiles)):
            for j in range(per):
                outs[i * per + j][g * gp : (g + 1) * gp, :] = result[j * gp : (j + 1) * gp]
            scatter_lanes(kept[i][g // across], keep, g % across, gp)
    rows = [kept[s // per][b][s % per] for s in range(n) for b in range(2)]
    side_ref[...] = jnp.concatenate(rows, axis=0)


def part_kernel(n, tok, pos, at_ref, gain_ref, held_ref, vt_ref, v_ref, *refs):
    blocks, done, came_ref = refs[:n], refs[n : 2 * n], refs[2 * n]
    outs, flag_ref, col_ref = refs[2 * n + 1 : 3 * n + 1], refs[3 * n + 1], refs[3 * n + 2]
    gp = tok // n
    per = n // 2
    parts = tok // pos
    me = lax.axis_index("frame")
    anchor = at_ref[0]
    quarter = me % parts
    odd = quarter * pos % BLOCK != 0
    late = quarter * pos >= BLOCK
    gain = jnp.where(me // parts == 1, gain_ref[n + 1 : n + 2, :], gain_ref[n : n + 1, :])
    at_side = 2 * tok + pos
    keep_flags(n, blocks, at_side, flag_ref)
    norms = [side_rows(blocks, at_side, NORM_ROW + 3 * b) for b in range(2)]
    rows = [jnp.where(late, norms[1], norms[0])]
    for norm in norms:
        row = norm[0:1]
        for s in range(1, n):
            row = jnp.where(anchor == me ^ s, norm[s : s + 1], row)
        rows.append(row)
    rows.append(jnp.zeros((HD - n - 2, HD), jnp.float32))
    col_ref[...] = jnp.concatenate(rows, axis=0).T
    va = turned(jnp.concatenate([held_ref[j, :pos, :] for j in range(parts)], axis=0))
    ka = jnp.concatenate([held_ref[j, pos:, :] for j in range(parts)], axis=0)
    norm = jnp.concatenate([col_ref[:, n + b : n + b + 1] for b in range(2)], axis=0)
    ka = scaled(ka, norm, gain)
    halves = [blocks[:per], blocks[per:]]
    lses = []
    for half in halves:
        lse = side_rows(half, at_side, LSE_ROW)
        lses.append(jnp.where(odd, pltpu.roll(lse, HD - pos, 1), lse))
    kept = [[jnp.zeros((1, HD), jnp.float32)] * per for _ in range(2)]
    tiles, places = [], []
    for u in range(pos // gp):
        first = pl.multiple_of(quarter * pos % BLOCK + u * gp, gp)
        cols = col_ref[pl.ds(first, gp), :]
        norm = jnp.concatenate([cols[:, s : s + 1] for s in range(n)], axis=0)
        at = tok + pos + u * gp
        keys = jnp.concatenate([v_ref[me ^ s, at : at + gp, :] for s in range(n)], axis=0)
        keys = scaled(keys, norm, gain)
        for i, half in enumerate(halves):
            query = stack_rows(half, 2 * tok + u * gp, gp)
            lse = gather_lanes(lses[i], u, gp)
            flag = flag_ref[i, pl.ds((quarter * (pos // gp) + u) ^ me, 1), :]
            tiles.append((query, keys, vt_ref[n + u], ka, va, lse, flag, i))
            places.append((tok + u * gp, u, i))
    for s in range(n):
        outs[s][:tok, :] = done[s][...]
    for (at, u, i), (result, keep) in zip(places, attend_tiles(tiles)):
        for j in range(per):
            outs[i * per + j][at : at + gp, :] = result[j * gp : (j + 1) * gp]
        scatter_lanes(kept[i], keep, u, gp)
    pad = jnp.zeros((ROWS - 3, HD), jnp.float32)
    for s in range(n):
        rows = [came_ref[2 * s : 2 * s + 2, :], kept[s // per][s % per], pad]
        rows = jnp.concatenate(rows, axis=0)
        outs[s][tok + pos : tok + pos + ROWS, :] = rows.astype(jnp.bfloat16)


def join_kernel(n, pos, own_ref, *refs):
    back, out_ref = refs[:n], refs[n]
    tok = own_ref.shape[0]
    parts = tok // pos
    me = lax.axis_index("frame")
    at_side = tok + pos
    sides = jnp.concatenate([block[at_side : at_side + ROWS, :] for block in back], axis=0).T
    sub = lax.broadcasted_iota(jnp.int32, (n * ROWS, HD), 0)

    def spread_lanes(row):
        pick = (sub == row).astype(jnp.bfloat16)
        return jnp.dot(sides, pick, preferred_element_type=jnp.float32)

    for s in range(n):
        d = me ^ s
        keeps = [spread_lanes(s * ROWS + r) for r in range(3)]
        whole = pl.ds(pl.multiple_of(d * HD, HD), HD)
        for b in range(tok // BLOCK):
            rows = slice(b * BLOCK, (b + 1) * BLOCK)
            got = back[s][rows, :].astype(jnp.float32)
            out_ref[rows, whole] = (own_ref[rows, whole] * keeps[b] + got).astype(jnp.bfloat16)
        part = pl.ds(pl.multiple_of((n + d // parts) * HD, HD), HD)
        rows = pl.ds(pl.multiple_of(d % parts * pos, pos), pos)
        got = back[s][tok : tok + pos, :].astype(jnp.float32)
        out_ref[rows, part] = (own_ref[rows, part] * keeps[2][:pos] + got).astype(jnp.bfloat16)


def call(kernel, out_shape, *args, vmem=40, **more):
    return pl.pallas_call(
        kernel,
        out_shape=out_shape,
        compiler_params=pltpu.CompilerParams(vmem_limit_bytes=vmem * 1024 * 1024),
        **more,
    )(*args)


def pairwise(array, axis, step):
    size = lax.axis_size(axis)
    return lax.ppermute(array, axis, [(i, i ^ step) for i in range(size)])


def swap_blocks(blocks):
    n = len(blocks)
    got = {0: blocks[0]}
    wide = sorted(range(n // 2, n), key=lambda s: (s % 2, s))
    for s in wide + [1, 2]:
        got[s] = pairwise(blocks[s], "frame", s)
    for s in range(3, n // 2):
        block, _ = lax.optimization_barrier((blocks[s], got[s - 1]))
        got[s] = pairwise(block, "frame", s)
    return [got[s] for s in range(n)]


def local_heads(
    q_raw, k_raw, values, q_gain, k_gain, spatial_mask, temporal_mask, anchor_frame
):
    tok, width = q_raw.shape
    n = lax.axis_size("frame")
    n_mp = lax.axis_size("mp")
    heads = width // HD
    parts = n // (heads - n)
    pos = tok // parts
    me = lax.axis_index("frame")
    shape = jax.ShapeDtypeStruct
    vm = pl.BlockSpec(memory_space=pltpu.VMEM)
    sm = pl.BlockSpec(memory_space=pltpu.SMEM)
    hbm = pl.BlockSpec(memory_space=pltpu.HBM)
    dma = pltpu.SemaphoreType.DMA
    bf16, f32 = jnp.bfloat16, jnp.float32

    v_blocks = call(
        functools.partial(cut_kernel, n, pos),
        shape((n, tok + 2 * pos, HD), bf16),
        k_raw,
        values,
        in_specs=[hbm] * 2,
        out_specs=hbm,
        scratch_shapes=[pltpu.VMEM((n, tok + 2 * pos, HD), bf16), dma((4, n))],
        vmem=60,
    )
    q_raw, k_raw, values, v_blocks = lax.optimization_barrier((q_raw, k_raw, values, v_blocks))
    sums = call(
        squares_kernel,
        shape((8, tok), f32),
        q_raw,
        k_raw,
        in_specs=[hbm] * 2,
        scratch_shapes=[pltpu.VMEM((2, tok, width), bf16), dma((2, 4))],
        vmem=60,
    )
    all_sums = [sums] + [pairwise(sums, "mp", step) for step in range(1, n_mp)]
    v_far = lax.all_to_all(v_blocks, "frame", split_axis=0, concat_axis=0, tiled=True)
    rows = 2 * tok + pos + ROWS
    *sent, own = call(
        functools.partial(own_kernel, n, pos),
        [shape((rows, HD), bf16)] * n + [shape((tok, width), f32)],
        q_raw,
        k_raw,
        values,
        *all_sums,
        q_gain.reshape(heads, HD),
        k_gain.reshape(heads, HD),
        spatial_mask[0],
        temporal_mask[0],
        in_specs=[hbm] * 11,
        out_specs=[hbm] * (n + 1),
        scratch_shapes=[
            pltpu.VMEM((3, heads, tok, HD), bf16),
            pltpu.VMEM((n, rows, HD), bf16),
            pltpu.VMEM((heads - n, tok, HD), bf16),
            pltpu.VMEM((heads, tok, HD), f32),
            pltpu.VMEM((4, 8, tok), f32),
            pltpu.VMEM((2, heads, HD), f32),
            pltpu.SMEM((2, 2, 2), jnp.int32),
            dma((3 * heads + 8,)),
            dma((2 * heads + n,)),
        ],
        vmem=60,
    )
    far = swap_blocks(sent)
    block, v_far = lax.optimization_barrier((sent[0], v_far))
    far[0] = call(copy_kernel, shape((rows, HD), bf16), block, vmem=8)

    anchor = anchor_frame[0]
    mine = lax.dynamic_slice(v_far, (anchor, tok, 0), (1, 2 * pos, HD))
    groups = [list(range(first, first + parts)) for first in range(0, n, parts)]
    held = lax.all_to_all(
        jnp.broadcast_to(mine, (parts, 2 * pos, HD)),
        "frame",
        split_axis=0,
        concat_axis=0,
        axis_index_groups=groups,
        tiled=True,
    )
    pencils = (tok + pos) // (tok // n)
    vt = call(
        functools.partial(turn_kernel, n, tok, pos),
        shape((pencils + 1, HD + ONES, tok), bf16),
        anchor_frame,
        v_far,
        in_specs=[sm, vm],
    )
    exps = n * tok * 2 * tok
    *done, side = call(
        functools.partial(whole_kernel, n, tok, pos),
        [shape((tok, HD), bf16)] * n + [shape((2 * n, HD), f32)],
        anchor_frame,
        vt,
        *far,
        in_specs=[sm] + [vm] * (n + 1),
        scratch_shapes=[pltpu.VMEM((tok, HD), bf16), pltpu.VMEM((2, n, HD), f32)],
        cost_estimate=pl.CostEstimate(
            flops=6 * exps * HD, bytes_accessed=8 * n * tok * HD, transcendentals=exps
        ),
    )
    result = call(
        functools.partial(part_kernel, n, tok, pos),
        [shape((tok + pos + ROWS, HD), bf16)] * n,
        anchor_frame,
        k_gain.reshape(heads, HD),
        held,
        vt,
        v_far,
        *far,
        *done,
        side,
        in_specs=[sm] + [vm] * (2 * n + 5),
        scratch_shapes=[pltpu.VMEM((2, n, HD), f32), pltpu.VMEM((HD, HD), f32)],
    )
    back = swap_blocks(result)
    return call(
        functools.partial(join_kernel, n, pos), shape((tok, width), bf16), own, *back
    )


def solution(mesh):
    n = mesh.shape["frame"]

    def local(*args):
        tok, width = args[0].shape
        fits = n == 8 and mesh.shape["mp"] == 4 and width == 10 * HD and tok == 2 * BLOCK
        return local_heads(*args) if fits else local_general(*args)

    return jax.shard_map(
        local,
        mesh=mesh,
        in_specs=(
            P("frame", "mp"),
            P("frame", "mp"),
            P("frame", "mp"),
            P("mp"),
            P("mp"),
            P("frame", None, None),
            P("frame", None, None),
            P(),
        ),
        out_specs=P("frame", "mp"),
        check_vma=False,
    )
```

```python
import functools

import jax
import jax.numpy as jnp
from jax import lax
from jax.experimental import pallas as pl
from jax.experimental.pallas import tpu as pltpu
from jax.sharding import PartitionSpec as P

D = 5120
HD = 128
BLOCK = 128
LOG2E = 1.4426950408889634
NEG = -1e30


def spread(value, axis, source):
    kept = jnp.where(lax.axis_index(axis) == source, value, 0).astype(value.dtype)
    return lax.psum(kept, axis)


def expand(block_mask):
    count = block_mask.shape[0]
    allowed = (block_mask == 1) | jnp.eye(count, dtype=jnp.bool_)
    return jnp.repeat(jnp.repeat(allowed, BLOCK, axis=0), BLOCK, axis=1)


def attend(query, keys, vals, allowed):
    rows = query.shape[0]
    width = query.shape[1]
    heads_dev = width // HD
    query3 = jnp.transpose(query.reshape(rows, heads_dev, HD), (1, 0, 2))
    keys3 = jnp.transpose(keys.reshape(keys.shape[0], heads_dev, HD), (1, 0, 2))
    vals3 = jnp.transpose(vals.reshape(vals.shape[0], heads_dev, HD), (1, 0, 2))
    scale = jnp.sqrt(jnp.float32(HD))

    def one_head(items):
        head_q, head_k, head_v = items
        scores = jnp.einsum("qd,kd->qk", head_q, head_k, preferred_element_type=jnp.float32) / scale
        scores = jnp.where(allowed, scores, -jnp.inf)
        probs = jax.nn.softmax(scores, axis=-1).astype(jnp.bfloat16)
        return jnp.dot(probs, head_v, preferred_element_type=jnp.float32)

    output = lax.map(one_head, (query3, keys3, vals3))
    return jnp.transpose(output, (1, 0, 2)).reshape(rows, width)


def local_general(
    q_raw, k_raw, values, q_gain, k_gain, spatial_mask, temporal_mask, anchor_frame
):
    frame_tok = q_raw.shape[0]
    width = q_raw.shape[1]
    q_float = q_raw.astype(jnp.float32)
    k_float = k_raw.astype(jnp.float32)
    sum_q, sum_k = lax.psum(
        (jnp.sum(q_float * q_float, axis=1), jnp.sum(k_float * k_float, axis=1)), "mp"
    )
    q_norm = (q_float / jnp.sqrt(sum_q[:, None] / D + 1e-06) * q_gain[None, :]).astype(jnp.bfloat16)
    k_norm = (k_float / jnp.sqrt(sum_k[:, None] / D + 1e-06) * k_gain[None, :]).astype(jnp.bfloat16)
    n_frames = lax.axis_size("frame")
    group_pos = frame_tok // n_frames

    def regroup(array):
        return lax.all_to_all(
            array.reshape(n_frames, group_pos, width),
            "frame",
            split_axis=0,
            concat_axis=0,
            tiled=True,
        ).reshape(frame_tok, width)

    anchor = anchor_frame[0]
    k_anchor, v_anchor = (spread(k_norm, "frame", anchor), spread(values, "frame", anchor))
    own_allowed = jnp.concatenate(
        [expand(spatial_mask[0]), jnp.ones((frame_tok, frame_tok), dtype=jnp.bool_)], axis=1
    )
    spatial = attend(
        q_norm,
        jnp.concatenate([k_norm, k_anchor], 0),
        jnp.concatenate([values, v_anchor], 0),
        own_allowed,
    )
    temporal = attend(
        regroup(q_norm), regroup(k_norm), regroup(values), expand(temporal_mask[0])
    ).astype(jnp.bfloat16)
    returned = regroup(temporal)
    return (spatial + returned.astype(jnp.float32)).astype(jnp.bfloat16)


ROWS = 16
LSE_ROW = 6
NORM_ROW = 9
MASK_ROW = 15
ONES = 8


def dot_t(a, b):
    return lax.dot_general(a, b, (((1,), (1,)), ((), ())), preferred_element_type=jnp.float32)


def weigh(weights, vals):
    ones = jnp.ones(vals.shape, vals.dtype)
    both = jnp.dot(
        weights.astype(jnp.bfloat16),
        jnp.concatenate([vals, ones], axis=1),
        preferred_element_type=jnp.float32,
    )
    return both[:, :HD], both[:, HD:]


def blocked_scores(query, keys, flag, i):
    scores = dot_t(query, keys)
    near = scores[:, i * BLOCK : (i + 1) * BLOCK]
    away = scores[:, (1 - i) * BLOCK : (2 - i) * BLOCK] + flag
    return jnp.concatenate([near, away] if i == 0 else [away, near], axis=1)


def scaled(rows, column, gain):
    return (rows.astype(jnp.float32) * column * gain).astype(jnp.bfloat16)


def cut_kernel(n, pos, k_ref, v_ref, out_ref, cut, sems):
    tok = k_ref.shape[0]
    parts = tok // pos
    loads, stores = [], []
    for d in range(n):
        row = d % parts * pos
        pieces = (
            (v_ref, d, 0, tok, 0),
            (v_ref, n + d // parts, row, pos, tok),
            (k_ref, n + d // parts, row, pos, tok + pos),
        )
        for j, (ref, head, row, rows, at) in enumerate(pieces):
            loads.append(
                pltpu.make_async_copy(
                    ref.at[pl.ds(row, rows), pl.ds(head * HD, HD)],
                    cut.at[d, pl.ds(at, rows)],
                    sems.at[j, d],
                )
            )
            loads[-1].start()
        stores.append(pltpu.make_async_copy(cut.at[d], out_ref.at[d], sems.at[3, d]))
    for d in range(n):
        for copy in loads[3 * d : 3 * d + 3]:
            copy.wait()
        stores[d].start()
    for copy in stores:
        copy.wait()


def squares_kernel(q_ref, k_ref, out_ref, held, sems):
    tok = q_ref.shape[0]
    chunks = sems.shape[1]
    step = tok // chunks
    copies = []
    for t, ref in enumerate((q_ref, k_ref)):
        for c in range(chunks):
            rows = pl.ds(c * step, step)
            copies.append(pltpu.make_async_copy(ref.at[rows], held.at[t, rows], sems.at[t, c]))
    for copy in copies:
        copy.start()
    rows = []
    for t in range(2):
        parts = []
        for c in range(chunks):
            copies[t * chunks + c].wait()
            total = None
            for h in range(q_ref.shape[1] // HD):
                part = held[t, c * step : (c + 1) * step, h * HD : (h + 1) * HD]
                part = part.astype(jnp.float32)
                total = part * part if total is None else total + part * part
            parts.append(total)
        rows.append(jnp.sum(jnp.concatenate(parts, axis=0).T, axis=0, keepdims=True))
    out_ref[...] = jnp.concatenate(rows + [jnp.zeros((6, tok), jnp.float32)], axis=0)


def copy_kernel(in_ref, out_ref):
    out_ref[...] = in_ref[...]


def own_kernel(n, pos, *refs):
    args, blocks, own_ref = refs[:11], refs[11 : 11 + n], refs[11 + n]
    ins, held, extra, own, sums, gains, masks, in_sems, out_sems = refs[12 + n :]
    q_ref, k_ref, v_ref = args[:3]
    tok = q_ref.shape[0]
    heads = q_ref.shape[1] // HD
    parts = tok // pos
    me = lax.axis_index("frame")
    order = [n + e for e in range(heads - n)] + [me ^ s for s in range(n)]

    def cols(h):
        return pl.ds(pl.multiple_of(h * HD, HD), HD)

    small = []
    for j in range(4):
        small.append(pltpu.make_async_copy(args[3 + j], sums.at[j], in_sems.at[3 * heads + j]))
    for j in range(2):
        at = in_sems.at[3 * heads + 4 + j]
        small.append(pltpu.make_async_copy(args[7 + j], gains.at[j], at))
        at = in_sems.at[3 * heads + 6 + j]
        small.append(pltpu.make_async_copy(args[9 + j], masks.at[j], at))
    loads = [
        pltpu.make_async_copy(ref.at[:, cols(h)], ins.at[t, x], in_sems.at[3 * x + t])
        for x, h in enumerate(order)
        for t, ref in enumerate((q_ref, k_ref, v_ref))
    ]
    for copy in small + loads:
        copy.start()
    for copy in small:
        copy.wait()
    inv = lax.rsqrt((sums[0] + sums[1] + sums[2] + sums[3]) / D + 1e-06)
    inv_row = inv[1:2, :]
    inv = inv.T
    inv_q = jnp.broadcast_to(inv[:, 0:1] * (LOG2E / float(HD) ** 0.5), (tok, HD))
    inv_k = jnp.broadcast_to(inv[:, 1:2], (tok, HD))
    flags = [jnp.where(masks[0, i, 1 - i] == 1, 0.0, NEG) for i in range(2)]
    lane = lax.broadcasted_iota(jnp.int32, (BLOCK, HD), 1)
    lses = [jnp.zeros((BLOCK, HD), jnp.float32) for _ in range(tok // BLOCK)]
    stores = []
    for x, h in enumerate(order):
        if x in (0, heads // 2):
            for copy in loads[3 * x : 3 * (x + heads // 2)]:
                copy.wait()
        query = scaled(ins[0, x], inv_q, gains[0, pl.ds(h, 1), :])
        keys = scaled(ins[1, x], inv_k, gains[1, pl.ds(h, 1), :])
        vals = ins[2, x]
        if x < heads - n:
            extra[x] = query
        else:
            s = x - (heads - n)
            held[s, :tok, :] = query
            held[s, tok : 2 * tok, :] = keys
            rows = pl.ds(pl.multiple_of((me ^ s) % parts * pos, pos), pos)
            held[s, 2 * tok : 2 * tok + pos, :] = extra[(me ^ s) // parts, rows, :]
            rows = pl.ds(0, 2 * tok + pos)
            stores.append(
                pltpu.make_async_copy(held.at[s, rows], blocks[s].at[rows], out_sems.at[x])
            )
            stores[-1].start()
        for i in range(tok // BLOCK):
            rows = slice(i * BLOCK, (i + 1) * BLOCK)
            scores = blocked_scores(query[rows], keys, flags[i], i)
            top = jnp.max(scores, axis=1, keepdims=True)
            out, weight = weigh(jnp.exp2(scores - top), vals)
            own[x, rows, :] = out / weight
            lses[i] = jnp.where(lane == x, top + jnp.log2(weight), lses[i])
        stores.append(
            pltpu.make_async_copy(own.at[x], own_ref.at[:, cols(h)], out_sems.at[heads + x])
        )
        stores[-1].start()
    def split(rest):
        parts = []
        for _ in range(3):
            parts.append(rest.astype(jnp.bfloat16).astype(jnp.float32))
            rest = rest - parts[-1]
        return parts

    lses = [split(lse.T[:ROWS]) for lse in lses]
    norms = [split(inv_row[:, i * BLOCK : (i + 1) * BLOCK]) for i in range(tok // BLOCK)]
    lane = lax.broadcasted_iota(jnp.int32, (1, HD), 1)
    mask = jnp.where(lane == 0, masks[1, 0, 1], masks[1, 1, 0])
    tail = norms[0] + norms[1] + [(mask == 1).astype(jnp.float32)]
    at = 2 * tok + pos
    for s in range(n):
        first = heads - n + s
        rows = [piece[first : first + 1, :] for half in lses for piece in half]
        late = (me ^ s) // parts == 1
        upper = (me ^ s) % parts * pos >= BLOCK
        for low, high in zip(*lses):
            piece = jnp.where(upper, high, low)
            rows.append(jnp.where(late, piece[1:2, :], piece[0:1, :]))
        held[s, at : at + ROWS, :] = jnp.concatenate(rows + tail, axis=0).astype(jnp.bfloat16)
        rows = pl.ds(at, ROWS)
        stores.append(
            pltpu.make_async_copy(held.at[s, rows], blocks[s].at[rows], out_sems.at[2 * heads + s])
        )
        stores[-1].start()
    for copy in stores:
        copy.wait()


FAR_ORDER = (0, 1, 2, 3, 4, 5, 6, 7)
BACK_ORDER = (0, 1, 2, 3, 4, 5, 6, 7)


def by_step(refs, order):
    return [refs[order.index(s)] for s in range(len(order))]


def inverse(value):
    guess = pl.reciprocal(value, approx=True)
    return guess * (2.0 - value * guess)


def turned(vals):
    return jnp.concatenate([vals.T, jnp.ones((ONES, vals.shape[0]), vals.dtype)], axis=0)


def turn_kernel(n, tok, pos, at_ref, v_ref, out_ref):
    gp = tok // n
    me = lax.axis_index("frame")
    for g in range((tok + pos) // gp):
        rows = [v_ref[me ^ s, g * gp : (g + 1) * gp, :] for s in range(n)]
        out_ref[g] = turned(jnp.concatenate(rows, axis=0))
    out_ref[(tok + pos) // gp] = turned(v_ref[at_ref[0], :tok, :])


def attend_tiles(tiles):
    scores = [(dot_t(t[1], t[0]), dot_t(t[3], t[0])) for t in tiles]
    weights = []
    for t, (paired, anchored) in zip(tiles, scores):
        lse, flag, i = t[5:]
        near = paired[i * BLOCK : (i + 1) * BLOCK]
        away = paired[(1 - i) * BLOCK : (2 - i) * BLOCK] + flag
        top = jnp.maximum(
            jnp.max(near, axis=0, keepdims=True), jnp.max(away, axis=0, keepdims=True)
        )
        both = [jnp.exp2(near - top), jnp.exp2(away - top)]
        both = jnp.concatenate(both if i == 0 else both[::-1], axis=0)
        top = jnp.maximum(jnp.max(anchored, axis=0, keepdims=True), lse)
        own = jnp.exp2(lse - top)
        anchored = jnp.exp2(anchored - top)
        weights.append((both.astype(jnp.bfloat16), anchored.astype(jnp.bfloat16), own))
    sums = [
        (
            jnp.dot(t[2], both, preferred_element_type=jnp.float32),
            jnp.dot(t[4], anchored, preferred_element_type=jnp.float32),
            own,
        )
        for t, (both, anchored, own) in zip(tiles, weights)
    ]
    results = []
    for paired, anchored, own in sums:
        scale = inverse(anchored[HD : HD + 1] + own)
        result = paired[:HD] * inverse(paired[HD : HD + 1]) + anchored[:HD] * scale
        results.append((result.T.astype(jnp.bfloat16), own * scale))
    return results


def spin(rows, parts):
    parts %= HD // rows[1]
    return rows[0] if parts == 0 else pltpu.roll(rows[0], parts * rows[1], 1)


def gather_lanes(rows, place, gp):
    lane = lax.broadcasted_iota(jnp.int32, (1, HD), 1) // gp
    out = None
    for j in range(rows.shape[0]):
        row = spin((rows, gp), j - place)[j : j + 1]
        out = row if out is None else jnp.where(lane == j, row, out)
    return out


def scatter_lanes(kept, row, place, gp):
    lane = lax.broadcasted_iota(jnp.int32, (1, HD), 1) // gp
    for j in range(len(kept)):
        kept[j] = jnp.where(lane == place, spin((row, gp), place - j), kept[j])


def side_rows(blocks, at, first):
    rows = []
    for block in blocks:
        side = block[at : at + ROWS, :].astype(jnp.float32)
        rows.append(side[first : first + 1] + side[first + 1 : first + 2] + side[first + 2 : first + 3])
    return jnp.concatenate(rows, axis=0)


def keep_flags(n, blocks, at, flag_ref):
    masks = [block[at : at + ROWS, :].astype(jnp.float32)[MASK_ROW:] for block in blocks]
    masks = jnp.concatenate(masks, axis=0)
    flags = [jnp.broadcast_to(masks[:, i : i + 1], (n, HD)) for i in range(2)]
    flags = [jnp.where(flag == 1.0, 0.0, NEG) for flag in flags]
    upper = lax.axis_index("frame") >= n // 2
    for i in range(2):
        flag_ref[i] = jnp.where(upper, flags[1 - i], flags[i])


def stack_rows(blocks, at, gp):
    return jnp.concatenate([block[at : at + gp, :] for block in blocks], axis=0)


def whole_kernel(n, tok, pos, at_ref, vt_ref, *refs):
    blocks, outs, side_ref = by_step(refs[:n], FAR_ORDER), refs[n : 2 * n], refs[2 * n]
    key_ref, flag_ref = refs[2 * n + 1 :]
    gp = tok // n
    per = n // 2
    me = lax.axis_index("frame")
    for s in range(n):

        @pl.when(at_ref[0] == me ^ s)
        def _():
            key_ref[...] = blocks[s][tok : 2 * tok, :]

    at_side = 2 * tok + pos
    keep_flags(n, blocks, at_side, flag_ref)
    ka, va = key_ref[...], vt_ref[(tok + pos) // gp]
    halves = [blocks[:per], blocks[per:]]
    lses = [[side_rows(half, at_side, 3 * b) for b in range(2)] for half in halves]
    kept = [[[jnp.zeros((1, HD), jnp.float32)] * per for _ in range(2)] for _ in range(2)]
    across = BLOCK // gp
    together = 4
    for g0 in range(0, n, together):
        tiles, places = [], []
        for g in range(g0, g0 + together):
            keys = stack_rows(blocks, tok + g * gp, gp)
            for i, half in enumerate(halves):
                query = stack_rows(half, g * gp, gp)
                lse = gather_lanes(lses[i][g // across], g % across, gp)
                flag = flag_ref[i, pl.ds(g ^ me, 1), :]
                tiles.append((query, keys, vt_ref[g], ka, va, lse, flag, i))
                places.append((g, i))
        for (g, i), (result, keep) in zip(places, attend_tiles(tiles)):
            for j in range(per):
                outs[i * per + j][g * gp : (g + 1) * gp, :] = result[j * gp : (j + 1) * gp]
            scatter_lanes(kept[i][g // across], keep, g % across, gp)
    rows = [kept[s // per][b][s % per] for s in range(n) for b in range(2)]
    side_ref[...] = jnp.concatenate(rows, axis=0)


def part_kernel(n, tok, pos, at_ref, gain_ref, held_ref, vt_ref, v_ref, *refs):
    blocks, done, came_ref = by_step(refs[:n], FAR_ORDER), refs[n : 2 * n], refs[2 * n]
    outs, flag_ref, col_ref = refs[2 * n + 1 : 3 * n + 1], refs[3 * n + 1], refs[3 * n + 2]
    gp = tok // n
    per = n // 2
    parts = tok // pos
    me = lax.axis_index("frame")
    anchor = at_ref[0]
    quarter = me % parts
    odd = quarter * pos % BLOCK != 0
    late = quarter * pos >= BLOCK
    gain = jnp.where(me // parts == 1, gain_ref[n + 1 : n + 2, :], gain_ref[n : n + 1, :])
    at_side = 2 * tok + pos
    keep_flags(n, blocks, at_side, flag_ref)
    norms = [side_rows(blocks, at_side, NORM_ROW + 3 * b) for b in range(2)]
    rows = [jnp.where(late, norms[1], norms[0])]
    for norm in norms:
        row = norm[0:1]
        for s in range(1, n):
            row = jnp.where(anchor == me ^ s, norm[s : s + 1], row)
        rows.append(row)
    rows.append(jnp.zeros((HD - n - 2, HD), jnp.float32))
    col_ref[...] = jnp.concatenate(rows, axis=0).T
    va = turned(jnp.concatenate([held_ref[j, :pos, :] for j in range(parts)], axis=0))
    ka = jnp.concatenate([held_ref[j, pos:, :] for j in range(parts)], axis=0)
    norm = jnp.concatenate([col_ref[:, n + b : n + b + 1] for b in range(2)], axis=0)
    ka = scaled(ka, norm, gain)
    halves = [blocks[:per], blocks[per:]]
    lses = []
    for half in halves:
        lse = side_rows(half, at_side, LSE_ROW)
        lses.append(jnp.where(odd, pltpu.roll(lse, HD - pos, 1), lse))
    kept = [[jnp.zeros((1, HD), jnp.float32)] * per for _ in range(2)]
    tiles, places = [], []
    for u in range(pos // gp):
        first = pl.multiple_of(quarter * pos % BLOCK + u * gp, gp)
        cols = col_ref[pl.ds(first, gp), :]
        norm = jnp.concatenate([cols[:, s : s + 1] for s in range(n)], axis=0)
        at = tok + pos + u * gp
        keys = jnp.concatenate([v_ref[me ^ s, at : at + gp, :] for s in range(n)], axis=0)
        keys = scaled(keys, norm, gain)
        for i, half in enumerate(halves):
            query = stack_rows(half, 2 * tok + u * gp, gp)
            lse = gather_lanes(lses[i], u, gp)
            flag = flag_ref[i, pl.ds((quarter * (pos // gp) + u) ^ me, 1), :]
            tiles.append((query, keys, vt_ref[n + u], ka, va, lse, flag, i))
            places.append((tok + u * gp, u, i))
    for s in range(n):
        outs[s][:tok, :] = done[s][...]
    for (at, u, i), (result, keep) in zip(places, attend_tiles(tiles)):
        for j in range(per):
            outs[i * per + j][at : at + gp, :] = result[j * gp : (j + 1) * gp]
        scatter_lanes(kept[i], keep, u, gp)
    pad = jnp.zeros((ROWS - 3, HD), jnp.float32)
    for s in range(n):
        rows = [came_ref[2 * s : 2 * s + 2, :], kept[s // per][s % per], pad]
        rows = jnp.concatenate(rows, axis=0)
        outs[s][tok + pos : tok + pos + ROWS, :] = rows.astype(jnp.bfloat16)


def join_kernel(n, pos, own_ref, *refs):
    back, out_ref = by_step(refs[:n], BACK_ORDER), refs[n]
    held, sems = refs[n + 1 :]
    tok = own_ref.shape[0]
    parts = tok // pos
    me = lax.axis_index("frame")
    at_side = tok + pos
    sides = jnp.concatenate([block[at_side : at_side + ROWS, :] for block in back], axis=0).T
    sub = lax.broadcasted_iota(jnp.int32, (n * ROWS, HD), 0)

    def spread_lanes(row):
        pick = (sub == row).astype(jnp.bfloat16)
        return jnp.dot(sides, pick, preferred_element_type=jnp.float32)

    copies = []
    for s in range(n):
        d = me ^ s
        keeps = [spread_lanes(s * ROWS + r) for r in range(3)]
        whole = pl.ds(pl.multiple_of(d * HD, HD), HD)
        for b in range(tok // BLOCK):
            rows = slice(b * BLOCK, (b + 1) * BLOCK)
            got = back[s][rows, :].astype(jnp.float32)
            held[s, rows, :] = (own_ref[rows, whole] * keeps[b] + got).astype(jnp.bfloat16)
        copies.append(pltpu.make_async_copy(held.at[s], out_ref.at[:, whole], sems.at[0, s]))
        copies[-1].start()
        part = pl.ds(pl.multiple_of((n + d // parts) * HD, HD), HD)
        rows = pl.ds(pl.multiple_of(d % parts * pos, pos), pos)
        got = back[s][tok : tok + pos, :].astype(jnp.float32)
        got = own_ref[rows, part] * keeps[2][:pos] + got
        held[n + s // parts, s % parts * pos : (s % parts + 1) * pos, :] = got.astype(jnp.bfloat16)
        copies.append(
            pltpu.make_async_copy(
                held.at[n + s // parts, pl.ds(s % parts * pos, pos)], out_ref.at[rows, part], sems.at[1, s]
            )
        )
        copies[-1].start()
    for copy in copies:
        copy.wait()


def call(kernel, out_shape, *args, vmem=40, **more):
    return pl.pallas_call(
        kernel,
        out_shape=out_shape,
        compiler_params=pltpu.CompilerParams(vmem_limit_bytes=vmem * 1024 * 1024),
        **more,
    )(*args)


def pairwise(array, axis, step):
    size = lax.axis_size(axis)
    return lax.ppermute(array, axis, [(i, i ^ step) for i in range(size)])


def swap_blocks(blocks, order, chain):
    got = {0: blocks[0]}
    for s in order:
        block = blocks[s]
        if s in chain:
            block, _ = lax.optimization_barrier((block, got[chain[s]]))
        got[s] = pairwise(block, "frame", s)
    return [got[s] for s in range(len(blocks))]


def local_heads(
    q_raw, k_raw, values, q_gain, k_gain, spatial_mask, temporal_mask, anchor_frame
):
    tok, width = q_raw.shape
    n = lax.axis_size("frame")
    n_mp = lax.axis_size("mp")
    heads = width // HD
    parts = n // (heads - n)
    pos = tok // parts
    me = lax.axis_index("frame")
    shape = jax.ShapeDtypeStruct
    vm = pl.BlockSpec(memory_space=pltpu.VMEM)
    sm = pl.BlockSpec(memory_space=pltpu.SMEM)
    hbm = pl.BlockSpec(memory_space=pltpu.HBM)
    dma = pltpu.SemaphoreType.DMA
    bf16, f32 = jnp.bfloat16, jnp.float32

    v_blocks = call(
        functools.partial(cut_kernel, n, pos),
        shape((n, tok + 2 * pos, HD), bf16),
        k_raw,
        values,
        in_specs=[hbm] * 2,
        out_specs=hbm,
        scratch_shapes=[pltpu.VMEM((n, tok + 2 * pos, HD), bf16), dma((4, n))],
        vmem=60,
    )
    q_raw, k_raw, values, v_blocks = lax.optimization_barrier((q_raw, k_raw, values, v_blocks))
    sums = call(
        squares_kernel,
        shape((8, tok), f32),
        q_raw,
        k_raw,
        in_specs=[hbm] * 2,
        scratch_shapes=[pltpu.VMEM((2, tok, width), bf16), dma((2, 4))],
        vmem=60,
    )
    all_sums = [sums] + [pairwise(sums, "mp", step) for step in range(1, n_mp)]
    v_far = lax.all_to_all(v_blocks, "frame", split_axis=0, concat_axis=0, tiled=True)
    rows = 2 * tok + pos + ROWS
    *sent, own = call(
        functools.partial(own_kernel, n, pos),
        [shape((rows, HD), bf16)] * n + [shape((tok, width), f32)],
        q_raw,
        k_raw,
        values,
        *all_sums,
        q_gain.reshape(heads, HD),
        k_gain.reshape(heads, HD),
        spatial_mask[0],
        temporal_mask[0],
        in_specs=[hbm] * 11,
        out_specs=[hbm] * (n + 1),
        scratch_shapes=[
            pltpu.VMEM((3, heads, tok, HD), bf16),
            pltpu.VMEM((n, rows, HD), bf16),
            pltpu.VMEM((heads - n, tok, HD), bf16),
            pltpu.VMEM((heads, tok, HD), f32),
            pltpu.VMEM((4, 8, tok), f32),
            pltpu.VMEM((2, heads, HD), f32),
            pltpu.SMEM((2, 2, 2), jnp.int32),
            dma((3 * heads + 8,)),
            dma((2 * heads + n,)),
        ],
        vmem=60,
    )
    far = swap_blocks(sent, (4, 6, 5, 7, 1, 2, 3), {3: 2})
    block, v_far, *_ = lax.optimization_barrier((sent[0], v_far, far[1], far[2]))
    far[0] = call(copy_kernel, shape((rows, HD), bf16), block, vmem=8)

    anchor = anchor_frame[0]
    mine = lax.dynamic_slice(v_far, (anchor, tok, 0), (1, 2 * pos, HD))
    groups = [list(range(first, first + parts)) for first in range(0, n, parts)]
    held = lax.all_to_all(
        jnp.broadcast_to(mine, (parts, 2 * pos, HD)),
        "frame",
        split_axis=0,
        concat_axis=0,
        axis_index_groups=groups,
        tiled=True,
    )
    pencils = (tok + pos) // (tok // n)
    vt = call(
        functools.partial(turn_kernel, n, tok, pos),
        shape((pencils + 1, HD + ONES, tok), bf16),
        anchor_frame,
        v_far,
        in_specs=[sm, vm],
    )
    exps = n * tok * 2 * tok
    *done, side = call(
        functools.partial(whole_kernel, n, tok, pos),
        [shape((tok, HD), bf16)] * n + [shape((2 * n, HD), f32)],
        anchor_frame,
        vt,
        *[far[s] for s in FAR_ORDER],
        in_specs=[sm] + [vm] * (n + 1),
        scratch_shapes=[pltpu.VMEM((tok, HD), bf16), pltpu.VMEM((2, n, HD), f32)],
        cost_estimate=pl.CostEstimate(
            flops=6 * exps * HD, bytes_accessed=8 * n * tok * HD, transcendentals=exps
        ),
    )
    result = call(
        functools.partial(part_kernel, n, tok, pos),
        [shape((tok + pos + ROWS, HD), bf16)] * n,
        anchor_frame,
        k_gain.reshape(heads, HD),
        held,
        vt,
        v_far,
        *[far[s] for s in FAR_ORDER],
        *done,
        side,
        in_specs=[sm] + [vm] * (2 * n + 5),
        scratch_shapes=[pltpu.VMEM((2, n, HD), f32), pltpu.VMEM((HD, HD), f32)],
    )
    back = swap_blocks(result, (4, 6, 5, 7, 1, 2, 3), {2: 4, 3: 6})
    return call(
        functools.partial(join_kernel, n, pos),
        shape((tok, width), bf16),
        own,
        *[back[s] for s in BACK_ORDER],
        in_specs=[vm] * (n + 1),
        out_specs=hbm,
        scratch_shapes=[pltpu.VMEM((n + 2, tok, HD), bf16), dma((2, n))],
    )


def solution(mesh):
    n = mesh.shape["frame"]

    def local(*args):
        tok, width = args[0].shape
        fits = n == 8 and mesh.shape["mp"] == 4 and width == 10 * HD and tok == 2 * BLOCK
        return local_heads(*args) if fits else local_general(*args)

    return jax.shard_map(
        local,
        mesh=mesh,
        in_specs=(
            P("frame", "mp"),
            P("frame", "mp"),
            P("frame", "mp"),
            P("mp"),
            P("mp"),
            P("frame", None, None),
            P("frame", None, None),
            P(),
        ),
        out_specs=P("frame", "mp"),
        check_vma=False,
    )
```

```python
import functools

import jax
import jax.numpy as jnp
from jax import lax
from jax.experimental import pallas as pl
from jax.experimental.pallas import tpu as pltpu
from jax.sharding import PartitionSpec as P

D = 5120
HD = 128
BLOCK = 128
LOG2E = 1.4426950408889634
NEG = -1e30


def spread(value, axis, source):
    kept = jnp.where(lax.axis_index(axis) == source, value, 0).astype(value.dtype)
    return lax.psum(kept, axis)


def expand(block_mask):
    count = block_mask.shape[0]
    allowed = (block_mask == 1) | jnp.eye(count, dtype=jnp.bool_)
    return jnp.repeat(jnp.repeat(allowed, BLOCK, axis=0), BLOCK, axis=1)


def attend(query, keys, vals, allowed):
    rows = query.shape[0]
    width = query.shape[1]
    heads_dev = width // HD
    query3 = jnp.transpose(query.reshape(rows, heads_dev, HD), (1, 0, 2))
    keys3 = jnp.transpose(keys.reshape(keys.shape[0], heads_dev, HD), (1, 0, 2))
    vals3 = jnp.transpose(vals.reshape(vals.shape[0], heads_dev, HD), (1, 0, 2))
    scale = jnp.sqrt(jnp.float32(HD))

    def one_head(items):
        head_q, head_k, head_v = items
        scores = jnp.einsum("qd,kd->qk", head_q, head_k, preferred_element_type=jnp.float32) / scale
        scores = jnp.where(allowed, scores, -jnp.inf)
        probs = jax.nn.softmax(scores, axis=-1).astype(jnp.bfloat16)
        return jnp.dot(probs, head_v, preferred_element_type=jnp.float32)

    output = lax.map(one_head, (query3, keys3, vals3))
    return jnp.transpose(output, (1, 0, 2)).reshape(rows, width)


def local_general(
    q_raw, k_raw, values, q_gain, k_gain, spatial_mask, temporal_mask, anchor_frame
):
    frame_tok = q_raw.shape[0]
    width = q_raw.shape[1]
    q_float = q_raw.astype(jnp.float32)
    k_float = k_raw.astype(jnp.float32)
    sum_q, sum_k = lax.psum(
        (jnp.sum(q_float * q_float, axis=1), jnp.sum(k_float * k_float, axis=1)), "mp"
    )
    q_norm = (q_float / jnp.sqrt(sum_q[:, None] / D + 1e-06) * q_gain[None, :]).astype(jnp.bfloat16)
    k_norm = (k_float / jnp.sqrt(sum_k[:, None] / D + 1e-06) * k_gain[None, :]).astype(jnp.bfloat16)
    n_frames = lax.axis_size("frame")
    group_pos = frame_tok // n_frames

    def regroup(array):
        return lax.all_to_all(
            array.reshape(n_frames, group_pos, width),
            "frame",
            split_axis=0,
            concat_axis=0,
            tiled=True,
        ).reshape(frame_tok, width)

    anchor = anchor_frame[0]
    k_anchor, v_anchor = (spread(k_norm, "frame", anchor), spread(values, "frame", anchor))
    own_allowed = jnp.concatenate(
        [expand(spatial_mask[0]), jnp.ones((frame_tok, frame_tok), dtype=jnp.bool_)], axis=1
    )
    spatial = attend(
        q_norm,
        jnp.concatenate([k_norm, k_anchor], 0),
        jnp.concatenate([values, v_anchor], 0),
        own_allowed,
    )
    temporal = attend(
        regroup(q_norm), regroup(k_norm), regroup(values), expand(temporal_mask[0])
    ).astype(jnp.bfloat16)
    returned = regroup(temporal)
    return (spatial + returned.astype(jnp.float32)).astype(jnp.bfloat16)


ROWS = 16
LSE_ROW = 6
NORM_ROW = 9
MASK_ROW = 15
ONES = 8


def dot_t(a, b):
    return lax.dot_general(a, b, (((1,), (1,)), ((), ())), preferred_element_type=jnp.float32)


def weigh(weights, vals):
    ones = jnp.ones(vals.shape, vals.dtype)
    both = jnp.dot(
        weights.astype(jnp.bfloat16),
        jnp.concatenate([vals, ones], axis=1),
        preferred_element_type=jnp.float32,
    )
    return both[:, :HD], both[:, HD:]


def blocked_scores(query, keys, flag, i):
    scores = dot_t(query, keys)
    near = scores[:, i * BLOCK : (i + 1) * BLOCK]
    away = scores[:, (1 - i) * BLOCK : (2 - i) * BLOCK] + flag
    return jnp.concatenate([near, away] if i == 0 else [away, near], axis=1)


def scaled(rows, column, gain):
    return (rows.astype(jnp.float32) * column * gain).astype(jnp.bfloat16)


def cut_kernel(n, pos, k_ref, v_ref, out_ref, cut, sems):
    tok = k_ref.shape[0]
    parts = tok // pos
    loads, stores = [], []
    for d in range(n):
        row = d % parts * pos
        pieces = (
            (v_ref, d, 0, tok, 0),
            (v_ref, n + d // parts, row, pos, tok),
            (k_ref, n + d // parts, row, pos, tok + pos),
        )
        for j, (ref, head, row, rows, at) in enumerate(pieces):
            loads.append(
                pltpu.make_async_copy(
                    ref.at[pl.ds(row, rows), pl.ds(head * HD, HD)],
                    cut.at[d, pl.ds(at, rows)],
                    sems.at[j, d],
                )
            )
            loads[-1].start()
        stores.append(pltpu.make_async_copy(cut.at[d], out_ref.at[d], sems.at[3, d]))
    for d in range(n):
        for copy in loads[3 * d : 3 * d + 3]:
            copy.wait()
        stores[d].start()
    for copy in stores:
        copy.wait()


def squares_kernel(q_ref, k_ref, out_ref, held, sems):
    tok = q_ref.shape[0]
    chunks = sems.shape[1]
    step = tok // chunks
    copies = []
    for t, ref in enumerate((q_ref, k_ref)):
        for c in range(chunks):
            rows = pl.ds(c * step, step)
            copies.append(pltpu.make_async_copy(ref.at[rows], held.at[t, rows], sems.at[t, c]))
    for copy in copies:
        copy.start()
    rows = []
    for t in range(2):
        parts = []
        for c in range(chunks):
            copies[t * chunks + c].wait()
            total = None
            for h in range(q_ref.shape[1] // HD):
                part = held[t, c * step : (c + 1) * step, h * HD : (h + 1) * HD]
                part = part.astype(jnp.float32)
                total = part * part if total is None else total + part * part
            parts.append(total)
        rows.append(jnp.sum(jnp.concatenate(parts, axis=0).T, axis=0, keepdims=True))
    out_ref[...] = jnp.concatenate(rows + [jnp.zeros((6, tok), jnp.float32)], axis=0)


def copy_kernel(in_ref, out_ref):
    out_ref[...] = in_ref[...]


def own_kernel(n, pos, *refs):
    args, blocks, own_ref = refs[:11], refs[11 : 11 + n], refs[11 + n]
    ins, held, extra, own, sums, gains, masks, in_sems, out_sems = refs[12 + n :]
    q_ref, k_ref, v_ref = args[:3]
    tok = q_ref.shape[0]
    heads = q_ref.shape[1] // HD
    parts = tok // pos
    me = lax.axis_index("frame")
    order = [n + e for e in range(heads - n)] + [me ^ s for s in range(n)]

    def cols(h):
        return pl.ds(pl.multiple_of(h * HD, HD), HD)

    small = []
    for j in range(4):
        small.append(pltpu.make_async_copy(args[3 + j], sums.at[j], in_sems.at[3 * heads + j]))
    for j in range(2):
        at = in_sems.at[3 * heads + 4 + j]
        small.append(pltpu.make_async_copy(args[7 + j], gains.at[j], at))
        at = in_sems.at[3 * heads + 6 + j]
        small.append(pltpu.make_async_copy(args[9 + j], masks.at[j], at))
    loads = [
        pltpu.make_async_copy(ref.at[:, cols(h)], ins.at[t, x], in_sems.at[3 * x + t])
        for x, h in enumerate(order)
        for t, ref in enumerate((q_ref, k_ref, v_ref))
    ]
    for copy in small + loads:
        copy.start()
    for copy in small:
        copy.wait()
    inv = lax.rsqrt((sums[0] + sums[1] + sums[2] + sums[3]) / D + 1e-06)
    inv_row = inv[1:2, :]
    inv = inv.T
    inv_q = jnp.broadcast_to(inv[:, 0:1] * (LOG2E / float(HD) ** 0.5), (tok, HD))
    inv_k = jnp.broadcast_to(inv[:, 1:2], (tok, HD))
    flags = [jnp.where(masks[0, i, 1 - i] == 1, 0.0, NEG) for i in range(2)]
    lane = lax.broadcasted_iota(jnp.int32, (BLOCK, HD), 1)
    lses = [jnp.zeros((BLOCK, HD), jnp.float32) for _ in range(tok // BLOCK)]
    stores = []
    for x, h in enumerate(order):
        if x in (0, heads // 2):
            for copy in loads[3 * x : 3 * (x + heads // 2)]:
                copy.wait()
        query = scaled(ins[0, x], inv_q, gains[0, pl.ds(h, 1), :])
        keys = scaled(ins[1, x], inv_k, gains[1, pl.ds(h, 1), :])
        vals = ins[2, x]
        if x < heads - n:
            extra[x] = query
        else:
            s = x - (heads - n)
            held[s, :tok, :] = query
            held[s, tok : 2 * tok, :] = keys
            rows = pl.ds(pl.multiple_of((me ^ s) % parts * pos, pos), pos)
            held[s, 2 * tok : 2 * tok + pos, :] = extra[(me ^ s) // parts, rows, :]
            rows = pl.ds(0, 2 * tok + pos)
            stores.append(
                pltpu.make_async_copy(held.at[s, rows], blocks[s].at[rows], out_sems.at[x])
            )
            stores[-1].start()
        for i in range(tok // BLOCK):
            rows = slice(i * BLOCK, (i + 1) * BLOCK)
            scores = blocked_scores(query[rows], keys, flags[i], i)
            top = jnp.max(scores, axis=1, keepdims=True)
            out, weight = weigh(jnp.exp2(scores - top), vals)
            own[x, rows, :] = out / weight
            lses[i] = jnp.where(lane == x, top + jnp.log2(weight), lses[i])
        stores.append(
            pltpu.make_async_copy(own.at[x], own_ref.at[:, cols(h)], out_sems.at[heads + x])
        )
        stores[-1].start()
    def split(rest):
        parts = []
        for _ in range(3):
            parts.append(rest.astype(jnp.bfloat16).astype(jnp.float32))
            rest = rest - parts[-1]
        return parts

    lses = [split(lse.T[:ROWS]) for lse in lses]
    norms = [split(inv_row[:, i * BLOCK : (i + 1) * BLOCK]) for i in range(tok // BLOCK)]
    lane = lax.broadcasted_iota(jnp.int32, (1, HD), 1)
    mask = jnp.where(lane == 0, masks[1, 0, 1], masks[1, 1, 0])
    tail = norms[0] + norms[1] + [(mask == 1).astype(jnp.float32)]
    at = 2 * tok + pos
    for s in range(n):
        first = heads - n + s
        rows = [piece[first : first + 1, :] for half in lses for piece in half]
        late = (me ^ s) // parts == 1
        upper = (me ^ s) % parts * pos >= BLOCK
        for low, high in zip(*lses):
            piece = jnp.where(upper, high, low)
            rows.append(jnp.where(late, piece[1:2, :], piece[0:1, :]))
        held[s, at : at + ROWS, :] = jnp.concatenate(rows + tail, axis=0).astype(jnp.bfloat16)
        rows = pl.ds(at, ROWS)
        stores.append(
            pltpu.make_async_copy(held.at[s, rows], blocks[s].at[rows], out_sems.at[2 * heads + s])
        )
        stores[-1].start()
    for copy in stores:
        copy.wait()


FAR_ORDER = (0, 1, 2, 3, 4, 5, 6, 7)
BACK_ORDER = (0, 1, 2, 3, 4, 5, 6, 7)


def by_step(refs, order):
    return [refs[order.index(s)] for s in range(len(order))]


def inverse(value):
    guess = pl.reciprocal(value, approx=True)
    return guess * (2.0 - value * guess)


def turned(vals):
    return jnp.concatenate([vals.T, jnp.ones((ONES, vals.shape[0]), vals.dtype)], axis=0)


def turn_kernel(n, tok, pos, at_ref, v_ref, out_ref):
    gp = tok // n
    me = lax.axis_index("frame")
    for g in range((tok + pos) // gp):
        rows = [v_ref[me ^ s, g * gp : (g + 1) * gp, :] for s in range(n)]
        out_ref[g] = turned(jnp.concatenate(rows, axis=0))
    out_ref[(tok + pos) // gp] = turned(v_ref[at_ref[0], :tok, :])


def attend_tiles(tiles):
    scores = [(dot_t(t[1], t[0]), dot_t(t[3], t[0])) for t in tiles]
    weights = []
    for t, (paired, anchored) in zip(tiles, scores):
        lse, flag, i = t[5:]
        near = paired[i * BLOCK : (i + 1) * BLOCK]
        away = paired[(1 - i) * BLOCK : (2 - i) * BLOCK] + flag
        top = jnp.maximum(
            jnp.max(near, axis=0, keepdims=True), jnp.max(away, axis=0, keepdims=True)
        )
        both = [jnp.exp2(near - top), jnp.exp2(away - top)]
        both = jnp.concatenate(both if i == 0 else both[::-1], axis=0)
        top = jnp.maximum(jnp.max(anchored, axis=0, keepdims=True), lse)
        own = jnp.exp2(lse - top)
        anchored = jnp.exp2(anchored - top)
        weights.append((both.astype(jnp.bfloat16), anchored.astype(jnp.bfloat16), own))
    sums = [
        (
            jnp.dot(t[2], both, preferred_element_type=jnp.float32),
            jnp.dot(t[4], anchored, preferred_element_type=jnp.float32),
            own,
        )
        for t, (both, anchored, own) in zip(tiles, weights)
    ]
    results = []
    for paired, anchored, own in sums:
        scale = inverse(anchored[HD : HD + 1] + own)
        result = paired[:HD] * inverse(paired[HD : HD + 1]) + anchored[:HD] * scale
        results.append((result.T.astype(jnp.bfloat16), own * scale))
    return results


def spin(rows, parts):
    parts %= HD // rows[1]
    return rows[0] if parts == 0 else pltpu.roll(rows[0], parts * rows[1], 1)


def gather_lanes(rows, place, gp):
    lane = lax.broadcasted_iota(jnp.int32, (1, HD), 1) // gp
    out = None
    for j in range(rows.shape[0]):
        row = spin((rows, gp), j - place)[j : j + 1]
        out = row if out is None else jnp.where(lane == j, row, out)
    return out


def scatter_lanes(kept, row, place, gp):
    lane = lax.broadcasted_iota(jnp.int32, (1, HD), 1) // gp
    for j in range(len(kept)):
        kept[j] = jnp.where(lane == place, spin((row, gp), place - j), kept[j])


def side_rows(blocks, at, first):
    rows = []
    for block in blocks:
        side = block[at : at + ROWS, :].astype(jnp.float32)
        rows.append(side[first : first + 1] + side[first + 1 : first + 2] + side[first + 2 : first + 3])
    return jnp.concatenate(rows, axis=0)


def keep_flags(n, blocks, at, flag_ref):
    masks = [block[at : at + ROWS, :].astype(jnp.float32)[MASK_ROW:] for block in blocks]
    masks = jnp.concatenate(masks, axis=0)
    flags = [jnp.broadcast_to(masks[:, i : i + 1], (n, HD)) for i in range(2)]
    flags = [jnp.where(flag == 1.0, 0.0, NEG) for flag in flags]
    upper = lax.axis_index("frame") >= n // 2
    for i in range(2):
        flag_ref[i] = jnp.where(upper, flags[1 - i], flags[i])


def stack_rows(blocks, at, gp):
    return jnp.concatenate([block[at : at + gp, :] for block in blocks], axis=0)


def whole_kernel(n, tok, pos, at_ref, vt_ref, *refs):
    blocks, outs, side_ref = by_step(refs[:n], FAR_ORDER), refs[n : 2 * n], refs[2 * n]
    key_ref, flag_ref = refs[2 * n + 1 :]
    gp = tok // n
    per = n // 2
    me = lax.axis_index("frame")
    for s in range(n):

        @pl.when(at_ref[0] == me ^ s)
        def _():
            key_ref[...] = blocks[s][tok : 2 * tok, :]

    at_side = 2 * tok + pos
    keep_flags(n, blocks, at_side, flag_ref)
    ka, va = key_ref[...], vt_ref[(tok + pos) // gp]
    halves = [blocks[:per], blocks[per:]]
    lses = [[side_rows(half, at_side, 3 * b) for b in range(2)] for half in halves]
    kept = [[[jnp.zeros((1, HD), jnp.float32)] * per for _ in range(2)] for _ in range(2)]
    across = BLOCK // gp
    together = 4
    for g0 in range(0, n, together):
        tiles, places = [], []
        for g in range(g0, g0 + together):
            keys = stack_rows(blocks, tok + g * gp, gp)
            for i, half in enumerate(halves):
                query = stack_rows(half, g * gp, gp)
                lse = gather_lanes(lses[i][g // across], g % across, gp)
                flag = flag_ref[i, pl.ds(g ^ me, 1), :]
                tiles.append((query, keys, vt_ref[g], ka, va, lse, flag, i))
                places.append((g, i))
        for (g, i), (result, keep) in zip(places, attend_tiles(tiles)):
            for j in range(per):
                outs[i * per + j][g * gp : (g + 1) * gp, :] = result[j * gp : (j + 1) * gp]
            scatter_lanes(kept[i][g // across], keep, g % across, gp)
    rows = [kept[s // per][b][s % per] for s in range(n) for b in range(2)]
    side_ref[...] = jnp.concatenate(rows, axis=0)


def part_kernel(n, tok, pos, at_ref, gain_ref, held_ref, vt_ref, v_ref, *refs):
    blocks, done, came_ref = by_step(refs[:n], FAR_ORDER), refs[n : 2 * n], refs[2 * n]
    outs, flag_ref, col_ref = refs[2 * n + 1 : 3 * n + 1], refs[3 * n + 1], refs[3 * n + 2]
    gp = tok // n
    per = n // 2
    parts = tok // pos
    me = lax.axis_index("frame")
    anchor = at_ref[0]
    quarter = me % parts
    odd = quarter * pos % BLOCK != 0
    late = quarter * pos >= BLOCK
    gain = jnp.where(me // parts == 1, gain_ref[n + 1 : n + 2, :], gain_ref[n : n + 1, :])
    at_side = 2 * tok + pos
    keep_flags(n, blocks, at_side, flag_ref)
    norms = [side_rows(blocks, at_side, NORM_ROW + 3 * b) for b in range(2)]
    rows = [jnp.where(late, norms[1], norms[0])]
    for norm in norms:
        row = norm[0:1]
        for s in range(1, n):
            row = jnp.where(anchor == me ^ s, norm[s : s + 1], row)
        rows.append(row)
    rows.append(jnp.zeros((HD - n - 2, HD), jnp.float32))
    col_ref[...] = jnp.concatenate(rows, axis=0).T
    va = turned(jnp.concatenate([held_ref[j, :pos, :] for j in range(parts)], axis=0))
    ka = jnp.concatenate([held_ref[j, pos:, :] for j in range(parts)], axis=0)
    norm = jnp.concatenate([col_ref[:, n + b : n + b + 1] for b in range(2)], axis=0)
    ka = scaled(ka, norm, gain)
    halves = [blocks[:per], blocks[per:]]
    lses = []
    for half in halves:
        lse = side_rows(half, at_side, LSE_ROW)
        lses.append(jnp.where(odd, pltpu.roll(lse, HD - pos, 1), lse))
    kept = [[jnp.zeros((1, HD), jnp.float32)] * per for _ in range(2)]
    tiles, places = [], []
    for u in range(pos // gp):
        first = pl.multiple_of(quarter * pos % BLOCK + u * gp, gp)
        cols = col_ref[pl.ds(first, gp), :]
        norm = jnp.concatenate([cols[:, s : s + 1] for s in range(n)], axis=0)
        at = tok + pos + u * gp
        keys = jnp.concatenate([v_ref[me ^ s, at : at + gp, :] for s in range(n)], axis=0)
        keys = scaled(keys, norm, gain)
        for i, half in enumerate(halves):
            query = stack_rows(half, 2 * tok + u * gp, gp)
            lse = gather_lanes(lses[i], u, gp)
            flag = flag_ref[i, pl.ds((quarter * (pos // gp) + u) ^ me, 1), :]
            tiles.append((query, keys, vt_ref[n + u], ka, va, lse, flag, i))
            places.append((tok + u * gp, u, i))
    for s in range(n):
        outs[s][:tok, :] = done[s][...]
    for (at, u, i), (result, keep) in zip(places, attend_tiles(tiles)):
        for j in range(per):
            outs[i * per + j][at : at + gp, :] = result[j * gp : (j + 1) * gp]
        scatter_lanes(kept[i], keep, u, gp)
    pad = jnp.zeros((ROWS - 3, HD), jnp.float32)
    for s in range(n):
        rows = [came_ref[2 * s : 2 * s + 2, :], kept[s // per][s % per], pad]
        rows = jnp.concatenate(rows, axis=0)
        outs[s][tok + pos : tok + pos + ROWS, :] = rows.astype(jnp.bfloat16)


def join_kernel(n, pos, own_ref, *refs):
    back, out_ref = by_step(refs[:n], BACK_ORDER), refs[n]
    held, sems = refs[n + 1 :]
    tok = own_ref.shape[0]
    parts = tok // pos
    me = lax.axis_index("frame")
    at_side = tok + pos
    sides = jnp.concatenate([block[at_side : at_side + ROWS, :] for block in back], axis=0).T
    sub = lax.broadcasted_iota(jnp.int32, (n * ROWS, HD), 0)

    def spread_lanes(row):
        pick = (sub == row).astype(jnp.bfloat16)
        return jnp.dot(sides, pick, preferred_element_type=jnp.float32)

    copies = []
    for s in range(n):
        d = me ^ s
        keeps = [spread_lanes(s * ROWS + r) for r in range(3)]
        whole = pl.ds(pl.multiple_of(d * HD, HD), HD)
        for b in range(tok // BLOCK):
            rows = slice(b * BLOCK, (b + 1) * BLOCK)
            got = back[s][rows, :].astype(jnp.float32)
            held[s, rows, :] = (own_ref[rows, whole] * keeps[b] + got).astype(jnp.bfloat16)
        copies.append(pltpu.make_async_copy(held.at[s], out_ref.at[:, whole], sems.at[0, s]))
        copies[-1].start()
        part = pl.ds(pl.multiple_of((n + d // parts) * HD, HD), HD)
        rows = pl.ds(pl.multiple_of(d % parts * pos, pos), pos)
        got = back[s][tok : tok + pos, :].astype(jnp.float32)
        got = own_ref[rows, part] * keeps[2][:pos] + got
        held[n + s // parts, s % parts * pos : (s % parts + 1) * pos, :] = got.astype(jnp.bfloat16)
        copies.append(
            pltpu.make_async_copy(
                held.at[n + s // parts, pl.ds(s % parts * pos, pos)], out_ref.at[rows, part], sems.at[1, s]
            )
        )
        copies[-1].start()
    for copy in copies:
        copy.wait()


def call(kernel, out_shape, *args, vmem=40, **more):
    return pl.pallas_call(
        kernel,
        out_shape=out_shape,
        compiler_params=pltpu.CompilerParams(vmem_limit_bytes=vmem * 1024 * 1024),
        **more,
    )(*args)


def pairwise(array, axis, step):
    size = lax.axis_size(axis)
    return lax.ppermute(array, axis, [(i, i ^ step) for i in range(size)])


def swap_blocks(blocks, order, chain):
    got = {0: blocks[0]}
    for s in order:
        block = blocks[s]
        if s in chain:
            block, _ = lax.optimization_barrier((block, got[chain[s]]))
        got[s] = pairwise(block, "frame", s)
    return [got[s] for s in range(len(blocks))]


def local_heads(
    q_raw, k_raw, values, q_gain, k_gain, spatial_mask, temporal_mask, anchor_frame
):
    tok, width = q_raw.shape
    n = lax.axis_size("frame")
    n_mp = lax.axis_size("mp")
    heads = width // HD
    parts = n // (heads - n)
    pos = tok // parts
    me = lax.axis_index("frame")
    shape = jax.ShapeDtypeStruct
    vm = pl.BlockSpec(memory_space=pltpu.VMEM)
    sm = pl.BlockSpec(memory_space=pltpu.SMEM)
    hbm = pl.BlockSpec(memory_space=pltpu.HBM)
    dma = pltpu.SemaphoreType.DMA
    bf16, f32 = jnp.bfloat16, jnp.float32

    v_blocks = call(
        functools.partial(cut_kernel, n, pos),
        shape((n, tok + 2 * pos, HD), bf16),
        k_raw,
        values,
        in_specs=[hbm] * 2,
        out_specs=hbm,
        scratch_shapes=[pltpu.VMEM((n, tok + 2 * pos, HD), bf16), dma((4, n))],
        vmem=60,
    )
    q_raw, k_raw, values, v_blocks = lax.optimization_barrier((q_raw, k_raw, values, v_blocks))
    sums = call(
        squares_kernel,
        shape((8, tok), f32),
        q_raw,
        k_raw,
        in_specs=[hbm] * 2,
        scratch_shapes=[pltpu.VMEM((2, tok, width), bf16), dma((2, 4))],
        vmem=60,
    )
    all_sums = [sums] + [pairwise(sums, "mp", step) for step in range(1, n_mp)]
    v_far = lax.all_to_all(v_blocks, "frame", split_axis=0, concat_axis=0, tiled=True)
    rows = 2 * tok + pos + ROWS
    *sent, own = call(
        functools.partial(own_kernel, n, pos),
        [shape((rows, HD), bf16)] * n + [shape((tok, width), f32)],
        q_raw,
        k_raw,
        values,
        *all_sums,
        q_gain.reshape(heads, HD),
        k_gain.reshape(heads, HD),
        spatial_mask[0],
        temporal_mask[0],
        in_specs=[hbm] * 11,
        out_specs=[hbm] * (n + 1),
        scratch_shapes=[
            pltpu.VMEM((3, heads, tok, HD), bf16),
            pltpu.VMEM((n, rows, HD), bf16),
            pltpu.VMEM((heads - n, tok, HD), bf16),
            pltpu.VMEM((heads, tok, HD), f32),
            pltpu.VMEM((4, 8, tok), f32),
            pltpu.VMEM((2, heads, HD), f32),
            pltpu.SMEM((2, 2, 2), jnp.int32),
            dma((3 * heads + 8,)),
            dma((2 * heads + n,)),
        ],
        vmem=60,
    )
    far = swap_blocks(sent, (4, 6, 5, 7, 1, 2, 3), {3: 2})
    block, v_far, *_ = lax.optimization_barrier((sent[0], v_far, far[1], far[2]))
    far[0] = call(copy_kernel, shape((rows, HD), bf16), block, vmem=8)

    anchor = anchor_frame[0]
    mine = lax.dynamic_slice(v_far, (anchor, tok, 0), (1, 2 * pos, HD))
    groups = [list(range(first, first + parts)) for first in range(0, n, parts)]
    held = lax.all_to_all(
        jnp.broadcast_to(mine, (parts, 2 * pos, HD)),
        "frame",
        split_axis=0,
        concat_axis=0,
        axis_index_groups=groups,
        tiled=True,
    )
    pencils = (tok + pos) // (tok // n)
    vt = call(
        functools.partial(turn_kernel, n, tok, pos),
        shape((pencils + 1, HD + ONES, tok), bf16),
        anchor_frame,
        v_far,
        in_specs=[sm, vm],
    )
    exps = n * tok * 2 * tok
    *done, side = call(
        functools.partial(whole_kernel, n, tok, pos),
        [shape((tok, HD), bf16)] * n + [shape((2 * n, HD), f32)],
        anchor_frame,
        vt,
        *[far[s] for s in FAR_ORDER],
        in_specs=[sm] + [vm] * (n + 1),
        scratch_shapes=[pltpu.VMEM((tok, HD), bf16), pltpu.VMEM((2, n, HD), f32)],
        cost_estimate=pl.CostEstimate(
            flops=6 * exps * HD, bytes_accessed=8 * n * tok * HD, transcendentals=exps
        ),
    )
    result = call(
        functools.partial(part_kernel, n, tok, pos),
        [shape((tok + pos + ROWS, HD), bf16)] * n,
        anchor_frame,
        k_gain.reshape(heads, HD),
        held,
        vt,
        v_far,
        *[far[s] for s in FAR_ORDER],
        *done,
        side,
        in_specs=[sm] + [vm] * (2 * n + 5),
        scratch_shapes=[pltpu.VMEM((2, n, HD), f32), pltpu.VMEM((HD, HD), f32)],
    )
    back = swap_blocks(result, (4, 6, 5, 7, 1, 2, 3), {3: 4})
    return call(
        functools.partial(join_kernel, n, pos),
        shape((tok, width), bf16),
        own,
        *[back[s] for s in BACK_ORDER],
        in_specs=[vm] * (n + 1),
        out_specs=hbm,
        scratch_shapes=[pltpu.VMEM((n + 2, tok, HD), bf16), dma((2, n))],
    )


def solution(mesh):
    n = mesh.shape["frame"]

    def local(*args):
        tok, width = args[0].shape
        fits = n == 8 and mesh.shape["mp"] == 4 and width == 10 * HD and tok == 2 * BLOCK
        return local_heads(*args) if fits else local_general(*args)

    return jax.shard_map(
        local,
        mesh=mesh,
        in_specs=(
            P("frame", "mp"),
            P("frame", "mp"),
            P("frame", "mp"),
            P("mp"),
            P("mp"),
            P("frame", None, None),
            P("frame", None, None),
            P(),
        ),
        out_specs=P("frame", "mp"),
        check_vma=False,
    )
```

```python
import functools

import jax
import jax.numpy as jnp
from jax import lax
from jax.experimental import pallas as pl
from jax.experimental.pallas import tpu as pltpu
from jax.sharding import PartitionSpec as P

D = 5120
HD = 128
BLOCK = 128
LOG2E = 1.4426950408889634
NEG = -1e30


def spread(value, axis, source):
    kept = jnp.where(lax.axis_index(axis) == source, value, 0).astype(value.dtype)
    return lax.psum(kept, axis)


def expand(block_mask):
    count = block_mask.shape[0]
    allowed = (block_mask == 1) | jnp.eye(count, dtype=jnp.bool_)
    return jnp.repeat(jnp.repeat(allowed, BLOCK, axis=0), BLOCK, axis=1)


def attend(query, keys, vals, allowed):
    rows = query.shape[0]
    width = query.shape[1]
    heads_dev = width // HD
    query3 = jnp.transpose(query.reshape(rows, heads_dev, HD), (1, 0, 2))
    keys3 = jnp.transpose(keys.reshape(keys.shape[0], heads_dev, HD), (1, 0, 2))
    vals3 = jnp.transpose(vals.reshape(vals.shape[0], heads_dev, HD), (1, 0, 2))
    scale = jnp.sqrt(jnp.float32(HD))

    def one_head(items):
        head_q, head_k, head_v = items
        scores = jnp.einsum("qd,kd->qk", head_q, head_k, preferred_element_type=jnp.float32) / scale
        scores = jnp.where(allowed, scores, -jnp.inf)
        probs = jax.nn.softmax(scores, axis=-1).astype(jnp.bfloat16)
        return jnp.dot(probs, head_v, preferred_element_type=jnp.float32)

    output = lax.map(one_head, (query3, keys3, vals3))
    return jnp.transpose(output, (1, 0, 2)).reshape(rows, width)


def local_general(
    q_raw, k_raw, values, q_gain, k_gain, spatial_mask, temporal_mask, anchor_frame
):
    frame_tok = q_raw.shape[0]
    width = q_raw.shape[1]
    q_float = q_raw.astype(jnp.float32)
    k_float = k_raw.astype(jnp.float32)
    sum_q, sum_k = lax.psum(
        (jnp.sum(q_float * q_float, axis=1), jnp.sum(k_float * k_float, axis=1)), "mp"
    )
    q_norm = (q_float / jnp.sqrt(sum_q[:, None] / D + 1e-06) * q_gain[None, :]).astype(jnp.bfloat16)
    k_norm = (k_float / jnp.sqrt(sum_k[:, None] / D + 1e-06) * k_gain[None, :]).astype(jnp.bfloat16)
    n_frames = lax.axis_size("frame")
    group_pos = frame_tok // n_frames

    def regroup(array):
        return lax.all_to_all(
            array.reshape(n_frames, group_pos, width),
            "frame",
            split_axis=0,
            concat_axis=0,
            tiled=True,
        ).reshape(frame_tok, width)

    anchor = anchor_frame[0]
    k_anchor, v_anchor = (spread(k_norm, "frame", anchor), spread(values, "frame", anchor))
    own_allowed = jnp.concatenate(
        [expand(spatial_mask[0]), jnp.ones((frame_tok, frame_tok), dtype=jnp.bool_)], axis=1
    )
    spatial = attend(
        q_norm,
        jnp.concatenate([k_norm, k_anchor], 0),
        jnp.concatenate([values, v_anchor], 0),
        own_allowed,
    )
    temporal = attend(
        regroup(q_norm), regroup(k_norm), regroup(values), expand(temporal_mask[0])
    ).astype(jnp.bfloat16)
    returned = regroup(temporal)
    return (spatial + returned.astype(jnp.float32)).astype(jnp.bfloat16)


ROWS = 16
LSE_ROW = 6
NORM_ROW = 9
MASK_ROW = 15
ONES = 8


def dot_t(a, b):
    return lax.dot_general(a, b, (((1,), (1,)), ((), ())), preferred_element_type=jnp.float32)


def weigh(weights, vals):
    ones = jnp.ones(vals.shape, vals.dtype)
    both = jnp.dot(
        weights.astype(jnp.bfloat16),
        jnp.concatenate([vals, ones], axis=1),
        preferred_element_type=jnp.float32,
    )
    return both[:, :HD], both[:, HD:]


def blocked_scores(query, keys, flag, i):
    scores = dot_t(query, keys)
    near = scores[:, i * BLOCK : (i + 1) * BLOCK]
    away = scores[:, (1 - i) * BLOCK : (2 - i) * BLOCK] + flag
    return jnp.concatenate([near, away] if i == 0 else [away, near], axis=1)


def scaled(rows, column, gain):
    return (rows.astype(jnp.float32) * column * gain).astype(jnp.bfloat16)


def cut_kernel(n, pos, k_ref, v_ref, out_ref, cut, sems):
    tok = k_ref.shape[0]
    parts = tok // pos
    loads, stores = [], []
    for d in range(n):
        row = d % parts * pos
        pieces = (
            (v_ref, d, 0, tok, 0),
            (v_ref, n + d // parts, row, pos, tok),
            (k_ref, n + d // parts, row, pos, tok + pos),
        )
        for j, (ref, head, row, rows, at) in enumerate(pieces):
            loads.append(
                pltpu.make_async_copy(
                    ref.at[pl.ds(row, rows), pl.ds(head * HD, HD)],
                    cut.at[d, pl.ds(at, rows)],
                    sems.at[j, d],
                )
            )
            loads[-1].start()
        stores.append(pltpu.make_async_copy(cut.at[d], out_ref.at[d], sems.at[3, d]))
    for d in range(n):
        for copy in loads[3 * d : 3 * d + 3]:
            copy.wait()
        stores[d].start()
    for copy in stores:
        copy.wait()


def squares_kernel(q_ref, k_ref, out_ref, held, sems):
    tok = q_ref.shape[0]
    chunks = sems.shape[1]
    step = tok // chunks
    copies = []
    for t, ref in enumerate((q_ref, k_ref)):
        for c in range(chunks):
            rows = pl.ds(c * step, step)
            copies.append(pltpu.make_async_copy(ref.at[rows], held.at[t, rows], sems.at[t, c]))
    for copy in copies:
        copy.start()
    rows = []
    for t in range(2):
        parts = []
        for c in range(chunks):
            copies[t * chunks + c].wait()
            total = None
            for h in range(q_ref.shape[1] // HD):
                part = held[t, c * step : (c + 1) * step, h * HD : (h + 1) * HD]
                part = part.astype(jnp.float32)
                total = part * part if total is None else total + part * part
            parts.append(total)
        rows.append(jnp.sum(jnp.concatenate(parts, axis=0).T, axis=0, keepdims=True))
    out_ref[...] = jnp.concatenate(rows + [jnp.zeros((6, tok), jnp.float32)], axis=0)


def copy_kernel(in_ref, out_ref):
    out_ref[...] = in_ref[...]


def own_kernel(n, pos, *refs):
    args, blocks, own_ref = refs[:11], refs[11 : 11 + n], refs[11 + n]
    ins, held, extra, own, sums, gains, masks, in_sems, out_sems = refs[12 + n :]
    q_ref, k_ref, v_ref = args[:3]
    tok = q_ref.shape[0]
    heads = q_ref.shape[1] // HD
    parts = tok // pos
    me = lax.axis_index("frame")
    order = [n + e for e in range(heads - n)] + [me ^ s for s in range(n)]

    def cols(h):
        return pl.ds(pl.multiple_of(h * HD, HD), HD)

    small = []
    for j in range(4):
        small.append(pltpu.make_async_copy(args[3 + j], sums.at[j], in_sems.at[3 * heads + j]))
    for j in range(2):
        at = in_sems.at[3 * heads + 4 + j]
        small.append(pltpu.make_async_copy(args[7 + j], gains.at[j], at))
        at = in_sems.at[3 * heads + 6 + j]
        small.append(pltpu.make_async_copy(args[9 + j], masks.at[j], at))
    loads = [
        pltpu.make_async_copy(ref.at[:, cols(h)], ins.at[t, x], in_sems.at[3 * x + t])
        for x, h in enumerate(order)
        for t, ref in enumerate((q_ref, k_ref, v_ref))
    ]
    for copy in small + loads:
        copy.start()
    for copy in small:
        copy.wait()
    inv = lax.rsqrt((sums[0] + sums[1] + sums[2] + sums[3]) / D + 1e-06)
    inv_row = inv[1:2, :]
    inv = inv.T
    inv_q = jnp.broadcast_to(inv[:, 0:1] * (LOG2E / float(HD) ** 0.5), (tok, HD))
    inv_k = jnp.broadcast_to(inv[:, 1:2], (tok, HD))
    flags = [jnp.where(masks[0, i, 1 - i] == 1, 0.0, NEG) for i in range(2)]
    lane = lax.broadcasted_iota(jnp.int32, (BLOCK, HD), 1)
    lses = [jnp.zeros((BLOCK, HD), jnp.float32) for _ in range(tok // BLOCK)]
    stores = []
    for x, h in enumerate(order):
        if x in (0, heads // 2):
            for copy in loads[3 * x : 3 * (x + heads // 2)]:
                copy.wait()
        query = scaled(ins[0, x], inv_q, gains[0, pl.ds(h, 1), :])
        keys = scaled(ins[1, x], inv_k, gains[1, pl.ds(h, 1), :])
        vals = ins[2, x]
        if x < heads - n:
            extra[x] = query
        else:
            s = x - (heads - n)
            held[s, :tok, :] = query
            held[s, tok : 2 * tok, :] = keys
            rows = pl.ds(pl.multiple_of((me ^ s) % parts * pos, pos), pos)
            held[s, 2 * tok : 2 * tok + pos, :] = extra[(me ^ s) // parts, rows, :]
            rows = pl.ds(0, 2 * tok + pos)
            stores.append(
                pltpu.make_async_copy(held.at[s, rows], blocks[s].at[rows], out_sems.at[x])
            )
            stores[-1].start()
        for i in range(tok // BLOCK):
            rows = slice(i * BLOCK, (i + 1) * BLOCK)
            scores = blocked_scores(query[rows], keys, flags[i], i)
            top = jnp.max(scores, axis=1, keepdims=True)
            out, weight = weigh(jnp.exp2(scores - top), vals)
            own[x, rows, :] = out / weight
            lses[i] = jnp.where(lane == x, top + jnp.log2(weight), lses[i])
        stores.append(
            pltpu.make_async_copy(own.at[x], own_ref.at[:, cols(h)], out_sems.at[heads + x])
        )
        stores[-1].start()
    def split(rest):
        parts = []
        for _ in range(3):
            parts.append(rest.astype(jnp.bfloat16).astype(jnp.float32))
            rest = rest - parts[-1]
        return parts

    lses = [split(lse.T[:ROWS]) for lse in lses]
    norms = [split(inv_row[:, i * BLOCK : (i + 1) * BLOCK]) for i in range(tok // BLOCK)]
    lane = lax.broadcasted_iota(jnp.int32, (1, HD), 1)
    mask = jnp.where(lane == 0, masks[1, 0, 1], masks[1, 1, 0])
    tail = norms[0] + norms[1] + [(mask == 1).astype(jnp.float32)]
    at = 2 * tok + pos
    for s in range(n):
        first = heads - n + s
        rows = [piece[first : first + 1, :] for half in lses for piece in half]
        late = (me ^ s) // parts == 1
        upper = (me ^ s) % parts * pos >= BLOCK
        for low, high in zip(*lses):
            piece = jnp.where(upper, high, low)
            rows.append(jnp.where(late, piece[1:2, :], piece[0:1, :]))
        held[s, at : at + ROWS, :] = jnp.concatenate(rows + tail, axis=0).astype(jnp.bfloat16)
        rows = pl.ds(at, ROWS)
        stores.append(
            pltpu.make_async_copy(held.at[s, rows], blocks[s].at[rows], out_sems.at[2 * heads + s])
        )
        stores[-1].start()
    for copy in stores:
        copy.wait()


FAR_ORDER = (0, 1, 2, 3, 4, 5, 6, 7)
BACK_ORDER = (0, 1, 2, 3, 4, 5, 6, 7)


def by_step(refs, order):
    return [refs[order.index(s)] for s in range(len(order))]


def inverse(value):
    guess = pl.reciprocal(value, approx=True)
    return guess * (2.0 - value * guess)


def turned(vals):
    return jnp.concatenate([vals.T, jnp.ones((ONES, vals.shape[0]), vals.dtype)], axis=0)


def turn_kernel(n, tok, pos, at_ref, v_ref, out_ref):
    gp = tok // n
    me = lax.axis_index("frame")
    for g in range((tok + pos) // gp):
        rows = [v_ref[me ^ s, g * gp : (g + 1) * gp, :] for s in range(n)]
        out_ref[g] = turned(jnp.concatenate(rows, axis=0))
    out_ref[(tok + pos) // gp] = turned(v_ref[at_ref[0], :tok, :])


def attend_tiles(tiles):
    scores = [(dot_t(t[1], t[0]), dot_t(t[3], t[0])) for t in tiles]
    weights = []
    for t, (paired, anchored) in zip(tiles, scores):
        lse, flag, i = t[5:]
        near = paired[i * BLOCK : (i + 1) * BLOCK]
        away = paired[(1 - i) * BLOCK : (2 - i) * BLOCK] + flag
        top = jnp.maximum(
            jnp.max(near, axis=0, keepdims=True), jnp.max(away, axis=0, keepdims=True)
        )
        both = [jnp.exp2(near - top), jnp.exp2(away - top)]
        both = jnp.concatenate(both if i == 0 else both[::-1], axis=0)
        top = jnp.maximum(jnp.max(anchored, axis=0, keepdims=True), lse)
        own = jnp.exp2(lse - top)
        anchored = jnp.exp2(anchored - top)
        weights.append((both.astype(jnp.bfloat16), anchored.astype(jnp.bfloat16), own))
    sums = [
        (
            jnp.dot(t[2], both, preferred_element_type=jnp.float32),
            jnp.dot(t[4], anchored, preferred_element_type=jnp.float32),
            own,
        )
        for t, (both, anchored, own) in zip(tiles, weights)
    ]
    results = []
    for paired, anchored, own in sums:
        scale = inverse(anchored[HD : HD + 1] + own)
        result = paired[:HD] * inverse(paired[HD : HD + 1]) + anchored[:HD] * scale
        results.append((result.T.astype(jnp.bfloat16), own * scale))
    return results


def spin(rows, parts):
    parts %= HD // rows[1]
    return rows[0] if parts == 0 else pltpu.roll(rows[0], parts * rows[1], 1)


def gather_lanes(rows, place, gp):
    lane = lax.broadcasted_iota(jnp.int32, (1, HD), 1) // gp
    out = None
    for j in range(rows.shape[0]):
        row = spin((rows, gp), j - place)[j : j + 1]
        out = row if out is None else jnp.where(lane == j, row, out)
    return out


def scatter_lanes(kept, row, place, gp):
    lane = lax.broadcasted_iota(jnp.int32, (1, HD), 1) // gp
    for j in range(len(kept)):
        kept[j] = jnp.where(lane == place, spin((row, gp), place - j), kept[j])


def side_rows(blocks, at, first):
    rows = []
    for block in blocks:
        side = block[at : at + ROWS, :].astype(jnp.float32)
        rows.append(side[first : first + 1] + side[first + 1 : first + 2] + side[first + 2 : first + 3])
    return jnp.concatenate(rows, axis=0)


def keep_flags(n, blocks, at, flag_ref):
    masks = [block[at : at + ROWS, :].astype(jnp.float32)[MASK_ROW:] for block in blocks]
    masks = jnp.concatenate(masks, axis=0)
    flags = [jnp.broadcast_to(masks[:, i : i + 1], (n, HD)) for i in range(2)]
    flags = [jnp.where(flag == 1.0, 0.0, NEG) for flag in flags]
    upper = lax.axis_index("frame") >= n // 2
    for i in range(2):
        flag_ref[i] = jnp.where(upper, flags[1 - i], flags[i])


def stack_rows(blocks, at, gp):
    return jnp.concatenate([block[at : at + gp, :] for block in blocks], axis=0)


def whole_kernel(n, tok, pos, at_ref, vt_ref, *refs):
    blocks, outs, side_ref = by_step(refs[:n], FAR_ORDER), refs[n : 2 * n], refs[2 * n]
    key_ref, flag_ref = refs[2 * n + 1 :]
    gp = tok // n
    per = n // 2
    me = lax.axis_index("frame")
    for s in range(n):

        @pl.when(at_ref[0] == me ^ s)
        def _():
            key_ref[...] = blocks[s][tok : 2 * tok, :]

    at_side = 2 * tok + pos
    keep_flags(n, blocks, at_side, flag_ref)
    ka, va = key_ref[...], vt_ref[(tok + pos) // gp]
    halves = [blocks[:per], blocks[per:]]
    lses = [[side_rows(half, at_side, 3 * b) for b in range(2)] for half in halves]
    kept = [[[jnp.zeros((1, HD), jnp.float32)] * per for _ in range(2)] for _ in range(2)]
    across = BLOCK // gp
    together = 4
    for g0 in range(0, n, together):
        tiles, places = [], []
        for g in range(g0, g0 + together):
            keys = stack_rows(blocks, tok + g * gp, gp)
            for i, half in enumerate(halves):
                query = stack_rows(half, g * gp, gp)
                lse = gather_lanes(lses[i][g // across], g % across, gp)
                flag = flag_ref[i, pl.ds(g ^ me, 1), :]
                tiles.append((query, keys, vt_ref[g], ka, va, lse, flag, i))
                places.append((g, i))
        for (g, i), (result, keep) in zip(places, attend_tiles(tiles)):
            for j in range(per):
                outs[i * per + j][g * gp : (g + 1) * gp, :] = result[j * gp : (j + 1) * gp]
            scatter_lanes(kept[i][g // across], keep, g % across, gp)
    rows = [kept[s // per][b][s % per] for s in range(n) for b in range(2)]
    side_ref[...] = jnp.concatenate(rows, axis=0)


def part_kernel(n, tok, pos, at_ref, gain_ref, held_ref, vt_ref, v_ref, *refs):
    blocks, done, came_ref = by_step(refs[:n], FAR_ORDER), refs[n : 2 * n], refs[2 * n]
    outs, flag_ref, col_ref = refs[2 * n + 1 : 3 * n + 1], refs[3 * n + 1], refs[3 * n + 2]
    gp = tok // n
    per = n // 2
    parts = tok // pos
    me = lax.axis_index("frame")
    anchor = at_ref[0]
    quarter = me % parts
    odd = quarter * pos % BLOCK != 0
    late = quarter * pos >= BLOCK
    gain = jnp.where(me // parts == 1, gain_ref[n + 1 : n + 2, :], gain_ref[n : n + 1, :])
    at_side = 2 * tok + pos
    keep_flags(n, blocks, at_side, flag_ref)
    norms = [side_rows(blocks, at_side, NORM_ROW + 3 * b) for b in range(2)]
    rows = [jnp.where(late, norms[1], norms[0])]
    for norm in norms:
        row = norm[0:1]
        for s in range(1, n):
            row = jnp.where(anchor == me ^ s, norm[s : s + 1], row)
        rows.append(row)
    rows.append(jnp.zeros((HD - n - 2, HD), jnp.float32))
    col_ref[...] = jnp.concatenate(rows, axis=0).T
    va = turned(jnp.concatenate([held_ref[j, :pos, :] for j in range(parts)], axis=0))
    ka = jnp.concatenate([held_ref[j, pos:, :] for j in range(parts)], axis=0)
    norm = jnp.concatenate([col_ref[:, n + b : n + b + 1] for b in range(2)], axis=0)
    ka = scaled(ka, norm, gain)
    halves = [blocks[:per], blocks[per:]]
    lses = []
    for half in halves:
        lse = side_rows(half, at_side, LSE_ROW)
        lses.append(jnp.where(odd, pltpu.roll(lse, HD - pos, 1), lse))
    kept = [[jnp.zeros((1, HD), jnp.float32)] * per for _ in range(2)]
    tiles, places = [], []
    for u in range(pos // gp):
        first = pl.multiple_of(quarter * pos % BLOCK + u * gp, gp)
        cols = col_ref[pl.ds(first, gp), :]
        norm = jnp.concatenate([cols[:, s : s + 1] for s in range(n)], axis=0)
        at = tok + pos + u * gp
        keys = jnp.concatenate([v_ref[me ^ s, at : at + gp, :] for s in range(n)], axis=0)
        keys = scaled(keys, norm, gain)
        for i, half in enumerate(halves):
            query = stack_rows(half, 2 * tok + u * gp, gp)
            lse = gather_lanes(lses[i], u, gp)
            flag = flag_ref[i, pl.ds((quarter * (pos // gp) + u) ^ me, 1), :]
            tiles.append((query, keys, vt_ref[n + u], ka, va, lse, flag, i))
            places.append((tok + u * gp, u, i))
    for s in range(n):
        outs[s][:tok, :] = done[s][...]
    for (at, u, i), (result, keep) in zip(places, attend_tiles(tiles)):
        for j in range(per):
            outs[i * per + j][at : at + gp, :] = result[j * gp : (j + 1) * gp]
        scatter_lanes(kept[i], keep, u, gp)
    pad = jnp.zeros((ROWS - 3, HD), jnp.float32)
    for s in range(n):
        rows = [came_ref[2 * s : 2 * s + 2, :], kept[s // per][s % per], pad]
        rows = jnp.concatenate(rows, axis=0)
        outs[s][tok + pos : tok + pos + ROWS, :] = rows.astype(jnp.bfloat16)


def join_kernel(n, pos, own_ref, *refs):
    back, out_ref = by_step(refs[:n], BACK_ORDER), refs[n]
    held, sems = refs[n + 1 :]
    tok = own_ref.shape[0]
    parts = tok // pos
    me = lax.axis_index("frame")
    at_side = tok + pos
    sides = jnp.concatenate([block[at_side : at_side + ROWS, :] for block in back], axis=0).T
    sub = lax.broadcasted_iota(jnp.int32, (n * ROWS, HD), 0)

    def spread_lanes(row):
        pick = (sub == row).astype(jnp.bfloat16)
        return jnp.dot(sides, pick, preferred_element_type=jnp.float32)

    copies = []
    for s in range(n):
        d = me ^ s
        keeps = [spread_lanes(s * ROWS + r) for r in range(3)]
        whole = pl.ds(pl.multiple_of(d * HD, HD), HD)
        for b in range(tok // BLOCK):
            rows = slice(b * BLOCK, (b + 1) * BLOCK)
            got = back[s][rows, :].astype(jnp.float32)
            held[s, rows, :] = (own_ref[rows, whole] * keeps[b] + got).astype(jnp.bfloat16)
        copies.append(pltpu.make_async_copy(held.at[s], out_ref.at[:, whole], sems.at[0, s]))
        copies[-1].start()
        part = pl.ds(pl.multiple_of((n + d // parts) * HD, HD), HD)
        rows = pl.ds(pl.multiple_of(d % parts * pos, pos), pos)
        got = back[s][tok : tok + pos, :].astype(jnp.float32)
        got = own_ref[rows, part] * keeps[2][:pos] + got
        held[n + s // parts, s % parts * pos : (s % parts + 1) * pos, :] = got.astype(jnp.bfloat16)
        copies.append(
            pltpu.make_async_copy(
                held.at[n + s // parts, pl.ds(s % parts * pos, pos)], out_ref.at[rows, part], sems.at[1, s]
            )
        )
        copies[-1].start()
    for copy in copies:
        copy.wait()


def call(kernel, out_shape, *args, vmem=40, **more):
    return pl.pallas_call(
        kernel,
        out_shape=out_shape,
        compiler_params=pltpu.CompilerParams(vmem_limit_bytes=vmem * 1024 * 1024),
        **more,
    )(*args)


def pairwise(array, axis, step):
    size = lax.axis_size(axis)
    return lax.ppermute(array, axis, [(i, i ^ step) for i in range(size)])


def swap_blocks(blocks, order, chain):
    got = {0: blocks[0]}
    for s in order:
        block = blocks[s]
        if s in chain:
            block, _ = lax.optimization_barrier((block, got[chain[s]]))
        got[s] = pairwise(block, "frame", s)
    return [got[s] for s in range(len(blocks))]


def local_heads(
    q_raw, k_raw, values, q_gain, k_gain, spatial_mask, temporal_mask, anchor_frame
):
    tok, width = q_raw.shape
    n = lax.axis_size("frame")
    n_mp = lax.axis_size("mp")
    heads = width // HD
    parts = n // (heads - n)
    pos = tok // parts
    me = lax.axis_index("frame")
    shape = jax.ShapeDtypeStruct
    vm = pl.BlockSpec(memory_space=pltpu.VMEM)
    sm = pl.BlockSpec(memory_space=pltpu.SMEM)
    hbm = pl.BlockSpec(memory_space=pltpu.HBM)
    dma = pltpu.SemaphoreType.DMA
    bf16, f32 = jnp.bfloat16, jnp.float32

    v_blocks = call(
        functools.partial(cut_kernel, n, pos),
        shape((n, tok + 2 * pos, HD), bf16),
        k_raw,
        values,
        in_specs=[hbm] * 2,
        out_specs=hbm,
        scratch_shapes=[pltpu.VMEM((n, tok + 2 * pos, HD), bf16), dma((4, n))],
        vmem=60,
    )
    q_raw, k_raw, values, v_blocks = lax.optimization_barrier((q_raw, k_raw, values, v_blocks))
    sums = call(
        squares_kernel,
        shape((8, tok), f32),
        q_raw,
        k_raw,
        in_specs=[hbm] * 2,
        scratch_shapes=[pltpu.VMEM((2, tok, width), bf16), dma((2, 4))],
        vmem=60,
    )
    all_sums = [sums] + [pairwise(sums, "mp", step) for step in range(1, n_mp)]
    v_far = lax.all_to_all(v_blocks, "frame", split_axis=0, concat_axis=0, tiled=True)
    rows = 2 * tok + pos + ROWS
    *sent, own = call(
        functools.partial(own_kernel, n, pos),
        [shape((rows, HD), bf16)] * n + [shape((tok, width), f32)],
        q_raw,
        k_raw,
        values,
        *all_sums,
        q_gain.reshape(heads, HD),
        k_gain.reshape(heads, HD),
        spatial_mask[0],
        temporal_mask[0],
        in_specs=[hbm] * 11,
        out_specs=[hbm] * (n + 1),
        scratch_shapes=[
            pltpu.VMEM((3, heads, tok, HD), bf16),
            pltpu.VMEM((n, rows, HD), bf16),
            pltpu.VMEM((heads - n, tok, HD), bf16),
            pltpu.VMEM((heads, tok, HD), f32),
            pltpu.VMEM((4, 8, tok), f32),
            pltpu.VMEM((2, heads, HD), f32),
            pltpu.SMEM((2, 2, 2), jnp.int32),
            dma((3 * heads + 8,)),
            dma((2 * heads + n,)),
        ],
        vmem=60,
    )
    far = swap_blocks(sent, (4, 6, 5, 7, 1, 2, 3), {3: 2})
    block, v_far, *_ = lax.optimization_barrier((sent[0], v_far, far[1], far[2]))
    far[0] = call(copy_kernel, shape((rows, HD), bf16), block, vmem=8)

    anchor = anchor_frame[0]
    mine = lax.dynamic_slice(v_far, (anchor, tok, 0), (1, 2 * pos, HD))
    groups = [list(range(first, first + parts)) for first in range(0, n, parts)]
    held = lax.all_to_all(
        jnp.broadcast_to(mine, (parts, 2 * pos, HD)),
        "frame",
        split_axis=0,
        concat_axis=0,
        axis_index_groups=groups,
        tiled=True,
    )
    pencils = (tok + pos) // (tok // n)
    vt = call(
        functools.partial(turn_kernel, n, tok, pos),
        shape((pencils + 1, HD + ONES, tok), bf16),
        anchor_frame,
        v_far,
        in_specs=[sm, vm],
    )
    exps = n * tok * 2 * tok
    *done, side = call(
        functools.partial(whole_kernel, n, tok, pos),
        [shape((tok, HD), bf16)] * n + [shape((2 * n, HD), f32)],
        anchor_frame,
        vt,
        *[far[s] for s in FAR_ORDER],
        in_specs=[sm] + [vm] * (n + 1),
        scratch_shapes=[pltpu.VMEM((tok, HD), bf16), pltpu.VMEM((2, n, HD), f32)],
        cost_estimate=pl.CostEstimate(
            flops=6 * exps * HD, bytes_accessed=8 * n * tok * HD, transcendentals=exps
        ),
    )
    result = call(
        functools.partial(part_kernel, n, tok, pos),
        [shape((tok + pos + ROWS, HD), bf16)] * n,
        anchor_frame,
        k_gain.reshape(heads, HD),
        held,
        vt,
        v_far,
        *[far[s] for s in FAR_ORDER],
        *done,
        side,
        in_specs=[sm] + [vm] * (2 * n + 5),
        scratch_shapes=[pltpu.VMEM((2, n, HD), f32), pltpu.VMEM((HD, HD), f32)],
    )
    back = swap_blocks(result, (4, 6, 5, 7, 1, 2, 3), {1: 4})
    return call(
        functools.partial(join_kernel, n, pos),
        shape((tok, width), bf16),
        own,
        *[back[s] for s in BACK_ORDER],
        in_specs=[vm] * (n + 1),
        out_specs=hbm,
        scratch_shapes=[pltpu.VMEM((n + 2, tok, HD), bf16), dma((2, n))],
    )


def solution(mesh):
    n = mesh.shape["frame"]

    def local(*args):
        tok, width = args[0].shape
        fits = n == 8 and mesh.shape["mp"] == 4 and width == 10 * HD and tok == 2 * BLOCK
        return local_heads(*args) if fits else local_general(*args)

    return jax.shard_map(
        local,
        mesh=mesh,
        in_specs=(
            P("frame", "mp"),
            P("frame", "mp"),
            P("frame", "mp"),
            P("mp"),
            P("mp"),
            P("frame", None, None),
            P("frame", None, None),
            P(),
        ),
        out_specs=P("frame", "mp"),
        check_vma=False,
    )
```
